32 devices in a mesh: fsdp: 8 (over z, y), seq: 4 (over x, core).
Axes of the slice: x: 2, y: 2, z: 4, core: 2. Of those that a mesh axis runs over, the one named last changes fastest.
Arguments:
- latents: bfloat16 [16, 512, 1152], P('fsdp', 'seq'), may hold values from -6 to 6
- condition: bfloat16 [16, 1152], P('fsdp'), may hold values from -6 to 6
- mod_weight: bfloat16 [1152, 6912], P('fsdp'), may hold values from -0.1875 to 0.1875
- mod_bias: bfloat16 [6912], P('fsdp'), may hold values from -4 to 4
- qkv_weight: bfloat16 [1152, 3456], P('fsdp'), may hold values from -0.1875 to 0.1875
- qv_bias: bfloat16 [2304], P('fsdp'), may hold values from -4 to 4
- out_weight: bfloat16 [1152, 1152], P('fsdp'), may hold values from -1.5 to 1.5
- out_bias: bfloat16 [1152], P('fsdp'), may hold values from -4 to 4
- up_weight: bfloat16 [1152, 4608], P('fsdp'), may hold values from -0.1875 to 0.1875
- up_bias: bfloat16 [4608], P('fsdp'), may hold values from -4 to 4
- down_weight: bfloat16 [4608, 1152], P('fsdp'), may hold values from -0.09375 to 0.09375
- down_bias: bfloat16 [1152], P('fsdp'), may hold values from -4 to 4
- cotangent: bfloat16 [16, 512, 1152], P('fsdp', 'seq'), may hold values from -6 to 6
Outputs:
- mixed: bfloat16 [16, 512, 1152], P('fsdp', 'seq')
- grad_latents: float32 [16, 512, 1152], P('fsdp', 'seq')
- grad_condition: float32 [16, 1152], P('fsdp')
- grad_mod_weight: float32 [1152, 6912], P('fsdp')
- grad_mod_bias: float32 [6912], P('fsdp')
- grad_qkv_weight: float32 [1152, 3456], P('fsdp')
- grad_qv_bias: float32 [2304], P('fsdp')
- grad_out_weight: float32 [1152, 1152], P('fsdp')
- grad_out_bias: float32 [1152], P('fsdp')
- grad_up_weight: float32 [1152, 4608], P('fsdp')
- grad_up_bias: float32 [4608], P('fsdp')
- grad_down_weight: float32 [4608, 1152], P('fsdp')
- grad_down_bias: float32 [1152], P('fsdp')
The draws below stay inside these ranges and needn't reach their ends.
All inputs are finite; a program needn't handle non-finite values.
Results may differ from the reference program's by a relative error of at most 0.015.
The reference program's roundings to bfloat16 on the way count: a program that leaves them out, or rounds other values in their place, can miss the bound.
Values may be sent and summed in bfloat16 or wider, within the bound.
No kernel may reach another device: no remote copies, remote signals or barrier semaphores. Data moves between devices by JAX's collectives and lax.ppermute only.
A program may use at most 256 MiB of HBM per device.

```python
import jax
import jax.numpy as jnp
from jax import lax

D = 1152
H = 16
HD = 72
FF = 4608
L = 512
LATENTS = 16


def steps_of(key, shape, cuts, smallest, largest):
    factor_of = 1.0
    for axis_at, parts in cuts:
        draws = jax.random.uniform(jax.random.fold_in(jax.random.fold_in(key, 6), axis_at), (parts,), jnp.float32, smallest / len(cuts), largest / len(cuts))
        factor_of = factor_of * jnp.repeat(jnp.exp(draws), shape[axis_at] // parts).reshape((-1,) + (1,) * (len(shape) - 1 - axis_at))
    return factor_of


def bell_draw(stream_key, shape, deviation, most, cuts=(), kind=jnp.bfloat16):
    result = jax.random.normal(stream_key, shape, jnp.float32) * deviation
    if len(cuts) > 0:
        result = steps_of(stream_key, shape, cuts, -0.22, 0.18) * result
    return jnp.clip(result, min=-most, max=most).astype(kind)


def setup_inputs(seed: int = 0) -> dict:
    key_of = jax.random.split(jax.random.key(seed), 14)
    return {
        "latents": bell_draw(key_of[0], (LATENTS, L, D), 1.0, 6.0, ((0, 8), (1, 4))),
        "condition": bell_draw(key_of[1], (LATENTS, D), 1.0, 6.0, ((0, 8),)),
        "mod_weight": bell_draw(key_of[2], (D, 6 * D), D ** -0.5, 0.1875, ((0, 8),)),
        "mod_bias": bell_draw(key_of[3], (6 * D,), 0.3, 4.0, ((0, 8),)),
        "qkv_weight": bell_draw(key_of[4], (D, 3 * D), D ** -0.5, 0.1875, ((0, 8),)),
        "qv_bias": bell_draw(key_of[5], (2 * D,), 0.3, 4.0, ((0, 8),)),
        "out_weight": bell_draw(key_of[6], (D, D), (D // 64) ** -0.5, 1.5, ((0, 8),)),
        "out_bias": bell_draw(key_of[7], (D,), 0.3, 4.0, ((0, 8),)),
        "up_weight": bell_draw(key_of[8], (D, FF), D ** -0.5, 0.1875, ((0, 8),)),
        "up_bias": bell_draw(key_of[9], (FF,), 0.3, 4.0, ((0, 8),)),
        "down_weight": bell_draw(key_of[10], (FF, D), FF ** -0.5, 0.09375, ((0, 8),)),
        "down_bias": bell_draw(key_of[11], (D,), 0.3, 4.0, ((0, 8),)),
        "cotangent": bell_draw(key_of[12], (LATENTS, L, D), 1.0, 6.0, ((0, 8), (1, 4))),
    }


@jax.custom_vjp
def low(v):
    return lax.optimization_barrier(v.astype(jnp.bfloat16)).astype(jnp.float32)

@jax.custom_vjp
def low_back(v):
    return v

def low_keep(v):
    return (low(v), None)

def low_pass(kept, grad):
    return (grad,)

def back_keep(v):
    return (v, None)

def back_low(kept, grad):
    return (low(grad),)
low.defvjp(low_keep, low_pass)
low_back.defvjp(back_keep, back_low)

def product(left_side, right_side):
    return jnp.dot(left_side, right_side, precision=lax.Precision.HIGHEST, preferred_element_type=jnp.float32)

def normalize(values):
    centre = values - lax.optimization_barrier(jnp.mean(values, axis=-1, keepdims=True))
    spread = lax.optimization_barrier(jnp.mean(centre * centre, axis=-1, keepdims=True))
    return centre * lax.rsqrt(spread + 1e-06)

def one_latent(tokens, conditioning, params):
    mod_weight, mod_bias, qkv_weight, qv_bias, out_weight, out_bias, up_weight, up_bias, down_weight, down_bias = params
    cond_low = low(jax.nn.silu(conditioning))
    modulation = low_back(product(cond_low, mod_weight) + mod_bias)
    shift_one, scale_one, gate_one, shift_two, scale_two, gate_two = jnp.split(modulation, 6)
    attn_in = low(normalize(tokens) * (1.0 + scale_one) + shift_one)
    qkv_bias = jnp.concatenate([qv_bias[:D], jnp.zeros((D,), jnp.float32), qv_bias[D:]])
    projected = low(low_back(product(attn_in, qkv_weight) + qkv_bias))
    queries = projected[:, :D].reshape(L, H, HD)
    keys_all = projected[:, D:2 * D].reshape(L, H, HD)
    values_all = projected[:, 2 * D:].reshape(L, H, HD)
    scores = low_back(jnp.einsum('qhd,khd->hqk', queries, keys_all, precision=lax.Precision.HIGHEST) * HD ** (-0.5))
    probabilities = jax.nn.softmax(scores, axis=-1)
    heads_out = jnp.einsum('hqk,khd->qhd', low(probabilities), values_all, precision=lax.Precision.HIGHEST).reshape(L, D)
    heads_out = low(low_back(heads_out))
    attn_branch = low_back(product(heads_out, out_weight) + out_bias)
    middle = tokens + gate_one * attn_branch
    mlp_in = low(normalize(middle) * (1.0 + scale_two) + shift_two)
    pre_act = low_back(product(mlp_in, up_weight) + up_bias)
    activated = low(jax.nn.gelu(pre_act, approximate=True))
    mlp_branch = low_back(product(activated, down_weight) + down_bias)
    return middle + gate_two * mlp_branch

def forward_all(tokens, conditions, params):
    checked = jax.checkpoint(one_latent)
    return lax.map(lambda paired: checked(paired[0], paired[1], params), (tokens, conditions))

def reference(latents, condition, mod_weight, mod_bias, qkv_weight, qv_bias, out_weight, out_bias, up_weight, up_bias, down_weight, down_bias, cotangent):
    params = (mod_weight.astype(jnp.float32), mod_bias.astype(jnp.float32), qkv_weight.astype(jnp.float32), qv_bias.astype(jnp.float32), out_weight.astype(jnp.float32), out_bias.astype(jnp.float32), up_weight.astype(jnp.float32), up_bias.astype(jnp.float32), down_weight.astype(jnp.float32), down_bias.astype(jnp.float32))
    outputs, pullback = jax.vjp(forward_all, latents.astype(jnp.float32), condition.astype(jnp.float32), params)
    grad_tokens, grad_cond, grads = pullback(cotangent.astype(jnp.float32))
    return (outputs.astype(jnp.bfloat16), grad_tokens, grad_cond, grads[0], grads[1], grads[2], grads[3], grads[4], grads[5], grads[6], grads[7], grads[8], grads[9])
```

```python
import jax
import jax.numpy as jnp
from jax import lax
from jax.sharding import PartitionSpec as P

H = 16
HD = 72
GELU_ROOT = (2.0 / 3.141592653589793) ** 0.5
GELU_CUBE = 0.044715


def matmul(left_side, right_side):
    return jnp.dot(left_side, right_side, preferred_element_type=jnp.float32)


def contract(left_side, right_side, left_dim, right_dim):
    return lax.dot_general(
        left_side,
        right_side,
        (((left_dim,), (right_dim,)), ((), ())),
        preferred_element_type=jnp.float32,
    )


def low(values):
    return values.astype(jnp.bfloat16)


def wide(values):
    return values.astype(jnp.float32)


def normalize(values):
    centre = values - jnp.mean(values, axis=-1, keepdims=True)
    spread = jnp.mean(centre * centre, axis=-1, keepdims=True)
    inverse = lax.rsqrt(spread + 1e-06)
    return centre * inverse, inverse


def normalize_back(normed, inverse, grad):
    inner = jnp.mean(grad * normed, axis=-1, keepdims=True)
    return (grad - jnp.mean(grad, axis=-1, keepdims=True) - normed * inner) * inverse


def pick(values, index, axis):
    return lax.dynamic_index_in_dim(values, index, axis, keepdims=False)


def ordered(first, mine, other, axis):
    return jnp.where(
        first, jnp.concatenate([mine, other], axis), jnp.concatenate([other, mine], axis)
    )


class Place:
    def __init__(self):
        self.shards = lax.axis_size("fsdp")
        self.seats = lax.axis_size("seq")
        self.line_size = self.shards // 2
        self.shard = lax.axis_index("fsdp")
        self.seat = lax.axis_index("seq")
        self.line = self.shard // 2
        self.pair = self.shard % 2
        self.side = self.seat // 2
        self.core = self.seat % 2

    def to_core(self, values):
        return lax.ppermute(values, "seq", [(i, i ^ 1) for i in range(self.seats)])

    def to_side(self, values):
        return lax.ppermute(values, "seq", [(i, i ^ 2) for i in range(self.seats)])

    def to_pair(self, values):
        return lax.ppermute(values, "fsdp", [(i, i ^ 1) for i in range(self.shards)])

    def to_line(self, values):
        return lax.ppermute(
            values, "fsdp", [(i, (i + 2) % self.shards) for i in range(self.shards)]
        )

    def spread(self, tokens):
        count = tokens.shape[0] // 2
        halves = tokens.reshape((2, count) + tokens.shape[1:])
        near = self.to_core(pick(halves, 1 - self.core, 0))
        both = jnp.concatenate([pick(halves, self.core, 0), near], axis=1)
        return jnp.concatenate([both, self.to_side(both)], axis=1)

    def unspread(self, mine):
        tokens = mine.shape[1] // 2
        near = self.to_core(mine[:, tokens:])
        return ordered(self.core == 0, mine[:, :tokens], near, 0)

    def gather(self, piece):
        total = jnp.zeros((self.shards,) + piece.shape, piece.dtype)
        for step in range(self.line_size):
            near = self.to_pair(piece)
            start = (self.line - step) % self.line_size * 2
            total = lax.dynamic_update_index_in_dim(total, piece, start + self.pair, 0)
            total = lax.dynamic_update_index_in_dim(total, near, start + 1 - self.pair, 0)
            if step + 1 < self.line_size:
                piece = self.to_line(piece)
        return total

    def reduce(self, mine, theirs):
        rows, columns = mine.shape
        met = self.to_core(low(theirs))
        total = low(mine + wide(met))
        blocks = total.reshape(self.line_size, 2, rows // self.shards, columns)
        got = self.to_pair(pick(blocks, 1 - self.pair, 1))
        kept = low(wide(pick(blocks, self.pair, 1)) + wide(got))
        run = None
        for step in range(1, self.line_size):
            block = pick(kept, (self.line - step) % self.line_size, 0)
            run = self.to_line(block if run is None else low(wide(block) + wide(run)))
        return low(wide(pick(kept, self.line, 0)) + wide(run))

    def share(self, quarter):
        half = self.to_side(quarter)
        sides = ordered(self.side == 0, quarter[None], half[None], 0)
        cores = self.to_core(sides)
        whole = ordered(self.core == 0, sides[:, None], cores[:, None], 1)
        return whole.reshape((4,) + quarter.shape)

    def exchange(self, values):
        return lax.all_to_all(values, "fsdp", split_axis=0, concat_axis=0, tiled=True)

    def to_all(self, values):
        return self.exchange(jnp.broadcast_to(values[None], (self.shards,) + values.shape))


def per_device(
    latents,
    condition,
    mod_weight,
    mod_bias,
    qkv_weight,
    qv_bias,
    out_weight,
    out_bias,
    up_weight,
    up_bias,
    down_weight,
    down_bias,
    cotangent,
):
    here = Place()
    shards, seat, side, core = here.shards, here.seat, here.side, here.core
    micros, tokens, width = latents.shape
    count = micros // 2
    length = 4 * tokens
    rows = width // shards
    hidden = up_weight.shape[1]
    heads = H // 4
    part = heads * HD
    factor = HD ** (-0.5)
    flat = (count * length, width)

    qkv_piece = pick(qkv_weight.reshape(rows, 3, 4, part), seat, 2).reshape(rows, 3 * part)
    block = hidden // shards // 4
    up_piece = pick(up_weight.reshape(rows, shards, 4, block), seat, 2).reshape(
        rows, shards * block
    )
    down_piece = pick(down_weight.reshape(4, block, width), seat, 0)
    out_piece = pick(out_weight.reshape(2, rows // 2, width), core, 0)

    qkv_mine = here.gather(qkv_piece).reshape(width, 3 * part)
    qkv_near = here.to_core(qkv_mine)

    small = jnp.concatenate(
        [condition.reshape(-1), mod_bias, qv_bias, out_bias, up_bias, down_bias]
    )
    small = here.to_all(small)
    cuts = [micros * width]
    for vector in (mod_bias, qv_bias, out_bias, up_bias):
        cuts.append(cuts[-1] + vector.shape[0])
    cond_all, mod_bias, qv_bias, out_bias, up_bias, down_bias = jnp.split(small, cuts, axis=1)
    mod_bias, qv_bias, out_bias, up_bias, down_bias = (
        wide(vector.reshape(-1)) for vector in (mod_bias, qv_bias, out_bias, up_bias, down_bias)
    )
    cond_all = cond_all.reshape(shards * micros, width)
    cond_low = low(jax.nn.silu(wide(cond_all)))
    cond_rows = lax.dynamic_slice_in_dim(cond_low, here.shard * rows, rows, 1)
    cond_mine = pick(cond_rows.reshape(shards, 2, count, rows), core, 1)
    mod_part = matmul(cond_mine.reshape(shards * count, rows), mod_weight)
    mod_part = here.exchange(mod_part.reshape(shards, count, 6 * width))
    modulation = jnp.sum(mod_part, axis=0) + mod_bias
    shift_one, scale_one, gate_one, shift_two, scale_two, gate_two = (
        vector[:, None] for vector in jnp.split(modulation, 6, axis=1)
    )

    inputs = wide(here.spread(latents))
    normed_one, inverse_one = normalize(inputs)
    attn_in = low(normed_one * (1.0 + scale_one) + shift_one).reshape(flat)

    qv_parts = jnp.concatenate([qv_bias[:width], jnp.zeros((width,), jnp.float32), qv_bias[width:]])
    qv_parts = qv_parts.reshape(3, 4, part)

    def project(weight, which):
        bias = pick(qv_parts, which, 1).reshape(3 * part, 1)
        values = low(contract(weight, attn_in, 0, 1) + bias)
        return values.reshape(3, heads, HD, count, length)

    def attend(values):
        queries, keys, contents = values
        scores = (
            jnp.einsum("hdbk,hdbq->hbkq", keys, queries, preferred_element_type=jnp.float32)
            * factor
        )
        raised = jnp.exp(scores - jnp.max(scores, axis=2, keepdims=True))
        probs = raised / jnp.sum(raised, axis=2, keepdims=True)
        result = jnp.einsum(
            "hdbk,hbkq->hdbq", contents, low(probs), preferred_element_type=jnp.float32
        )
        return probs, low(result).reshape(part, count * length)

    values_mine = project(qkv_mine, seat)
    probs_mine, result_mine = attend(values_mine)
    near_seat = seat + 1 - 2 * core
    values_near = project(qkv_near, near_seat)
    probs_near, result_near = attend(values_near)
    heads_half = ordered(core == 0, result_mine, result_near, 0)

    heads_far = here.to_side(heads_half).reshape(2 * part, count, 2, length // 2)
    heads_far = heads_far[:, :, ::-1].reshape(heads_half.shape)
    heads_out = ordered(side == 0, heads_half, heads_far, 0)

    out_mine = here.gather(out_piece)
    out_near = here.to_core(out_mine)
    out_full = ordered(core == 0, out_mine[:, None], out_near[:, None], 1).reshape(width, width)
    up_mine = here.gather(up_piece).reshape(width, shards * block)
    up_near = here.to_core(up_mine)
    down_mine = here.gather(down_piece).reshape(shards * block, width)
    down_near = here.to_core(down_mine)

    attn_branch = (contract(heads_out, out_full, 0, 0) + out_bias).reshape(inputs.shape)
    middle = inputs + gate_one * attn_branch
    normed_two, inverse_two = normalize(middle)
    mlp_in = low(normed_two * (1.0 + scale_two) + shift_two).reshape(flat)

    grad_y = wide(here.spread(cotangent))
    grad_mlp = low(gate_two * grad_y).reshape(flat)
    up_parts = up_bias.reshape(shards, 4, block)

    def feed(up, which):
        bias = pick(up_parts, which, 1).reshape(shards * block)
        pre_act = matmul(mlp_in, up) + bias
        squared = pre_act * pre_act
        bent = jnp.tanh(GELU_ROOT * pre_act * (1.0 + GELU_CUBE * squared))
        activated = low(0.5 * pre_act * (1.0 + bent))
        slope = 0.5 * (1.0 + bent) + 0.5 * GELU_ROOT * pre_act * (1.0 - bent * bent) * (
            1.0 + 3.0 * GELU_CUBE * squared
        )
        return activated, slope

    def feed_back(down, slope):
        return low(contract(grad_mlp, down, 1, 1) * slope)

    act_mine, slope_mine = feed(up_mine, seat)
    act_near, slope_near = feed(up_near, near_seat)
    pre_mine = feed_back(down_mine, slope_mine)
    pre_near = feed_back(down_near, slope_near)

    mlp_grad_part = low(contract(pre_mine, up_mine, 1, 1) + contract(pre_near, up_near, 1, 1))
    mlp_grad_far = here.to_side(mlp_grad_part).reshape(count, 2, length // 2, width)
    mlp_grad_far = mlp_grad_far[:, ::-1].reshape(inputs.shape)
    grad_mlp_in = wide(mlp_grad_part.reshape(inputs.shape)) + wide(mlp_grad_far)

    branch_part = matmul(act_mine, down_mine) + matmul(act_near, down_near)
    branch_part = branch_part.reshape(inputs.shape)
    own = length // 2
    branch_far = here.to_side(low(branch_part[:, own:]))
    mlp_branch = branch_part[:, :own] + wide(branch_far) + down_bias
    grad_gate_two = jnp.sum(grad_y[:, :own] * mlp_branch, axis=1)
    mixed = here.unspread(low(middle[:, :own] + gate_two * mlp_branch))

    grad_down = here.reduce(
        contract(act_mine, grad_mlp, 0, 0), contract(act_near, grad_mlp, 0, 0)
    )
    grad_up = here.reduce(contract(mlp_in, pre_mine, 0, 0), contract(mlp_in, pre_near, 0, 0))

    grad_shift_two = jnp.sum(grad_mlp_in[:, :own], axis=1)
    grad_scale_two = jnp.sum((grad_mlp_in * normed_two)[:, :own], axis=1)
    grad_middle = grad_y + normalize_back(
        normed_two, inverse_two, grad_mlp_in * (1.0 + scale_two)
    )
    grad_gate_one = jnp.sum((grad_middle * attn_branch)[:, :own], axis=1)
    grad_attn = low(gate_one * grad_middle).reshape(flat)

    out_half = lax.dynamic_slice_in_dim(out_full, side * 2 * part, 2 * part, 0)
    grad_heads = low(contract(out_half, grad_attn, 1, 1))
    grad_heads = grad_heads.reshape(2, heads, HD, count, length)
    grad_attn_cuts = grad_attn.reshape(count * length, 4, width // 4)
    grad_out = here.reduce(
        contract(heads_out, pick(grad_attn_cuts, seat, 1), 1, 0),
        contract(heads_out, pick(grad_attn_cuts, near_seat, 1), 1, 0),
    )

    def attend_back(values, probs, grad_result):
        queries, keys, contents = values
        grad_probs = jnp.einsum(
            "hdbk,hdbq->hbkq", contents, grad_result, preferred_element_type=jnp.float32
        )
        inner = jnp.sum(probs * grad_probs, axis=2, keepdims=True)
        grad_scores = low(probs * (grad_probs - inner))
        grad_queries = factor * jnp.einsum(
            "hdbk,hbkq->hdbq", keys, grad_scores, preferred_element_type=jnp.float32
        )
        grad_keys = factor * jnp.einsum(
            "hdbq,hbkq->hdbk", queries, grad_scores, preferred_element_type=jnp.float32
        )
        grad_contents = jnp.einsum(
            "hdbq,hbkq->hdbk", grad_result, low(probs), preferred_element_type=jnp.float32
        )
        grads = jnp.stack([low(grad_queries), low(grad_keys), low(grad_contents)])
        return grads.reshape(3 * part, count * length)

    qkv_grad_mine = attend_back(values_mine, probs_mine, pick(grad_heads, core, 0))
    qkv_grad_near = attend_back(values_near, probs_near, pick(grad_heads, 1 - core, 0))
    grad_qkv = here.reduce(
        contract(attn_in, qkv_grad_mine, 0, 1), contract(attn_in, qkv_grad_near, 0, 1)
    )
    attn_grad_part = contract(qkv_grad_mine, qkv_mine, 0, 1) + contract(
        qkv_grad_near, qkv_near, 0, 1
    )
    attn_grad_part = attn_grad_part.reshape(inputs.shape)
    part_shift = jnp.sum(attn_grad_part, axis=1)
    part_scale = jnp.sum(attn_grad_part * normed_one, axis=1)
    attn_grad_far = here.to_side(low(attn_grad_part[:, own:]))
    grad_attn_in = attn_grad_part[:, :own] + wide(attn_grad_far)
    grad_tokens = grad_middle[:, :own] + normalize_back(
        normed_one[:, :own], inverse_one[:, :own], grad_attn_in * (1.0 + scale_one)
    )
    grad_latents = here.unspread(grad_tokens)

    grad_mod = jnp.concatenate(
        [part_shift, part_scale, grad_gate_one, grad_shift_two, grad_scale_two, grad_gate_two],
        axis=1,
    )
    qv_sums = jnp.zeros((2, 4, part), jnp.float32)
    up_sums = jnp.zeros((shards, 4, block), jnp.float32)
    for grads, pre, which in (
        (qkv_grad_mine, pre_mine, seat),
        (qkv_grad_near, pre_near, near_seat),
    ):
        sums = jnp.sum(wide(grads), axis=1).reshape(3, part)[::2]
        qv_sums = lax.dynamic_update_index_in_dim(qv_sums, sums, which, 1)
        sums = jnp.sum(wide(pre), axis=0).reshape(shards, block)
        up_sums = lax.dynamic_update_index_in_dim(up_sums, sums, which, 1)
    out_sums = jnp.sum(wide(grad_attn).reshape(inputs.shape)[:, :own], axis=(0, 1))
    down_sums = jnp.sum(wide(grad_mlp).reshape(inputs.shape)[:, :own], axis=(0, 1))
    bias_sums = jnp.concatenate(
        [
            vector.reshape(shards, -1)
            for vector in (qv_sums, out_sums, up_sums, down_sums)
        ],
        axis=1,
    )
    vector = jnp.concatenate([grad_mod.reshape(-1), bias_sums.reshape(-1)])
    vector = vector + here.to_side(vector)
    grad_mod = vector[: count * 6 * width]
    bias_sums = vector[count * 6 * width :]
    near = here.to_core(vector)
    bias_sums = (bias_sums + near[count * 6 * width :]).reshape(shards, -1)
    grad_mod = ordered(
        core == 0,
        grad_mod.reshape(1, count * 6 * width),
        near[: count * 6 * width].reshape(1, count * 6 * width),
        0,
    )
    mod_low = low(grad_mod).reshape(1, -1)
    sent = jnp.concatenate(
        [jnp.broadcast_to(wide(mod_low), (shards, mod_low.shape[1])), bias_sums], axis=1
    )
    got = here.exchange(sent)
    mod_all = low(got[:, : mod_low.shape[1]]).reshape(shards * micros, 6 * width)
    bias_sums = jnp.sum(got[:, mod_low.shape[1] :], axis=0)
    cuts = []
    for vector in (qv_bias, out_bias, up_bias):
        cuts.append((cuts[-1] if cuts else 0) + vector.shape[0] // shards)
    grad_qv_bias, grad_out_bias, grad_up_bias, grad_down_bias = jnp.split(bias_sums, cuts)
    grad_mod_weight = contract(cond_rows, mod_all, 0, 0)
    span = 6 * width // shards
    grad_mod_bias = jnp.sum(
        wide(lax.dynamic_slice_in_dim(mod_all, here.shard * span, span, 1)), axis=0
    )
    grad_low = contract(mod_all, mod_weight, 1, 1).reshape(shards, micros, rows)
    grad_low = here.exchange(grad_low).transpose(1, 0, 2).reshape(micros, width)
    _, silu_pull = jax.vjp(jax.nn.silu, wide(condition))
    grad_condition = silu_pull(grad_low)[0]

    grad_qkv = wide(here.share(grad_qkv)).reshape(4, rows, 3, part)
    grad_qkv = grad_qkv.transpose(1, 2, 0, 3).reshape(rows, 3 * width)
    grad_out = wide(here.share(grad_out)).transpose(1, 0, 2).reshape(rows, width)
    grad_up = wide(here.share(grad_up)).reshape(4, rows, shards, block)
    grad_up = grad_up.transpose(1, 2, 0, 3).reshape(rows, hidden)
    grad_down = wide(here.share(grad_down)).reshape(4 * block, width)

    return (
        mixed,
        grad_latents,
        grad_condition,
        grad_mod_weight,
        grad_mod_bias,
        grad_qkv,
        grad_qv_bias,
        grad_out,
        grad_out_bias,
        grad_up,
        grad_up_bias,
        grad_down,
        grad_down_bias,
    )


def solution(mesh):
    tokens = P("fsdp", "seq", None)
    matrix = P("fsdp", None)
    vector = P("fsdp")
    parameters = (matrix, vector) * 5
    in_specs = (tokens, matrix) + parameters + (tokens,)
    out_specs = (tokens, tokens, matrix) + parameters
    return jax.shard_map(
        per_device, mesh=mesh, in_specs=in_specs, out_specs=out_specs, check_vma=False
    )
```

```python
import jax
import jax.numpy as jnp
from jax import lax
from jax.experimental import pallas as pl
from jax.experimental.pallas import tpu as pltpu
from jax.sharding import PartitionSpec as P

H = 16
HD = 72
GELU_ROOT = (2.0 / 3.141592653589793) ** 0.5
GELU_CUBE = 0.044715


def matmul(left_side, right_side):
    return jnp.dot(left_side, right_side, preferred_element_type=jnp.float32)


def contract(left_side, right_side, left_dim, right_dim):
    return lax.dot_general(
        left_side,
        right_side,
        (((left_dim,), (right_dim,)), ((), ())),
        preferred_element_type=jnp.float32,
    )


def low(values):
    return values.astype(jnp.bfloat16)


def wide(values):
    return values.astype(jnp.float32)


def normalize(values):
    centre = values - jnp.mean(values, axis=-1, keepdims=True)
    spread = jnp.mean(centre * centre, axis=-1, keepdims=True)
    inverse = lax.rsqrt(spread + 1e-06)
    return centre * inverse, inverse


def normalize_back(normed, inverse, grad):
    inner = jnp.mean(grad * normed, axis=-1, keepdims=True)
    return (grad - jnp.mean(grad, axis=-1, keepdims=True) - normed * inner) * inverse


def pick(values, index, axis):
    return lax.dynamic_index_in_dim(values, index, axis, keepdims=False)


def ordered(first, mine, other, axis):
    return jnp.where(
        first, jnp.concatenate([mine, other], axis), jnp.concatenate([other, mine], axis)
    )


SCALARS = pl.BlockSpec(memory_space=pltpu.SMEM)
WHOLE = pl.BlockSpec(memory_space=pltpu.VMEM)
ROOM = pltpu.CompilerParams(vmem_limit_bytes=48 << 20)


def scalars(*values):
    return jnp.stack(values).astype(jnp.int32)


def flip_halves(values, axis):
    first, second = jnp.split(values, 2, axis)
    return jnp.concatenate([second, first], axis)


def cut_columns(weight, seat, groups):
    rows, columns = weight.shape
    part = columns // groups // 4

    def kernel(seat_ref, source, target):
        for quarter in range(4):

            @pl.when(seat_ref[0] == quarter)
            def _():
                for group in range(groups):
                    start = (group * 4 + quarter) * part
                    target[:, group * part : (group + 1) * part] = source[:, start : start + part]

    return pl.pallas_call(
        kernel,
        out_shape=jax.ShapeDtypeStruct((rows, groups * part), weight.dtype),
        in_specs=[SCALARS, WHOLE],
        out_specs=WHOLE,
        compiler_params=ROOM,
    )(scalars(seat), weight)


def lay_columns(mine, far, near, seat, groups):
    rows, columns = mine.shape
    part = columns // groups

    def kernel(seat_ref, mine_ref, far_ref, near_ref, target):
        for own in range(4):

            @pl.when(seat_ref[0] == own)
            def _():
                for group in range(groups):
                    span = slice(group * part, (group + 1) * part)
                    blocks = (
                        (own, mine_ref[:, span]),
                        (own ^ 2, far_ref[:, span]),
                        (own ^ 1, near_ref[0, :, span]),
                        (own ^ 3, near_ref[1, :, span]),
                    )
                    for quarter, block in blocks:
                        start = (group * 4 + quarter) * part
                        target[:, start : start + part] = block.astype(jnp.float32)

    return pl.pallas_call(
        kernel,
        out_shape=jax.ShapeDtypeStruct((rows, 4 * columns), jnp.float32),
        in_specs=[SCALARS, WHOLE, WHOLE, WHOLE],
        out_specs=WHOLE,
        compiler_params=ROOM,
    )(scalars(seat), mine, far, near)


def place_blocks(pieces, spots):
    count = len(pieces)

    def kernel(spots_ref, *refs):
        target = refs[count]
        for index in range(count):
            target[spots_ref[index]] = refs[index][...]

    return pl.pallas_call(
        kernel,
        out_shape=jax.ShapeDtypeStruct((count,) + pieces[0].shape, pieces[0].dtype),
        in_specs=[SCALARS] + [WHOLE] * count,
        out_specs=WHOLE,
        compiler_params=ROOM,
    )(scalars(*spots), *pieces)


class Place:
    def __init__(self):
        self.shards = lax.axis_size("fsdp")
        self.seats = lax.axis_size("seq")
        self.line_size = self.shards // 2
        self.shard = lax.axis_index("fsdp")
        self.seat = lax.axis_index("seq")
        self.line = self.shard // 2
        self.pair = self.shard % 2
        self.side = self.seat // 2
        self.core = self.seat % 2

    def to_core(self, values):
        return lax.ppermute(values, "seq", [(i, i ^ 1) for i in range(self.seats)])

    def to_side(self, values):
        return lax.ppermute(values, "seq", [(i, i ^ 2) for i in range(self.seats)])

    def to_pair(self, values):
        return lax.ppermute(values, "fsdp", [(i, i ^ 1) for i in range(self.shards)])

    def to_line(self, values):
        return lax.ppermute(
            values, "fsdp", [(i, (i + 2) % self.shards) for i in range(self.shards)]
        )

    def exchange(self, values):
        return lax.all_to_all(values, "fsdp", split_axis=0, concat_axis=0, tiled=True)

    def to_all(self, values):
        return self.exchange(jnp.broadcast_to(values[None], (self.shards,) + values.shape))


class Order:
    def __init__(self):
        self.last = ()

    def take(self, *values):
        values = lax.optimization_barrier((values, self.last))[0]
        return values if len(values) > 1 else values[0]

    def keep(self, *values):
        self.last = values
        return values if len(values) > 1 else values[0]

    def wait(self, *values):
        return self.keep(*lax.optimization_barrier((values, self.last))[0])


class Gather:
    def __init__(self, here, order, piece):
        self.here, self.order, self.piece = here, order, piece
        self.pieces, self.spots, self.step = [], [], 0
        self.send()

    def send(self):
        here, step = self.here, self.step
        start = (here.line - step) % here.line_size * 2
        self.pieces += [self.piece, here.to_pair(self.piece)]
        self.spots += [start + here.pair, start + 1 - here.pair]
        if step + 1 < here.line_size:
            self.piece = here.to_line(self.piece)
        self.step = step + 1

    def turn(self):
        if self.step < self.here.line_size:
            self.piece = self.order.wait(self.piece)
            self.send()

    def finish(self):
        while self.step < self.here.line_size:
            self.turn()
        pieces = self.order.wait(*self.pieces)
        return self.order.keep(place_blocks(pieces, self.spots))


class GatherPairs(Gather):
    def __init__(self, here, order, piece):
        self.here, self.order, self.mine = here, order, piece
        self.near = here.to_pair(piece)
        self.pieces, self.spots, self.step = [], [], 0

    def join(self):
        near, mine = self.order.wait(self.near, self.mine)
        self.piece = self.order.keep(ordered(self.here.pair == 0, mine[None], near[None], 0))
        self.send()

    def send(self):
        here, step = self.here, self.step
        self.pieces.append(self.piece)
        self.spots.append((here.line - step) % here.line_size)
        if step + 1 < here.line_size:
            self.piece = here.to_line(self.piece)
        self.step = step + 1


class Scatter:
    def __init__(self, here, order, total):
        rows, columns = total.shape
        self.here, self.order = here, order
        blocks = total.reshape(here.line_size, 2, rows // here.shards, columns)
        self.give = pick(blocks, 1 - here.pair, 1)
        self.mine = pick(blocks, here.pair, 1)
        self.give, self.mine = order.keep(self.give, self.mine)
        self.got = here.to_pair(self.give)
        self.step = 0

    def join(self):
        got, mine = self.order.wait(self.got, self.mine)
        self.kept = self.order.keep(low(wide(mine) + wide(got)))
        self.send()

    def send(self):
        here = self.here
        self.step += 1
        block = pick(self.kept, (here.line - self.step) % here.line_size, 0)
        if self.step > 1:
            block = low(wide(block) + wide(self.run))
        if self.step < here.line_size:
            block = self.order.keep(block)
            self.run = here.to_line(block)
        else:
            self.run = self.order.keep(block)

    def turn(self):
        if self.step < self.here.line_size:
            self.run, self.kept = self.order.wait(self.run, self.kept)
            self.send()

    def finish(self):
        while self.step < self.here.line_size:
            self.turn()
        return self.run


class ScatterLines(Scatter):
    def __init__(self, here, order, total):
        rows, columns = total.shape
        self.here, self.order, self.step = here, order, 0
        self.kept = total.reshape(here.line_size, 2, rows // here.shards, columns)
        self.send()

    def finish(self):
        while self.step < self.here.line_size:
            self.turn()
        here = self.here
        give = self.order.keep(pick(self.run, 1 - here.pair, 0))
        self.got = here.to_pair(give)
        return self

    def end(self):
        got, run = self.order.wait(self.got, self.run)
        return self.order.keep(low(wide(pick(run, self.here.pair, 0)) + wide(got)))


def per_device(
    latents,
    condition,
    mod_weight,
    mod_bias,
    qkv_weight,
    qv_bias,
    out_weight,
    out_bias,
    up_weight,
    up_bias,
    down_weight,
    down_bias,
    cotangent,
):
    here, order = Place(), Order()
    shards, seat, side, core = here.shards, here.seat, here.side, here.core
    near_seat = seat ^ 1
    micros, tokens, width = latents.shape
    count = micros // 2
    length = 4 * tokens
    own = length // 2
    rows = width // shards
    hidden = up_weight.shape[1]
    heads = H // 4
    part = heads * HD
    factor = HD ** (-0.5)
    flat = (count * length, width)
    block = hidden // shards // 4
    take, keep, wait = order.take, order.keep, order.wait

    qkv_ring = Gather(here, order, keep(cut_columns(qkv_weight, seat, 3)))

    def halves(tokens):
        parts = tokens.reshape((2, count) + tokens.shape[1:])
        return pick(parts, core, 0), pick(parts, 1 - core, 0)

    lat_mine, lat_give = keep(*halves(take(latents)))
    lat_near = here.to_core(lat_give)
    small = jnp.concatenate(
        [take(condition).reshape(-1), mod_bias, qv_bias, out_bias, up_bias, down_bias]
    )
    small = here.to_all(keep(small))
    lat_mine, lat_near = wait(lat_mine, lat_near)
    lat_both = keep(jnp.concatenate([lat_mine, lat_near], axis=1))
    lat_far = here.to_side(lat_both)
    qkv_ring.turn()

    small = wait(small)
    cuts = [micros * width]
    for vector in (mod_bias, qv_bias, out_bias, up_bias):
        cuts.append(cuts[-1] + vector.shape[0])
    cond_all, mod_bias, qv_bias, out_bias, up_bias, down_bias = jnp.split(small, cuts, axis=1)
    mod_bias, qv_bias, out_bias, up_bias, down_bias = (
        wide(vector.reshape(-1)) for vector in (mod_bias, qv_bias, out_bias, up_bias, down_bias)
    )
    cond_all = cond_all.reshape(shards * micros, width)
    cond_low = low(jax.nn.silu(wide(cond_all)))
    cond_rows = lax.dynamic_slice_in_dim(cond_low, here.shard * rows, rows, 1)
    cond_mine = pick(cond_rows.reshape(shards, 2, count, rows), core, 1)
    mod_part = matmul(cond_mine.reshape(shards * count, rows), mod_weight)
    mod_part = here.exchange(keep(mod_part.reshape(shards, count, 6 * width)))
    qkv_ring.turn()
    up_piece = keep(cut_columns(take(up_weight), seat, shards))
    out_piece = keep(pick(take(out_weight).reshape(2, rows // 2, width), core, 0))
    qkv_ring.turn()
    out_ring = GatherPairs(here, order, out_piece)
    up_ring = Gather(here, order, take(up_piece))
    mod_part = wait(mod_part)
    modulation = keep(jnp.sum(mod_part, axis=0) + mod_bias)
    shift_one, scale_one, gate_one, shift_two, scale_two, gate_two = (
        vector[:, None] for vector in jnp.split(modulation, 6, axis=1)
    )
    out_ring.join()
    lat_far, lat_both = wait(lat_far, lat_both)
    inputs = wide(jnp.concatenate([lat_both, lat_far], axis=1))
    normed_one, inverse_one = normalize(inputs)
    attn_in = low(normed_one * (1.0 + scale_one) + shift_one).reshape(flat)
    normed_one, inverse_one, attn_in = keep(normed_one, inverse_one, attn_in)
    qkv_mine = qkv_ring.finish().reshape(width, 3 * part)
    qkv_near = here.to_core(qkv_mine)
    up_ring.turn()

    qv_parts = jnp.concatenate([qv_bias[:width], jnp.zeros((width,), jnp.float32), qv_bias[width:]])
    qv_parts = qv_parts.reshape(3, 4, part)

    def project(weight, which):
        bias = pick(qv_parts, which, 1).reshape(3 * part, 1)
        values = low(contract(weight, attn_in, 0, 1) + bias)
        return values.reshape(3, heads, HD, count, length)

    def attend(values):
        queries, keys, contents = values
        scores = (
            jnp.einsum("hdbk,hdbq->hbkq", keys, queries, preferred_element_type=jnp.float32)
            * factor
        )
        raised = jnp.exp(scores - jnp.max(scores, axis=2, keepdims=True))
        probs = raised / jnp.sum(raised, axis=2, keepdims=True)
        result = jnp.einsum(
            "hdbk,hbkq->hdbq", contents, low(probs), preferred_element_type=jnp.float32
        )
        return probs, low(result).reshape(part, count * length)

    values_mine = keep(project(take(qkv_mine), seat))
    out_ring.turn()
    down_piece = keep(pick(take(down_weight).reshape(4, block, width), seat, 0))
    probs_mine, result_mine = keep(*attend(take(values_mine)))
    up_ring.turn()
    down_ring = Gather(here, order, take(down_piece))
    qkv_near = wait(qkv_near)
    values_near = keep(project(qkv_near, near_seat))
    out_ring.turn()
    probs_near, result_near = keep(*attend(take(values_near)))
    heads_half = keep(ordered(core == 0, result_mine, result_near, 0))
    heads_far = here.to_side(heads_half)
    up_ring.turn()

    out_mine = out_ring.finish()
    out_near = here.to_core(out_mine)
    cot_mine, cot_give = keep(*halves(take(cotangent)))
    cot_near = here.to_core(cot_give)
    down_ring.turn()
    out_near, out_mine = wait(out_near, out_mine)
    out_shape = (shards, 1, rows // 2, width)
    out_full = ordered(core == 0, out_mine.reshape(out_shape), out_near.reshape(out_shape), 1)
    out_full = keep(out_full.reshape(width, width))
    cot_mine, cot_near = wait(cot_mine, cot_near)
    cot_both = keep(jnp.concatenate([cot_mine, cot_near], axis=1))
    cot_far = here.to_side(cot_both)

    heads_far, heads_half = wait(heads_far, heads_half)
    heads_far = heads_far.reshape(2 * part, count, length)
    heads_far = flip_halves(heads_far, 2).reshape(heads_half.shape)
    heads_out = keep(ordered(side == 0, heads_half, heads_far, 0))
    attn_branch = (contract(heads_out, out_full, 0, 0) + out_bias).reshape(inputs.shape)
    middle = inputs + gate_one * attn_branch
    normed_two, inverse_two = normalize(middle)
    mlp_in = low(normed_two * (1.0 + scale_two) + shift_two).reshape(flat)
    attn_branch, middle, normed_two, inverse_two, mlp_in = keep(
        attn_branch, middle, normed_two, inverse_two, mlp_in
    )
    up_mine = up_ring.finish().reshape(width, shards * block)
    up_near = here.to_core(up_mine)
    down_ring.turn()
    up_parts = up_bias.reshape(shards, 4, block)

    def feed(up, which):
        bias = pick(up_parts, which, 1).reshape(shards * block)
        pre_act = matmul(mlp_in, up) + bias
        squared = pre_act * pre_act
        bent = jnp.tanh(GELU_ROOT * pre_act * (1.0 + GELU_CUBE * squared))
        activated = low(0.5 * pre_act * (1.0 + bent))
        slope = 0.5 * (1.0 + bent) + 0.5 * GELU_ROOT * pre_act * (1.0 - bent * bent) * (
            1.0 + 3.0 * GELU_CUBE * squared
        )
        return activated, slope

    def feed_back(down, slope):
        return low(contract(grad_mlp, down, 1, 1) * slope)

    act_mine, slope_mine = keep(*feed(take(up_mine), seat))
    down_ring.turn()
    up_near = wait(up_near)
    act_near, slope_near = keep(*feed(up_near, near_seat))
    cot_far, cot_both = wait(cot_far, cot_both)
    grad_y = wide(jnp.concatenate([cot_both, cot_far], axis=1))
    grad_mlp = keep(low(gate_two * grad_y).reshape(flat))
    down_mine = down_ring.finish().reshape(shards * block, width)
    down_near = here.to_core(down_mine)
    pre_mine = keep(feed_back(take(down_mine), slope_mine))
    down_near = wait(down_near)
    pre_near = keep(feed_back(down_near, slope_near))

    mlp_grad_part = keep(
        low(contract(pre_mine, up_mine, 1, 1) + contract(take(pre_near), up_near, 1, 1))
    )
    mlp_grad_far = here.to_side(mlp_grad_part)
    down_met = here.to_core(keep(low(contract(take(act_near), grad_mlp, 0, 0))))
    up_met = here.to_core(keep(low(contract(take(mlp_in), pre_near, 0, 0))))
    down_total = contract(take(act_mine), grad_mlp, 0, 0)
    down_met = wait(down_met)
    down_sum = Scatter(here, order, low(down_total + wide(down_met)))
    up_total = contract(take(mlp_in), pre_mine, 0, 0)
    up_met = wait(up_met)
    up_sum = ScatterLines(here, order, keep(low(up_total + wide(up_met))))

    act_last = take(act_mine, act_near)
    branch_part = matmul(act_last[0], down_mine) + matmul(act_last[1], down_near)
    branch_part = keep(branch_part.reshape(inputs.shape))
    branch_far = here.to_side(keep(low(branch_part[:, own:])))

    mlp_grad_far = wait(mlp_grad_far).reshape(inputs.shape)
    grad_mlp_in = wide(mlp_grad_part.reshape(inputs.shape)) + wide(flip_halves(mlp_grad_far, 1))
    grad_shift_two = jnp.sum(grad_mlp_in[:, :own], axis=1)
    grad_scale_two = jnp.sum((grad_mlp_in * normed_two)[:, :own], axis=1)
    grad_middle = grad_y + normalize_back(
        normed_two, inverse_two, grad_mlp_in * (1.0 + scale_two)
    )
    grad_attn = low(gate_one * grad_middle).reshape(flat)
    grad_shift_two, grad_scale_two, grad_middle, grad_attn = keep(
        grad_shift_two, grad_scale_two, grad_middle, grad_attn
    )
    up_sum.turn()
    grad_attn = take(grad_attn)
    grad_attn_cuts = grad_attn.reshape(count * length, 4, width // 4)
    out_half = lax.dynamic_slice_in_dim(out_full, side * 2 * part, 2 * part, 0)
    grad_heads = keep(low(contract(out_half, grad_attn, 1, 1)))
    grad_heads = grad_heads.reshape(2, heads, HD, count, length)

    def attend_back(values, probs, grad_result):
        queries, keys, contents = values
        grad_probs = jnp.einsum(
            "hdbk,hdbq->hbkq", contents, grad_result, preferred_element_type=jnp.float32
        )
        inner = jnp.sum(probs * grad_probs, axis=2, keepdims=True)
        grad_scores = low(probs * (grad_probs - inner))
        grad_queries = factor * jnp.einsum(
            "hdbk,hbkq->hdbq", keys, grad_scores, preferred_element_type=jnp.float32
        )
        grad_keys = factor * jnp.einsum(
            "hdbq,hbkq->hdbk", queries, grad_scores, preferred_element_type=jnp.float32
        )
        grad_contents = jnp.einsum(
            "hdbq,hbkq->hdbk", grad_result, low(probs), preferred_element_type=jnp.float32
        )
        grads = jnp.stack([low(grad_queries), low(grad_keys), low(grad_contents)])
        return grads.reshape(3 * part, count * length)

    qkv_grad_near = keep(
        attend_back(values_near, probs_near, take(pick(grad_heads, 1 - core, 0)))
    )
    down_sum.join()
    qkv_met = here.to_core(keep(low(contract(attn_in, take(qkv_grad_near), 0, 1))))
    up_sum.turn()
    out_met = here.to_core(
        keep(low(contract(heads_out, pick(take(grad_attn_cuts), near_seat, 1), 1, 0)))
    )
    qkv_grad_mine = keep(attend_back(values_mine, probs_mine, take(pick(grad_heads, core, 0))))
    down_sum.turn()
    qkv_met = wait(qkv_met)
    qkv_total = contract(attn_in, take(qkv_grad_mine), 0, 1) + wide(qkv_met)
    qkv_sum = Scatter(here, order, low(qkv_total))
    out_met = wait(out_met)
    out_total = contract(heads_out, pick(take(grad_attn_cuts), seat, 1), 1, 0) + wide(out_met)
    out_sum = Scatter(here, order, low(out_total))
    up_sum = up_sum.finish()

    qkv_grads = take(qkv_grad_mine, qkv_grad_near)
    attn_grad_part = contract(qkv_grads[0], qkv_mine, 0, 1) + contract(
        qkv_grads[1], qkv_near, 0, 1
    )
    attn_grad_part = keep(attn_grad_part.reshape(inputs.shape))
    attn_grad_far = here.to_side(keep(low(attn_grad_part[:, own:])))
    down_sum.turn()
    part_shift = jnp.sum(take(attn_grad_part), axis=1)
    part_scale = jnp.sum(attn_grad_part * normed_one, axis=1)
    part_shift, part_scale = keep(part_shift, part_scale)

    branch_far, branch_part = wait(branch_far, branch_part)
    mlp_branch = branch_part[:, :own] + wide(branch_far) + down_bias
    grad_gate_two = jnp.sum(grad_y[:, :own] * mlp_branch, axis=1)
    mixed_mine = low(middle[:, :own] + gate_two * mlp_branch)
    grad_gate_two, mixed_mine = keep(grad_gate_two, mixed_mine)
    mixed_near = here.to_core(mixed_mine[:, tokens:])
    grad_gate_one = jnp.sum((take(grad_middle) * attn_branch)[:, :own], axis=1)
    grad_mod = jnp.concatenate(
        [part_shift, part_scale, grad_gate_one, grad_shift_two, grad_scale_two, grad_gate_two],
        axis=1,
    )
    qv_sums = jnp.zeros((2, 4, part), jnp.float32)
    up_sums = jnp.zeros((shards, 4, block), jnp.float32)
    for grads, pre, which in (
        (qkv_grad_mine, pre_mine, seat),
        (qkv_grad_near, pre_near, near_seat),
    ):
        sums = jnp.sum(wide(grads), axis=1).reshape(3, part)[::2]
        qv_sums = lax.dynamic_update_index_in_dim(qv_sums, sums, which, 1)
        sums = jnp.sum(wide(pre), axis=0).reshape(shards, block)
        up_sums = lax.dynamic_update_index_in_dim(up_sums, sums, which, 1)
    out_sums = jnp.sum(wide(grad_attn).reshape(inputs.shape)[:, :own], axis=(0, 1))
    down_sums = jnp.sum(wide(grad_mlp).reshape(inputs.shape)[:, :own], axis=(0, 1))
    bias_sums = jnp.concatenate(
        [
            vector.reshape(shards, -1)
            for vector in (qv_sums, out_sums, up_sums, down_sums)
        ],
        axis=1,
    )
    vector = keep(jnp.concatenate([grad_mod.reshape(-1), bias_sums.reshape(-1)]))
    vector_far = here.to_side(vector)
    grad_down = down_sum.finish()
    down_far = here.to_side(grad_down)
    vector_far, vector = wait(vector_far, vector)
    vector = keep(vector + vector_far)
    near = here.to_core(vector)
    grad_up = up_sum.end()
    up_far = here.to_side(grad_up)
    near, vector = wait(near, vector)
    grad_mod = vector[: count * 6 * width]
    bias_sums = vector[count * 6 * width :]
    bias_sums = (bias_sums + near[count * 6 * width :]).reshape(shards, -1)
    grad_mod = ordered(
        core == 0,
        grad_mod.reshape(1, count * 6 * width),
        near[: count * 6 * width].reshape(1, count * 6 * width),
        0,
    )
    mod_low = low(grad_mod).reshape(1, -1)
    sent = jnp.concatenate(
        [jnp.broadcast_to(wide(mod_low), (shards, mod_low.shape[1])), bias_sums], axis=1
    )
    got = here.exchange(keep(sent))
    qkv_sum.join()
    down_far, grad_down = wait(down_far, grad_down)
    down_near = here.to_core(keep(jnp.stack([grad_down, down_far])))
    got = wait(got)
    mod_all = low(got[:, : mod_low.shape[1]]).reshape(shards * micros, 6 * width)
    bias_sums = jnp.sum(got[:, mod_low.shape[1] :], axis=0)
    cuts = []
    for vector in (qv_bias, out_bias, up_bias):
        cuts.append((cuts[-1] if cuts else 0) + vector.shape[0] // shards)
    grad_qv_bias, grad_out_bias, grad_up_bias, grad_down_bias = jnp.split(bias_sums, cuts)
    grad_low = keep(contract(mod_all, mod_weight, 1, 1).reshape(shards, micros, rows))
    grad_low = here.exchange(grad_low)
    qkv_sum.turn()
    out_sum.join()
    grad_mod_weight = keep(contract(cond_rows, take(mod_all), 0, 0))
    qkv_sum.turn()
    out_sum.turn()
    up_far, grad_up = wait(up_far, grad_up)
    up_near = here.to_core(keep(jnp.stack([grad_up, up_far])))
    qkv_sum.turn()
    out_sum.turn()
    grad_qkv = qkv_sum.finish()
    qkv_far = here.to_side(grad_qkv)
    grad_out = out_sum.finish()
    out_far = here.to_side(grad_out)
    span = 6 * width // shards
    grad_mod_bias = jnp.sum(
        wide(lax.dynamic_slice_in_dim(take(mod_all), here.shard * span, span, 1)), axis=0
    )

    attn_grad_far, attn_grad_part = wait(attn_grad_far, attn_grad_part)
    grad_attn_in = attn_grad_part[:, :own] + wide(attn_grad_far)
    grad_tokens = grad_middle[:, :own] + normalize_back(
        normed_one[:, :own], inverse_one[:, :own], grad_attn_in * (1.0 + scale_one)
    )
    grad_tokens = keep(grad_tokens)
    tokens_near = here.to_core(grad_tokens[:, tokens:])

    up_near = wait(up_near)
    grad_up = keep(lay_columns(grad_up, up_far, up_near, seat, shards))
    down_near = wait(down_near)
    quarters = (
        (grad_down, seat),
        (down_far, seat ^ 2),
        (down_near[0], seat ^ 1),
        (down_near[1], seat ^ 3),
    )
    grad_down = jnp.zeros((4, block, width), jnp.float32)
    for quarter, spot in quarters:
        grad_down = lax.dynamic_update_index_in_dim(grad_down, wide(quarter), spot, 0)
    grad_down = keep(grad_down.reshape(4 * block, width))
    mixed_near, mixed_mine = wait(mixed_near, mixed_mine)
    mixed = keep(ordered(core == 0, mixed_mine[:, :tokens], mixed_near, 0))
    tokens_near, grad_tokens = wait(tokens_near, grad_tokens)
    grad_latents = keep(ordered(core == 0, grad_tokens[:, :tokens], tokens_near, 0))
    grad_low = wait(grad_low).transpose(1, 0, 2).reshape(micros, width)
    _, silu_pull = jax.vjp(jax.nn.silu, wide(condition))
    grad_condition = keep(silu_pull(grad_low)[0])
    qkv_far, grad_qkv = wait(qkv_far, grad_qkv)
    qkv_near = here.to_core(keep(jnp.stack([grad_qkv, qkv_far])))
    out_far, grad_out = wait(out_far, grad_out)
    out_near = here.to_core(keep(jnp.stack([grad_out, out_far])))
    qkv_near = wait(qkv_near)
    grad_qkv = keep(lay_columns(grad_qkv, qkv_far, qkv_near, seat, 3))
    out_near = wait(out_near)
    grad_out = lay_columns(grad_out, out_far, out_near, seat, 1)

    return (
        mixed,
        grad_latents,
        grad_condition,
        grad_mod_weight,
        grad_mod_bias,
        grad_qkv,
        grad_qv_bias,
        grad_out,
        grad_out_bias,
        grad_up,
        grad_up_bias,
        grad_down,
        grad_down_bias,
    )


def solution(mesh):
    tokens = P("fsdp", "seq", None)
    matrix = P("fsdp", None)
    vector = P("fsdp")
    parameters = (matrix, vector) * 5
    in_specs = (tokens, matrix) + parameters + (tokens,)
    out_specs = (tokens, tokens, matrix) + parameters
    return jax.shard_map(
        per_device, mesh=mesh, in_specs=in_specs, out_specs=out_specs, check_vma=False
    )
```

```python
import jax
import jax.numpy as jnp
from jax import lax
from jax.experimental import pallas as pl
from jax.experimental.pallas import tpu as pltpu
from jax.sharding import PartitionSpec as P

H = 16
HD = 72
GELU_ROOT = (2.0 / 3.141592653589793) ** 0.5
GELU_CUBE = 0.044715
SEAT, CORE, PAIR, LINE = range(4)

SCALARS = pl.BlockSpec(memory_space=pltpu.SMEM)
WHOLE = pl.BlockSpec(memory_space=pltpu.VMEM)
ANY = pl.BlockSpec(memory_space=pl.ANY)
ROOM = pltpu.CompilerParams(vmem_limit_bytes=48 << 20)
SHORT = pl.CostEstimate(flops=1, transcendentals=0, bytes_accessed=1)


def low(values):
    return values.astype(jnp.bfloat16)


def wide(values):
    return values.astype(jnp.float32)


def struct(shape, dtype):
    return jax.ShapeDtypeStruct(shape, dtype)


def whole(shape):
    return pl.BlockSpec(shape, lambda step: (0,) * len(shape))


def column_block(shape, columns):
    return pl.BlockSpec(shape[:-1] + (columns,), lambda step: (0,) * (len(shape) - 1) + (step,))


def row_block(shape, rows):
    return pl.BlockSpec((rows,) + shape[1:], lambda step: (step,) + (0,) * (len(shape) - 1))


def dot(left_side, right_side, left_dim, right_dim):
    return lax.dot_general(
        left_side,
        right_side,
        (((left_dim,), (right_dim,)), ((), ())),
        preferred_element_type=jnp.float32,
    )


def normalize_back(normed, inverse, grad):
    inner = jnp.mean(grad * normed, axis=-1, keepdims=True)
    return (grad - jnp.mean(grad, axis=-1, keepdims=True) - normed * inner) * inverse


def soft_columns(queries, keys):
    scores = dot(keys, queries, 0, 0) * HD ** (-0.5)
    raised = jnp.exp(scores - jnp.max(scores, axis=0, keepdims=True))
    return raised * (1.0 / jnp.sum(raised, axis=0, keepdims=True))


def pick(values, index, axis):
    return lax.dynamic_index_in_dim(values, index, axis, keepdims=False)


class Order:
    def __init__(self, place):
        self.place = place
        self.token = jnp.zeros((8, 128), jnp.float32)

    def wait(self, *values):
        self.token, values = lax.optimization_barrier((self.token, values))
        return values if len(values) > 1 else values[0]

    def run(self, kernel, outs, *args, grid=(), in_specs=None, out_specs=None, scratch=()):
        count, given = len(outs), len(args)

        def body(place, *refs):
            kernel(place, *refs[:given], *refs[given + 1 : given + 1 + count], *refs[given + 2 + count :])

        results = pl.pallas_call(
            body,
            out_shape=tuple(outs) + (struct(self.token.shape, self.token.dtype),),
            grid=grid,
            in_specs=[SCALARS] + list(in_specs or [WHOLE] * given) + [ANY],
            out_specs=tuple(out_specs or [WHOLE] * count) + (ANY,),
            scratch_shapes=scratch,
            input_output_aliases={given + 1: count},
            compiler_params=ROOM,
            cost_estimate=SHORT,
        )(self.place, *args, self.token)
        self.token = results[-1]
        return results[:-1] if count > 1 else results[0]

    def pass_on(self, blocks, step, sums):
        lines, rows, columns = blocks[0].shape
        count = len(blocks)

        def kernel(place, *refs):
            outs = refs[-1 - count : -1]
            for index in range(count):
                result = refs[index][0]
                if sums:
                    result = low(wide(result) + wide(refs[count + index][...]))
                outs[index][...] = result

        def block_at(unused, place):
            return (lax.rem(place[LINE] + (lines - step), lines), 0, 0)

        piece = pl.BlockSpec((rows, columns), lambda unused, place: (0, 0))
        spec = pltpu.PrefetchScalarGridSpec(
            num_scalar_prefetch=1,
            grid=(1,),
            in_specs=[pl.BlockSpec((1, rows, columns), block_at)] * count
            + [piece] * len(sums)
            + [ANY],
            out_specs=(piece,) * count + (ANY,),
        )
        results = pl.pallas_call(
            kernel,
            grid_spec=spec,
            out_shape=(struct((rows, columns), jnp.bfloat16),) * count
            + (struct(self.token.shape, self.token.dtype),),
            input_output_aliases={1 + count + len(sums): count},
            compiler_params=ROOM,
            cost_estimate=SHORT,
        )(self.place, *blocks, *sums, self.token)
        self.token = results[-1]
        return results[:-1]


class Place:
    def __init__(self):
        self.shards = lax.axis_size("fsdp")
        self.seats = lax.axis_size("seq")
        self.line_size = self.shards // 2
        self.shard = lax.axis_index("fsdp")
        self.seat = lax.axis_index("seq")
        self.core = self.seat % 2
        places = [self.seat, self.core, self.shard % 2, self.shard // 2]
        self.place = jnp.stack(places).astype(jnp.int32)

    def to_core(self, values):
        return lax.ppermute(values, "seq", [(i, i ^ 1) for i in range(self.seats)])

    def to_side(self, values):
        return lax.ppermute(values, "seq", [(i, i ^ 2) for i in range(self.seats)])

    def to_pair(self, values):
        return lax.ppermute(values, "fsdp", [(i, i ^ 1) for i in range(self.shards)])

    def to_line(self, values):
        return lax.ppermute(
            values, "fsdp", [(i, (i + 2) % self.shards) for i in range(self.shards)]
        )

    def exchange(self, values):
        return lax.all_to_all(values, "fsdp", split_axis=0, concat_axis=0, tiled=True)

    def to_all(self, values):
        return self.exchange(jnp.broadcast_to(values[None], (self.shards,) + values.shape))


class Gather:
    def __init__(self, here, order, piece, near=False):
        self.here, self.order, self.piece, self.near = here, order, piece, near
        self.pieces, self.copies = [], []
        self.steps, self.pending = 0, []
        self.send([piece])

    def send(self, pieces):
        here = self.here
        self.pieces += pieces
        sent = []
        if self.steps < here.line_size:
            if self.steps + 1 < here.line_size:
                sent.append(here.to_line(pieces[0]))
            sent.append(here.to_pair(pieces[0]))
        self.steps += 1
        self.copied = [here.to_core(piece) for piece in pieces] if self.near else []
        self.pending = sent

    def turn(self):
        if self.pending:
            arrived = self.order.wait(*self.pending, *self.copied)
            arrived = list(arrived) if len(self.pending) + len(self.copied) > 1 else [arrived]
            count = len(self.pending)
            self.copies += arrived[count:]
            self.send(arrived[:count])

    def finish(self, widths):
        while self.pending:
            self.turn()
        return self.place(self.pieces, widths)

    def finish_near(self, widths):
        return self.place(self.copies + [self.order.wait(*self.copied)], widths)

    def place(self, pieces, widths):
        shards, lines = self.here.shards, self.here.line_size
        rows = pieces[0].shape[0]

        def kernel(place, *refs):
            targets = refs[shards:]
            for index in range(shards):
                near = index > 0 and (index % 2 == 0 or index == shards - 1)
                back = (index - 1) // 2 if near else (index + 1) // 2
                line = lax.rem(place[LINE] + (lines - back), lines)
                pair = 1 - place[PAIR] if near else place[PAIR]
                start = 0
                for target, columns in zip(targets, widths):
                    target[2 * line + pair] = refs[index][:, start : start + columns]
                    start += columns

        outs = [struct((shards, rows, columns), pieces[0].dtype) for columns in widths]
        return self.order.run(kernel, outs, *pieces)


class Scatter:
    def __init__(self, here, order, give, mine):
        self.here, self.order, self.mine = here, order, mine
        self.got = here.to_pair(give)
        self.step = 0

    def join(self):
        got = self.order.wait(self.got)

        def kernel(place, got_ref, mine_ref, out):
            out[...] = low(wide(mine_ref[...]) + wide(got_ref[...]))

        shape = struct(self.mine.shape, jnp.bfloat16)
        self.kept = [self.order.run(kernel, [shape], got, self.mine)]
        self.sums = []
        self.send()

    def send(self):
        self.step += 1
        sums = self.order.pass_on(self.kept, self.step, self.sums)
        if self.step < self.here.line_size:
            sums = [self.here.to_line(total) for total in sums]
        self.sums = sums

    def turn(self):
        if self.step < self.here.line_size:
            sums = self.order.wait(*self.sums)
            self.sums = list(sums) if len(self.kept) > 1 else [sums]
            self.send()

    def finish(self):
        while self.step < self.here.line_size:
            self.turn()
        return self.sums[0]


class ScatterLines(Scatter):
    def __init__(self, here, order, both):
        self.here, self.order, self.step = here, order, 0
        self.kept, self.sums = [both], []
        self.send()

    def join(self):
        while self.step < self.here.line_size:
            self.turn()
        total = self.sums[0]
        rows = total.shape[0] // 2
        self.mine = total[rows:]
        self.got = self.here.to_pair(total[:rows])

    def finish(self):
        got = self.order.wait(self.got)

        def kernel(place, got_ref, mine_ref, out):
            out[...] = low(wide(mine_ref[...]) + wide(got_ref[...]))

        shape = struct(got.shape, jnp.bfloat16)
        return self.order.run(kernel, [shape], got, self.mine)


def cut_columns(place, source, target, offset, index, parts, groups):
    part = source.shape[1] // groups // parts
    for choice in range(parts):

        @pl.when(index == choice)
        def _():
            for group in range(groups):
                start = (group * parts + choice) * part
                goal = offset + group * part
                target[:, goal : goal + part] = source[:, start : start + part]


def cut_attention(order, qkv_weight, out_weight):
    rows, width = out_weight.shape
    columns = qkv_weight.shape[1] // 4

    def kernel(place, qkv_ref, out_ref, target):
        cut_columns(place, qkv_ref, target, 0, place[SEAT], 4, 3)
        cut_columns(place, out_ref, target, columns, place[CORE], 2, 1)

    shape = struct((rows, columns + width // 2), qkv_weight.dtype)
    return order.run(kernel, [shape], qkv_weight, out_weight)


def cut_feed(order, up_weight, down_weight, shards):
    hidden, width = down_weight.shape
    rows, columns = up_weight.shape

    def kernel(place, up_ref, down_ref, target):
        cut_columns(place, up_ref, target, 0, place[SEAT], 4, shards)
        target[:, columns // 4 :] = down_ref[place[SEAT]]

    shape = struct((rows, columns // 4 + width), up_weight.dtype)
    return order.run(
        kernel, [shape], up_weight, down_weight.reshape(4, hidden // 4, width)
    )


def cut_tokens(order, tokens):
    shape = struct(tokens.shape[1:], tokens.dtype)

    def kernel(place, source, mine, give):
        mine[...] = source[place[CORE]]
        give[...] = source[1 - place[CORE]]

    return order.run(kernel, [shape, shape], tokens)


def lay_columns(order, quarters, groups):
    rows, columns = quarters[0].shape
    part = columns // groups

    def kernel(place, *refs):
        target = refs[4]
        for own in range(4):

            @pl.when(place[SEAT] == own)
            def _():
                for group in range(groups):
                    for other in range(4):
                        start = (group * 4 + (own ^ other)) * part
                        block = refs[other][:, group * part : (group + 1) * part]
                        target[:, start : start + part] = wide(block)

    return order.run(kernel, [struct((rows, 4 * columns), jnp.float32)], *quarters)


def lay_rows(order, quarters):
    rows, columns = quarters[0].shape

    def kernel(place, *refs):
        for other in range(4):
            refs[4][place[SEAT] ^ other] = wide(refs[other][...])

    result = order.run(kernel, [struct((4, rows, columns), jnp.float32)], *quarters)
    return result.reshape(4 * rows, columns)


def lay_tokens(order, *pairs):
    def kernel(place, *refs):
        for index in range(len(pairs)):
            target = refs[2 * len(pairs) + index]
            target[place[CORE]] = refs[2 * index][...]
            target[1 - place[CORE]] = refs[2 * index + 1][...]

    outs = [struct((2,) + mine.shape, mine.dtype) for mine, near in pairs]
    return order.run(kernel, outs, *(value for values in pairs for value in values))


def norm_tokens(order, pieces, mod):
    tokens, width = pieces[0].shape
    length = 4 * tokens

    def kernel(place, *refs):
        mod_ref, out, turned, means, inverses = refs[4:]
        for index in range(4):
            span = slice(index * tokens, (index + 1) * tokens)
            values = wide(refs[index][...])
            mean = jnp.mean(values, axis=1, keepdims=True)
            centre = values - mean
            inverse = lax.rsqrt(jnp.mean(centre * centre, axis=1, keepdims=True) + 1e-06)
            result = centre * inverse * (1.0 + mod_ref[1:2, :]) + mod_ref[0:1, :]
            out[span, :] = low(result)
            turned[:, span] = low(result.T)
            means[span, :] = mean
            inverses[span, :] = inverse

    outs = (
        struct((length, width), jnp.bfloat16),
        struct((width, length), jnp.bfloat16),
        struct((length, 1), jnp.float32),
        struct((length, 1), jnp.float32),
    )
    return order.run(kernel, outs, *pieces, mod)


def attend(order, attn_in, weight, bias):
    length = attn_in.shape[0]
    heads = H // 4

    def kernel(place, in_ref, weight_ref, bias_ref, parts, result):
        values = (dot(in_ref[...], weight_ref[...], 1, 0) + bias_ref[...]).T
        for index in range(3 * heads):
            parts[index] = low(values[index * HD : (index + 1) * HD])
        results = []
        for head in range(heads):
            probs = soft_columns(parts[head], parts[heads + head])
            results.append(dot(parts[2 * heads + head], low(probs), 1, 0))
        result[...] = low(jnp.concatenate(results, axis=0))

    outs = (
        struct((3 * heads, HD, length), jnp.bfloat16),
        struct((heads * HD, length), jnp.bfloat16),
    )
    return order.run(kernel, outs, attn_in, weight, bias)


def attend_back(order, other, parts, out_weight, grad_attn):
    length = grad_attn.shape[0]
    heads = H // 4
    part = heads * HD
    factor = HD ** (-0.5)

    def kernel(place, parts_ref, weight_ref, grad_ref, out, sums):
        rows = pl.ds(pl.multiple_of((place[SEAT] ^ other) * part, part), part)
        grad_heads = dot(weight_ref[rows, :], grad_ref[...], 1, 1)
        grads = [None] * (3 * heads)
        for head in range(heads):
            queries, keys = parts_ref[head], parts_ref[heads + head]
            contents = parts_ref[2 * heads + head]
            grad = low(grad_heads[head * HD : (head + 1) * HD])
            probs = soft_columns(queries, keys)
            grad_probs = dot(contents, grad, 0, 0)
            inner = jnp.sum(probs * grad_probs, axis=0, keepdims=True)
            grad_scores = low(probs * (grad_probs - inner))
            grads[head] = factor * dot(keys, grad_scores, 1, 0)
            grads[heads + head] = factor * dot(queries, grad_scores, 1, 1)
            grads[2 * heads + head] = dot(grad, low(probs), 1, 1)
        result = low(jnp.concatenate(grads, axis=0).T)
        out[...] = result
        sums[...] = jnp.sum(wide(result), axis=0, keepdims=True)

    outs = (
        struct((length, 3 * part), jnp.bfloat16),
        struct((1, 3 * part), jnp.float32),
    )
    return order.run(kernel, outs, parts, out_weight, grad_attn)


def attention_out(order, quarters, out_mine, out_near, out_bias, pieces, mod):
    tokens, width = pieces[0].shape
    half, length = 2 * tokens, 4 * tokens
    part = quarters[0].shape[0]
    columns = width // 2

    def kernel(place, *refs):
        out_mine_ref, out_near_ref, bias_ref = refs[4:7]
        mod_ref, heads, weight, branch, normed, inverses, mlp_in = refs[11:]
        for other in range(4):
            rows = pl.ds(pl.multiple_of((place[SEAT] ^ other) * part, part), part)
            if other < 2:
                heads[rows, :] = refs[other][...]
            else:
                heads[rows, :half] = refs[other][:, half:]
                heads[rows, half:] = refs[other][:, :half]
        for own in range(2):

            @pl.when(place[CORE] == own)
            def _():
                weight[:, own * columns : (own + 1) * columns] = out_mine_ref[...]
                weight[:, (1 - own) * columns : (2 - own) * columns] = out_near_ref[...]

        result = dot(heads[...], weight[...], 0, 0) + bias_ref[...]
        branch[...] = result[:half]
        shift, scale = mod_ref[3:4, :], 1.0 + mod_ref[4:5, :]
        for index in range(4):
            span = slice(index * tokens, (index + 1) * tokens)
            values = wide(refs[7 + index][...]) + mod_ref[2:3, :] * result[span]
            centre = values - jnp.mean(values, axis=1, keepdims=True)
            inverse = lax.rsqrt(jnp.mean(centre * centre, axis=1, keepdims=True) + 1e-06)
            centre = centre * inverse
            normed[span, :] = centre
            inverses[span, :] = inverse
            mlp_in[span, :] = low(centre * scale + shift)

    outs = (
        struct((width, length), jnp.bfloat16),
        struct((width, width), jnp.bfloat16),
        struct((half, width), jnp.float32),
        struct((length, width), jnp.float32),
        struct((length, 1), jnp.float32),
        struct((length, width), jnp.bfloat16),
    )
    return order.run(kernel, outs, *quarters, out_mine, out_near, out_bias, *pieces, mod)


def gate_grad(order, pieces, mod):
    tokens, width = pieces[0].shape

    def kernel(place, *refs):
        mod_ref, out, sums = refs[4:]
        total = jnp.zeros(sums.shape, jnp.float32)
        for index in range(4):
            result = low(mod_ref[5:6, :] * wide(refs[index][...]))
            out[index * tokens : (index + 1) * tokens, :] = result
            if index < 2:
                total = total + jnp.sum(wide(result), axis=0, keepdims=True)
        sums[...] = total

    outs = (struct((4 * tokens, width), jnp.bfloat16), struct((1, width), jnp.float32))
    return order.run(kernel, outs, *pieces, mod)


def feed(order, mlp_in, weight, bias):
    length, width = mlp_in.shape
    hidden = weight.shape[1]
    step = hidden // 3

    def kernel(place, in_ref, weight_ref, bias_ref, act, slope):
        pre_act = dot(in_ref[...], weight_ref[...], 1, 0) + bias_ref[...]
        squared = pre_act * pre_act
        bent = jnp.tanh(GELU_ROOT * pre_act * (1.0 + GELU_CUBE * squared))
        raised = 0.5 + 0.5 * bent
        act[...] = low(pre_act * raised)
        slope[...] = raised + pre_act * (1.0 - bent * bent) * (
            0.5 * GELU_ROOT + (1.5 * GELU_ROOT * GELU_CUBE) * squared
        )

    return order.run(
        kernel,
        (
            struct((length, hidden), jnp.bfloat16),
            struct((length, hidden), jnp.float32),
        ),
        mlp_in, weight, bias,
        grid=(3,),
        in_specs=[
            whole((length, width)),
            column_block((width, hidden), step),
            column_block((1, hidden), step),
        ],
        out_specs=(
            column_block((length, hidden), step),
            column_block((length, hidden), step),
        ),
    )


def feed_back(order, grad_mlp, weight, slope):
    length, width = grad_mlp.shape
    hidden = weight.shape[0]
    step = hidden // 3

    def kernel(place, grad_ref, weight_ref, slope_ref, out, sums):
        result = low(dot(grad_ref[...], weight_ref[...], 1, 1) * slope_ref[...])
        out[...] = result
        sums[...] = jnp.sum(wide(result), axis=0, keepdims=True)

    return order.run(
        kernel,
        (struct((length, hidden), jnp.bfloat16), struct((1, hidden), jnp.float32)),
        grad_mlp, weight, slope,
        grid=(3,),
        in_specs=[
            whole((length, width)),
            row_block((hidden, width), step),
            column_block((length, hidden), step),
        ],
        out_specs=(column_block((length, hidden), step), column_block((1, hidden), step)),
    )


def feed_in_back(order, pre_mine, up_mine, pre_near, up_near):
    length, hidden = pre_mine.shape
    width = up_mine.shape[0]
    step = width // 3

    def kernel(place, pre_mine_ref, up_mine_ref, pre_near_ref, up_near_ref, out):
        out[...] = low(
            dot(pre_mine_ref[...], up_mine_ref[...], 1, 1)
            + dot(pre_near_ref[...], up_near_ref[...], 1, 1)
        )

    return order.run(
        kernel,
        [struct((length, width), jnp.bfloat16)],
        pre_mine, up_mine, pre_near, up_near,
        grid=(3,),
        in_specs=[
            whole((length, hidden)),
            row_block((width, hidden), step),
            whole((length, hidden)),
            row_block((width, hidden), step),
        ],
        out_specs=[column_block((length, width), step)],
    )


def feed_out(order, act_mine, down_mine, act_near, down_near):
    length, hidden = act_mine.shape
    width = down_mine.shape[1]
    half, step = length // 2, width // 3

    def kernel(place, act_mine_ref, down_mine_ref, act_near_ref, down_near_ref, own, give):
        result = dot(act_mine_ref[...], down_mine_ref[...], 1, 0) + dot(
            act_near_ref[...], down_near_ref[...], 1, 0
        )
        own[...] = result[:half]
        give[...] = low(result[half:])

    return order.run(
        kernel,
        (struct((half, width), jnp.float32), struct((half, width), jnp.bfloat16)),
        act_mine, down_mine, act_near, down_near,
        grid=(3,),
        in_specs=[
            whole((length, hidden)),
            column_block((hidden, width), step),
            whole((length, hidden)),
            column_block((hidden, width), step),
        ],
        out_specs=(column_block((half, width), step), column_block((half, width), step)),
    )


def weight_grad(order, shards, left_side, right_side, left_dim, other=None, chunks=4):
    rows = left_side.shape[1 - left_dim]
    piece = rows // shards
    share = shards // chunks
    columns, scratch = quarter_of(right_side, other)

    def kernel(place, left_ref, right_ref, *refs):
        right = take_quarter(place, right_ref, refs[chunks:], other)
        total = low(dot(left_ref[...], right, left_dim, 0))
        for shard in range(shards):
            block = total[shard * piece : (shard + 1) * piece]
            refs[shard // share][shard % share] = block

    outs = [struct((share, piece, columns), jnp.bfloat16)] * chunks
    return order.run(kernel, outs, left_side, right_side, scratch=scratch)


def quarter_of(right_side, other):
    length, columns = right_side.shape
    if other is None:
        return columns, ()
    return columns // 4, (pltpu.VMEM((length, columns // 4), right_side.dtype),)


def take_quarter(place, right_ref, held, other):
    if other is None:
        return right_ref[...]
    columns = held[0].shape[1]
    for index in range(4):

        @pl.when((place[SEAT] ^ other) == index)
        def _():
            held[0][...] = right_ref[:, index * columns : (index + 1) * columns]

    return held[0][...]


def weight_sum(order, shards, left_side, right_side, left_dim, met, other=None, join=False):
    rows = left_side.shape[1 - left_dim]
    piece = rows // shards
    lines = shards // 2
    share = shards // len(met)
    columns, scratch = quarter_of(right_side, other)

    def kernel(place, left_ref, right_ref, *refs):
        met_refs, refs = refs[: len(met)], refs[len(met) :]
        right = take_quarter(place, right_ref, refs[1 if join else 2 :], other)
        total = dot(left_ref[...], right, left_dim, 0)
        for own in range(2):

            @pl.when(place[PAIR] == own)
            def _():
                for shard in range(shards):
                    part = total[shard * piece : (shard + 1) * piece]
                    part = low(part + wide(met_refs[shard // share][shard % share]))
                    mine = shard % 2 == own
                    if join:
                        start = piece if mine else 0
                        refs[0][shard // 2, start : start + piece] = part
                    else:
                        refs[1 if mine else 0][shard // 2] = part

    if join:
        outs = (struct((lines, 2 * piece, columns), jnp.bfloat16),)
    else:
        outs = (struct((lines, piece, columns), jnp.bfloat16),) * 2
    return order.run(kernel, outs, left_side, right_side, *met, scratch=scratch)


def middle_back(order, part, far, normed, inverses, pieces, mod, branch):
    length, width = part.shape
    tokens = length // 4

    def kernel(place, part_ref, far_ref, normed_ref, inverse_ref, *refs):
        mod_ref, branch_ref, grad_attn, grad_middle, sums = refs[4:]
        gate, scale = mod_ref[2:3, :], 1.0 + mod_ref[4:5, :]
        totals = [jnp.zeros((1, width), jnp.float32)] * 4
        for index in range(4):
            span = slice(index * tokens, (index + 1) * tokens)
            other = slice((index ^ 2) * tokens, ((index ^ 2) + 1) * tokens)
            grad_in = wide(part_ref[span, :]) + wide(far_ref[other, :])
            values = normed_ref[span, :]
            grad = wide(refs[index][...]) + normalize_back(
                values, inverse_ref[span, :], grad_in * scale
            )
            result = low(gate * grad)
            grad_attn[span, :] = result
            if index < 2:
                grad_middle[span, :] = grad
                terms = (grad_in, grad_in * values, grad * branch_ref[span, :], wide(result))
                totals = [
                    total + jnp.sum(term, axis=0, keepdims=True)
                    for total, term in zip(totals, terms)
                ]
        for row, total in enumerate(totals):
            sums[row : row + 1, :] = total

    outs = (
        struct((length, width), jnp.bfloat16),
        struct((2 * tokens, width), jnp.float32),
        struct((4, width), jnp.float32),
    )
    return order.run(kernel, outs, part, far, normed, inverses, *pieces, mod, branch)


def attention_in_back(order, grad_mine, qkv_mine, grad_near, qkv_near, pieces, means, inverses):
    length, columns = grad_mine.shape
    width = qkv_mine.shape[0]
    tokens, half, step = length // 4, length // 2, width // 3

    def kernel(place, grad_mine_ref, qkv_mine_ref, grad_near_ref, qkv_near_ref, *refs):
        mean_ref, inverse_ref, own, give, sums = refs[4:]
        result = dot(grad_mine_ref[...], qkv_mine_ref[...], 1, 1) + dot(
            grad_near_ref[...], qkv_near_ref[...], 1, 1
        )
        own[...] = result[:half]
        give[...] = low(result[half:])
        scaled = jnp.zeros((1, step), jnp.float32)
        for index in range(4):
            span = slice(index * tokens, (index + 1) * tokens)
            normed = (wide(refs[index][...]) - mean_ref[span, :]) * inverse_ref[span, :]
            scaled = scaled + jnp.sum(result[span] * normed, axis=0, keepdims=True)
        sums[0:1, :] = jnp.sum(result, axis=0, keepdims=True)
        sums[1:2, :] = scaled

    outs = (
        struct((half, width), jnp.float32),
        struct((half, width), jnp.bfloat16),
        struct((2, width), jnp.float32),
    )
    weights = row_block((width, columns), step)
    grads = whole((length, columns))
    stats = whole((length, 1))
    return order.run(
        kernel,
        outs,
        grad_mine,
        qkv_mine,
        grad_near,
        qkv_near,
        *pieces,
        means,
        inverses,
        grid=(3,),
        in_specs=[grads, weights, grads, weights]
        + [column_block((tokens, width), step)] * 4
        + [stats, stats],
        out_specs=[
            column_block((half, width), step),
            column_block((half, width), step),
            column_block((2, width), step),
        ],
    )


def tokens_back(order, own, far, pieces, means, inverses, mod, grad_middle):
    half, width = own.shape
    tokens = half // 2

    def kernel(
        place, own_ref, far_ref, mine_ref, near_ref, mean_ref, inverse_ref, mod_ref, grad_ref,
        mine, give,
    ):
        for index, (source, target) in enumerate(((mine_ref, mine), (near_ref, give))):
            span = slice(index * tokens, (index + 1) * tokens)
            inverse = inverse_ref[span, :]
            normed = (wide(source[...]) - mean_ref[span, :]) * inverse
            grad = (own_ref[span, :] + wide(far_ref[span, :])) * (1.0 + mod_ref[1:2, :])
            target[...] = grad_ref[span, :] + normalize_back(normed, inverse, grad)

    outs = (struct((tokens, width), jnp.float32),) * 2
    return order.run(
        kernel, outs, own, far, pieces[0], pieces[1], means, inverses, mod, grad_middle
    )


def mix(order, own, far, down_bias, pieces, branch, grads, mod):
    half, width = own.shape
    tokens = half // 2

    def kernel(
        place, own_ref, far_ref, bias_ref, mine_ref, near_ref, branch_ref, grad_mine, grad_near,
        mod_ref, mine, give, sums,
    ):
        total = jnp.zeros((1, width), jnp.float32)
        sources = ((mine_ref, grad_mine, mine), (near_ref, grad_near, give))
        for index, (source, grad, target) in enumerate(sources):
            span = slice(index * tokens, (index + 1) * tokens)
            mlp_branch = own_ref[span, :] + wide(far_ref[span, :]) + bias_ref[...]
            middle = wide(source[...]) + mod_ref[2:3, :] * branch_ref[span, :]
            target[...] = low(middle + mod_ref[5:6, :] * mlp_branch)
            total = total + jnp.sum(wide(grad[...]) * mlp_branch, axis=0, keepdims=True)
        sums[...] = total

    outs = (struct((tokens, width), jnp.bfloat16),) * 2 + (struct((1, width), jnp.float32),)
    return order.run(
        kernel, outs, own, far, down_bias, pieces[0], pieces[1], branch, grads[0], grads[1], mod
    )


def per_device(
    latents,
    condition,
    mod_weight,
    mod_bias,
    qkv_weight,
    qv_bias,
    out_weight,
    out_bias,
    up_weight,
    up_bias,
    down_weight,
    down_bias,
    cotangent,
):
    here = Place()
    order = Order(here.place)
    shards, seat, core = here.shards, here.seat, here.core
    near_seat = seat ^ 1
    micros, tokens, width = latents.shape
    rows = width // shards
    hidden = up_weight.shape[1]
    heads = H // 4
    part = heads * HD
    block = hidden // shards // 4
    wait = order.wait

    hidden_part = shards * block
    attention_widths = (3 * part, width // 2)

    ring = Gather(here, order, cut_attention(order, qkv_weight, out_weight), near=True)
    lat_mine, lat_give = cut_tokens(order, latents)
    lat_near = here.to_core(lat_give)
    lat_far = here.to_side(lat_mine)
    lat_near = wait(lat_near)
    lat_far_near = here.to_side(lat_near)
    feed_piece = cut_feed(order, up_weight, down_weight, shards)
    ring.turn()
    small = jnp.concatenate(
        [wait(condition).reshape(-1), mod_bias, qv_bias, out_bias, up_bias, down_bias]
    )
    small = here.to_all(wait(small))
    ring.turn()

    small = wait(small)
    cuts = [micros * width]
    for vector in (mod_bias, qv_bias, out_bias, up_bias):
        cuts.append(cuts[-1] + vector.shape[0])
    cond_all, mod_bias, qv_bias, out_bias, up_bias, down_bias = jnp.split(small, cuts, axis=1)
    cond_all = cond_all.reshape(shards * micros, width)
    cond_low = low(jax.nn.silu(wide(cond_all)))
    cond_rows = lax.dynamic_slice_in_dim(cond_low, here.shard * rows, rows, 1)
    cond_mine = pick(cond_rows.reshape(shards, micros, rows), core, 1)
    mod_part = wait(dot(cond_mine, mod_weight, 1, 0).reshape(shards, 1, 6 * width))
    mod_part = here.exchange(mod_part)
    ring.turn()
    feed_ring = Gather(here, order, wait(feed_piece))
    ring.turn()
    mod_bias, qv_bias, out_bias, up_bias, down_bias = wait(
        mod_bias, qv_bias, out_bias, up_bias, down_bias
    )
    qv_parts = wide(qv_bias).reshape(2, 4, part)
    up_parts = wide(up_bias).reshape(shards, 4, block)

    def qkv_row(which):
        both = pick(qv_parts, which, 1)
        row = jnp.concatenate([both[0], jnp.zeros((part,), jnp.float32), both[1]])
        return row.reshape(1, 3 * part)

    bias_rows = wait(
        wide(mod_bias).reshape(6, width),
        qkv_row(seat),
        qkv_row(near_seat),
        wide(out_bias).reshape(1, width),
        pick(up_parts, seat, 1).reshape(1, hidden_part),
        pick(up_parts, near_seat, 1).reshape(1, hidden_part),
        wide(down_bias).reshape(1, width),
    )
    mod_bias, qkv_bias_mine, qkv_bias_near, out_bias, up_bias_mine, up_bias_near, down_bias = (
        bias_rows
    )
    mod_part = wait(mod_part)
    mod = wait(jnp.sum(mod_part, axis=0).reshape(6, width) + mod_bias)
    lats = (lat_mine, lat_near) + wait(lat_far, lat_far_near)
    attn_in, attn_turned, means_one, inverses_one = norm_tokens(order, lats, mod)
    feed_ring.turn()
    qkv_mine, out_mine = ring.finish(attention_widths)
    qkv_mine = qkv_mine.reshape(width, 3 * part)
    parts_mine, heads_mine = attend(order, attn_in, qkv_mine, qkv_bias_mine)
    heads_far = here.to_side(heads_mine)
    qkv_near, out_near = ring.finish_near(attention_widths)
    qkv_near = qkv_near.reshape(width, 3 * part)
    feed_ring.turn()
    parts_near, heads_near = attend(order, attn_in, qkv_near, qkv_bias_near)
    heads_far_near = here.to_side(heads_near)
    cot_mine, cot_give = cut_tokens(order, cotangent)
    cot_near = here.to_core(cot_give)
    cot_far = here.to_side(cot_mine)
    cot_near = wait(cot_near)
    cot_far_near = here.to_side(cot_near)
    quarters = (heads_mine, heads_near) + wait(heads_far, heads_far_near)
    feed_ring.turn()
    heads_out, out_full, branch, normed_two, inverses_two, mlp_in = attention_out(
        order,
        quarters,
        out_mine.reshape(width, width // 2),
        out_near.reshape(width, width // 2),
        out_bias,
        lats,
        mod,
    )
    cots = (cot_mine, cot_near) + wait(cot_far, cot_far_near)
    grad_mlp, down_sums = gate_grad(order, cots, mod)
    up_mine, down_mine = feed_ring.finish((hidden_part, width))
    up_near, down_near = here.to_core(up_mine), here.to_core(down_mine)
    up_mine = up_mine.reshape(width, hidden_part)
    down_mine = down_mine.reshape(hidden_part, width)
    act_mine, slope_mine = feed(order, mlp_in, up_mine, up_bias_mine)
    pre_mine, up_sums_mine = feed_back(order, grad_mlp, down_mine, slope_mine)
    up_near = wait(up_near).reshape(width, hidden_part)
    act_near, slope_near = feed(order, mlp_in, up_near, up_bias_near)
    down_near = wait(down_near).reshape(hidden_part, width)
    pre_near, up_sums_near = feed_back(order, grad_mlp, down_near, slope_near)

    mlp_part = feed_in_back(order, pre_mine, up_mine, pre_near, up_near)
    mlp_far = here.to_side(mlp_part)

    def to_core(chunks):
        return [here.to_core(chunk) for chunk in chunks]

    up_met = to_core(weight_grad(order, shards, mlp_in, pre_near, 0, chunks=8))
    down_met = to_core(weight_grad(order, shards, act_near, grad_mlp, 0, chunks=8))
    up_met = wait(*up_met)
    up_sum = ScatterLines(
        here, order, weight_sum(order, shards, mlp_in, pre_mine, 0, up_met, join=True)
    )
    down_met = wait(*down_met)
    down_sum = Scatter(here, order, *weight_sum(order, shards, act_mine, grad_mlp, 0, down_met))
    feed_own, feed_give = feed_out(order, act_mine, down_mine, act_near, down_near)
    feed_far = here.to_side(feed_give)

    mlp_far = wait(mlp_far)
    grad_attn, grad_middle, middle_sums = middle_back(
        order, mlp_part, mlp_far, normed_two, inverses_two, cots, mod, branch
    )
    up_sum.turn()
    qkv_grad_near, qv_sums_near = attend_back(order, 1, parts_near, out_full, grad_attn)
    qkv_met = to_core(weight_grad(order, shards, attn_turned, qkv_grad_near, 1))
    qkv_grad_mine, qv_sums_mine = attend_back(order, 0, parts_mine, out_full, grad_attn)
    down_sum.join()
    qkv_met = wait(*qkv_met)
    qkv_sum = Scatter(
        here, order, *weight_sum(order, shards, attn_turned, qkv_grad_mine, 1, qkv_met)
    )
    up_sum.turn()
    attn_own, attn_give, attn_sums = attention_in_back(
        order, qkv_grad_mine, qkv_mine, qkv_grad_near, qkv_near, lats, means_one, inverses_one
    )
    attn_far = here.to_side(attn_give)
    down_sum.turn()
    out_met = to_core(
        weight_grad(order, shards, heads_out, grad_attn, 1, other=1, chunks=2)
    )
    feed_far = wait(feed_far)
    mixed_mine, mixed_give, mix_sums = mix(
        order, feed_own, feed_far, down_bias, lats, branch, cots, mod
    )
    mixed_near = here.to_core(mixed_give)
    down_sum.turn()
    up_sum.join()
    out_met = wait(*out_met)
    out_sum = Scatter(
        here, order, *weight_sum(order, shards, heads_out, grad_attn, 1, out_met, other=0)
    )
    qkv_sum.join()

    grad_mod = jnp.concatenate(
        [wait(attn_sums), middle_sums[2:3], middle_sums[:2], mix_sums], axis=0
    ).reshape(-1)
    qv_sums = jnp.zeros((2, 4, part), jnp.float32)
    up_sums = jnp.zeros((shards, 4, block), jnp.float32)
    for qv, up, which in (
        (qv_sums_mine, up_sums_mine, seat),
        (qv_sums_near, up_sums_near, near_seat),
    ):
        qv_sums = lax.dynamic_update_index_in_dim(qv_sums, qv.reshape(3, part)[::2], which, 1)
        up_sums = lax.dynamic_update_index_in_dim(up_sums, up.reshape(shards, block), which, 1)
    bias_sums = jnp.concatenate(
        [
            vector.reshape(shards, -1)
            for vector in (qv_sums, middle_sums[3], up_sums, down_sums)
        ],
        axis=1,
    )
    count = grad_mod.shape[0]
    vector = wait(jnp.concatenate([grad_mod, bias_sums.reshape(-1)]))
    vector_far = here.to_side(vector)
    grad_down = down_sum.finish()
    down_far, down_near = here.to_side(grad_down), here.to_core(grad_down)
    qkv_sum.turn()
    out_sum.join()
    vector_far = wait(vector_far)
    vector = wait(vector + vector_far)
    near = here.to_core(vector)
    grad_up = up_sum.finish()
    up_far, up_near = here.to_side(grad_up), here.to_core(grad_up)
    near = wait(near)
    bias_sums = (vector[count:] + near[count:]).reshape(shards, -1)
    pair_mod = jnp.where(
        core == 0,
        jnp.concatenate([vector[:count], near[:count]]),
        jnp.concatenate([near[:count], vector[:count]]),
    )
    pair_mod = wide(low(pair_mod)).reshape(1, -1)
    sent = jnp.concatenate(
        [jnp.broadcast_to(pair_mod, (shards, 2 * count)), bias_sums], axis=1
    )
    qkv_sum.turn()
    out_sum.turn()
    got = here.exchange(wait(sent))
    qkv_sum.turn()
    grad_qkv = qkv_sum.finish()
    qkv_far, qkv_near = here.to_side(grad_qkv), here.to_core(grad_qkv)
    out_sum.turn()
    got = wait(got)
    mod_all = low(got[:, : 2 * count]).reshape(shards * micros, 6 * width)
    bias_sums = jnp.sum(got[:, 2 * count :], axis=0)
    cuts = [2 * width // shards, 3 * width // shards, (3 * width + hidden) // shards]
    grad_qv_bias, grad_out_bias, grad_up_bias, grad_down_bias = jnp.split(bias_sums, cuts)
    grad_low = wait(dot(mod_all, mod_weight, 1, 1).reshape(shards, micros, rows))
    grad_low = here.exchange(grad_low)
    down_far, down_near = wait(down_far, down_near)
    down_far_near = here.to_core(down_far)
    up_far, up_near = wait(up_far, up_near)
    up_far_near = here.to_core(up_far)
    out_sum.turn()
    grad_out = out_sum.finish()
    out_far, out_near = here.to_side(grad_out), here.to_core(grad_out)
    attn_far = wait(attn_far)
    tokens_mine, tokens_give = tokens_back(
        order, attn_own, attn_far, lats, means_one, inverses_one, mod, grad_middle
    )
    tokens_near = here.to_core(tokens_give)
    qkv_far, qkv_near = wait(qkv_far, qkv_near)
    qkv_far_near = here.to_core(qkv_far)
    mod_all = wait(mod_all)
    grad_mod_weight = wait(dot(cond_rows, mod_all, 0, 0))
    down_far_near = wait(down_far_near)
    grad_down = lay_rows(order, (grad_down, down_near, down_far, down_far_near))
    up_far_near = wait(up_far_near)
    grad_up = lay_columns(order, (grad_up, up_near, up_far, up_far_near), shards)
    out_far, out_near = wait(out_far, out_near)
    out_far_near = here.to_core(out_far)
    mixed_near, tokens_near = wait(mixed_near, tokens_near)
    mixed, grad_latents = lay_tokens(
        order, (mixed_mine, mixed_near), (tokens_mine, tokens_near)
    )
    qkv_far_near = wait(qkv_far_near)
    grad_qkv = lay_columns(order, (grad_qkv, qkv_near, qkv_far, qkv_far_near), 3)
    span = 6 * width // shards
    mod_span = lax.dynamic_slice_in_dim(wait(mod_all), here.shard * span, span, 1)
    grad_mod_bias = wait(jnp.sum(wide(mod_span), axis=0))
    out_far_near = wait(out_far_near)
    grad_out = lay_columns(order, (grad_out, out_near, out_far, out_far_near), 1)
    grad_low = wait(grad_low).transpose(1, 0, 2).reshape(micros, width)
    _, silu_pull = jax.vjp(jax.nn.silu, wide(condition))
    grad_condition = silu_pull(grad_low)[0]

    return (
        mixed,
        grad_latents,
        grad_condition,
        grad_mod_weight,
        grad_mod_bias,
        grad_qkv,
        grad_qv_bias,
        grad_out,
        grad_out_bias,
        grad_up,
        grad_up_bias,
        grad_down,
        grad_down_bias,
    )


def solution(mesh):
    tokens = P("fsdp", "seq", None)
    matrix = P("fsdp", None)
    vector = P("fsdp")
    parameters = (matrix, vector) * 5
    in_specs = (tokens, matrix) + parameters + (tokens,)
    out_specs = (tokens, tokens, matrix) + parameters
    return jax.shard_map(
        per_device, mesh=mesh, in_specs=in_specs, out_specs=out_specs, check_vma=False
    )
```

```python
import jax
import jax.numpy as jnp
from jax import lax
from jax.experimental import pallas as pl
from jax.experimental.pallas import tpu as pltpu
from jax.sharding import PartitionSpec as P

H = 16
HD = 72
GELU_ROOT = (2.0 / 3.141592653589793) ** 0.5
GELU_CUBE = 0.044715
SEAT, CORE, PAIR, LINE = range(4)
HEAD = 16

SCALARS = pl.BlockSpec(memory_space=pltpu.SMEM)
WHOLE = pl.BlockSpec(memory_space=pltpu.VMEM)
ANY = pl.BlockSpec(memory_space=pl.ANY)
ROOM = pltpu.CompilerParams(vmem_limit_bytes=20 << 20)
SHORT = pl.CostEstimate(flops=1, transcendentals=0, bytes_accessed=1)


def low(values):
    return values.astype(jnp.bfloat16)


def wide(values):
    return values.astype(jnp.float32)


def struct(shape, dtype):
    return jax.ShapeDtypeStruct(shape, dtype)


def whole(shape):
    return pl.BlockSpec(shape, lambda step: (0,) * len(shape))


def column_block(shape, columns):
    return pl.BlockSpec(shape[:-1] + (columns,), lambda step: (0,) * (len(shape) - 1) + (step,))


def row_block(shape, rows):
    return pl.BlockSpec((rows,) + shape[1:], lambda step: (step,) + (0,) * (len(shape) - 1))


def dot(left_side, right_side, left_dim, right_dim):
    return lax.dot_general(
        left_side,
        right_side,
        (((left_dim,), (right_dim,)), ((), ())),
        preferred_element_type=jnp.float32,
    )


def normalize_back(normed, inverse, grad):
    inner = jnp.mean(grad * normed, axis=-1, keepdims=True)
    return (grad - jnp.mean(grad, axis=-1, keepdims=True) - normed * inner) * inverse


def soft_columns(queries, keys):
    scores = dot(keys, queries, 0, 0) * HD ** (-0.5)
    raised = jnp.exp(scores - jnp.max(scores, axis=0, keepdims=True))
    return raised * (1.0 / jnp.sum(raised, axis=0, keepdims=True))


def pick(values, index, axis):
    return lax.dynamic_index_in_dim(values, index, axis, keepdims=False)


class Order:
    def __init__(self, place):
        self.place = place
        self.token = jnp.zeros((8, 128), jnp.float32)

    def wait(self, *values):
        self.token, values = lax.optimization_barrier((self.token, values))
        return values if len(values) > 1 else values[0]

    def run(self, kernel, outs, *args, grid=(), in_specs=None, out_specs=None, scratch=()):
        count, given = len(outs), len(args)

        def body(place, *refs):
            kernel(place, *refs[:given], *refs[given + 1 : given + 1 + count], *refs[given + 2 + count :])

        results = pl.pallas_call(
            body,
            out_shape=tuple(outs) + (struct(self.token.shape, self.token.dtype),),
            grid=grid,
            in_specs=[SCALARS] + list(in_specs or [WHOLE] * given) + [ANY],
            out_specs=tuple(out_specs or [WHOLE] * count) + (ANY,),
            scratch_shapes=scratch,
            input_output_aliases={given + 1: count},
            compiler_params=ROOM,
            cost_estimate=SHORT,
        )(self.place, *args, self.token)
        self.token = results[-1]
        return results[:-1] if count > 1 else results[0]

    def pass_on(self, blocks, step, sums):
        lines, rows, columns = blocks[0].shape
        count = len(blocks)

        def kernel(place, *refs):
            outs = refs[-1 - count : -1]
            for index in range(count):
                result = refs[index][0]
                if sums:
                    result = low(wide(result) + wide(refs[count + index][...]))
                outs[index][...] = result

        def block_at(unused, place):
            return (lax.rem(place[LINE] + (lines - step), lines), 0, 0)

        piece = pl.BlockSpec((rows, columns), lambda unused, place: (0, 0))
        spec = pltpu.PrefetchScalarGridSpec(
            num_scalar_prefetch=1,
            grid=(1,),
            in_specs=[pl.BlockSpec((1, rows, columns), block_at)] * count
            + [piece] * len(sums)
            + [ANY],
            out_specs=(piece,) * count + (ANY,),
        )
        results = pl.pallas_call(
            kernel,
            grid_spec=spec,
            out_shape=(struct((rows, columns), jnp.bfloat16),) * count
            + (struct(self.token.shape, self.token.dtype),),
            input_output_aliases={1 + count + len(sums): count},
            compiler_params=ROOM,
            cost_estimate=SHORT,
        )(self.place, *blocks, *sums, self.token)
        self.token = results[-1]
        return results[:-1]


class Place:
    def __init__(self):
        self.shards = lax.axis_size("fsdp")
        self.seats = lax.axis_size("seq")
        self.line_size = self.shards // 2
        self.shard = lax.axis_index("fsdp")
        self.seat = lax.axis_index("seq")
        self.core = self.seat % 2
        places = [self.seat, self.core, self.shard % 2, self.shard // 2]
        self.place = jnp.stack(places).astype(jnp.int32)

    def to_core(self, values):
        return lax.ppermute(values, "seq", [(i, i ^ 1) for i in range(self.seats)])

    def to_side(self, values):
        return lax.ppermute(values, "seq", [(i, i ^ 2) for i in range(self.seats)])

    def to_pair(self, values):
        return lax.ppermute(values, "fsdp", [(i, i ^ 1) for i in range(self.shards)])

    def to_line(self, values):
        return lax.ppermute(
            values, "fsdp", [(i, (i + 2) % self.shards) for i in range(self.shards)]
        )

    def exchange(self, values):
        results = [values[0]]
        for step in range(1, self.shards):
            shift = [(i, (i + step) % self.shards) for i in range(self.shards)]
            results.append(lax.ppermute(values[step], "fsdp", shift))
        return results


class Gather:
    def __init__(self, here, order, piece, near=False, hold=False):
        self.here, self.order, self.near = here, order, near
        self.pieces, self.copies = [], []
        self.steps, self.pending = 0, []
        self.send([piece], hold)

    def send(self, pieces, hold=False):
        here = self.here
        self.pieces += pieces
        sent = []
        if self.steps < here.line_size:
            if self.steps + 1 < here.line_size:
                sent.append(here.to_line(pieces[0]))
            if not hold:
                sent.append(here.to_pair(pieces[0]))
        self.steps += 1
        self.copied = [here.to_core(piece) for piece in pieces] if self.near else []
        self.pending = sent

    def release(self):
        self.pending.append(self.here.to_pair(self.order.wait(self.pieces[0])))

    def turn(self):
        if self.pending:
            arrived = self.order.wait(*self.pending, *self.copied)
            arrived = list(arrived) if len(self.pending) + len(self.copied) > 1 else [arrived]
            count = len(self.pending)
            self.copies += arrived[count:]
            self.send(arrived[:count])

    def finish(self, widths, head=0, keep_head=False):
        while self.pending:
            self.turn()
        return self.place(self.pieces, widths, head, keep_head)

    def finish_near(self, widths, head=0):
        return self.place(self.copies + [self.order.wait(*self.copied)], widths, head, False)

    def place(self, pieces, widths, head, keep_head):
        shards, lines = self.here.shards, self.here.line_size
        rows, total = pieces[0].shape
        rows -= head

        def kernel(place, *refs):
            targets = refs[shards:]
            for index in range(shards):
                near = index > 0 and (index % 2 == 0 or index == shards - 1)
                back = (index - 1) // 2 if near else (index + 1) // 2
                line = lax.rem(place[LINE] + (lines - back), lines)
                pair = 1 - place[PAIR] if near else place[PAIR]
                shard = 2 * line + pair
                start = 0
                for target, columns in zip(targets, widths):
                    target[shard] = refs[index][head:, start : start + columns]
                    start += columns
                if keep_head:
                    targets[-1][shard] = refs[index][:head, :]

        outs = [struct((shards, rows, columns), pieces[0].dtype) for columns in widths]
        if keep_head:
            outs.append(struct((shards, head, total), pieces[0].dtype))
        return self.order.run(kernel, outs, *pieces)


class Scatter:
    def __init__(self, here, order, give, mine):
        self.here, self.order, self.mine = here, order, mine
        self.got = here.to_pair(give)
        self.step = 0

    def join(self):
        got = self.order.wait(self.got)

        def kernel(place, got_ref, mine_ref, out):
            out[...] = low(wide(mine_ref[...]) + wide(got_ref[...]))

        shape = struct(self.mine.shape, jnp.bfloat16)
        self.kept = [self.order.run(kernel, [shape], got, self.mine)]
        self.sums = []
        self.send()

    def send(self):
        self.step += 1
        sums = self.order.pass_on(self.kept, self.step, self.sums)
        if self.step < self.here.line_size:
            sums = [self.here.to_line(total) for total in sums]
        self.sums = sums

    def turn(self):
        if self.step < self.here.line_size:
            sums = self.order.wait(*self.sums)
            self.sums = list(sums) if len(self.kept) > 1 else [sums]
            self.send()

    def finish(self):
        while self.step < self.here.line_size:
            self.turn()
        return self.sums[0]


class ScatterLines(Scatter):
    def __init__(self, here, order, both):
        self.here, self.order, self.step = here, order, 0
        self.kept, self.sums = [both], []
        self.send()

    def join(self):
        while self.step < self.here.line_size:
            self.turn()
        total = self.sums[0]
        rows = total.shape[0] // 2
        self.mine = total[rows:]
        self.got = self.here.to_pair(total[:rows])

    def finish(self):
        got = self.order.wait(self.got)

        def kernel(place, got_ref, mine_ref, out):
            out[...] = low(wide(mine_ref[...]) + wide(got_ref[...]))

        shape = struct(got.shape, jnp.bfloat16)
        return self.order.run(kernel, [shape], got, self.mine)


def cut_columns(place, source, target, offset, index, parts, groups):
    part = source.shape[1] // groups // parts
    for choice in range(parts):

        @pl.when(index == choice)
        def _():
            for group in range(groups):
                start = (group * parts + choice) * part
                goal = offset + group * part
                target[:, goal : goal + part] = source[:, start : start + part]


def cut_attention(order, condition, biases, qkv_weight, out_weight):
    rows, width = out_weight.shape
    columns = qkv_weight.shape[1] // 4
    total = columns + width // 2
    micros = condition.shape[0]

    def kernel(place, condition_ref, biases_ref, qkv_ref, out_ref, target, held):
        held[...] = jnp.zeros(held.shape, jnp.float32)
        held[:micros, :width] = wide(condition_ref[...])
        for row, start in enumerate(range(0, biases.shape[1], total)):
            count = min(total, biases.shape[1] - start)
            held[micros + row : micros + row + 1, :count] = wide(
                biases_ref[:, start : start + count]
            )
        target[:HEAD, :] = low(held[...])
        rest = target.at[HEAD:, :]
        cut_columns(place, qkv_ref, rest, 0, place[SEAT], 4, 3)
        cut_columns(place, out_ref, rest, columns, place[CORE], 2, 1)

    return order.run(
        kernel,
        [struct((HEAD + rows, total), qkv_weight.dtype)],
        condition,
        biases,
        qkv_weight,
        out_weight,
        scratch=(pltpu.VMEM((HEAD, total), jnp.float32),),
    )


def modulation_parts(order, heads, mod_weight, micros, width, hidden):
    shards, head, total = heads.shape
    rows, columns = mod_weight.shape
    part = H // 4 * HD
    block = hidden // shards // 4
    sizes = {"mod": columns, "qv": 2 * width, "out": width, "up": hidden, "down": width}

    def kernel(place, heads_ref, weight_ref, *refs):
        cond_rows, mod_bias, qkv_mine, qkv_near, out_bias, up_mine, up_near, down_bias = refs[:8]
        parts, (cond, mine, products) = refs[8 : 8 + shards], refs[8 + shards :]
        shard = 2 * place[LINE] + place[PAIR]
        for index in range(shards):
            values = wide(heads_ref[index, :micros, :width])
            values = wide(low(values / (1.0 + jnp.exp(-values))))
            cond[index * micros : (index + 1) * micros, :] = values
        for index in range(shards):

            @pl.when(shard == index)
            def _():
                mine[...] = low(cond[:, index * rows : (index + 1) * rows])

        cond_rows[...] = mine[...]
        products[...] = dot(mine[...], weight_ref[...], 1, 0)
        for step in range(shards):
            row = lax.rem(shard + step, shards) * micros + place[CORE]
            parts[step][...] = products[pl.ds(row, 1), :]

        def copy(target, row, column, name, start, count):
            base = 0
            for other, size in sizes.items():
                if other == name:
                    break
                base += size // shards
            share = sizes[name] // shards
            while count > 0:
                index, offset = divmod(start, share)
                line, lane = divmod(base + offset, total)
                length = min(count, share - offset, total - lane)
                source = heads_ref[index, micros + line : micros + line + 1, lane : lane + length]
                target[row : row + 1, column : column + length] = wide(source)
                start, column, count = start + length, column + length, count - length

        for row in range(6):
            copy(mod_bias, row, 0, "mod", row * width, width)
        copy(out_bias, 0, 0, "out", 0, width)
        copy(down_bias, 0, 0, "down", 0, width)
        for own in range(4):

            @pl.when(place[SEAT] == own)
            def _():
                for seat, qkv, up in ((own, qkv_mine, up_mine), (own ^ 1, qkv_near, up_near)):
                    copy(qkv, 0, 0, "qv", seat * part, part)
                    qkv[:, part : 2 * part] = jnp.zeros((1, part), jnp.float32)
                    copy(qkv, 0, 2 * part, "qv", width + seat * part, part)
                    for index in range(shards):
                        start = (index * 4 + seat) * block
                        copy(up, 0, index * block, "up", start, block)

    row = lambda count: struct((1, count), jnp.float32)
    outs = [
        struct((shards * micros, rows), jnp.bfloat16),
        struct((6, width), jnp.float32),
        row(3 * part),
        row(3 * part),
        row(width),
        row(shards * block),
        row(shards * block),
        row(width),
    ] + [row(columns)] * shards
    scratch = (
        pltpu.VMEM((shards * micros, width), jnp.float32),
        pltpu.VMEM((shards * micros, rows), jnp.bfloat16),
        pltpu.VMEM((shards * micros, columns), jnp.float32),
    )
    return order.run(kernel, outs, heads, mod_weight, scratch=scratch)


def token_sums(order, shards, attn, middle, mixed, down, qv_mine, qv_near, up_mine, up_near):
    width = attn.shape[1]
    part = qv_mine.shape[1] // 3
    hidden = 4 * up_mine.shape[1]
    block = hidden // shards // 4
    sizes = (2 * width // shards, width // shards, hidden // shards, width // shards)
    starts = [sum(sizes[:index]) for index in range(4)]

    def kernel(
        place, attn_ref, middle_ref, mixed_ref, down_ref, qv_mine_ref, qv_near_ref, up_mine_ref,
        up_near_ref, mods, biases,
    ):
        mods[0:2, :] = attn_ref[...]
        mods[2:3, :] = middle_ref[2:3, :]
        mods[3:5, :] = middle_ref[0:2, :]
        mods[5:6, :] = mixed_ref[...]
        biases[...] = jnp.zeros(biases.shape, jnp.float32)

        def copy(source, row, column, which, start, count):
            while count > 0:
                index, offset = divmod(start, sizes[which])
                length = min(count, sizes[which] - offset)
                goal = starts[which] + offset
                biases[index : index + 1, goal : goal + length] = source[
                    row : row + 1, column : column + length
                ]
                start, column, count = start + length, column + length, count - length

        copy(middle_ref, 3, 0, 1, 0, width)
        copy(down_ref, 0, 0, 3, 0, width)
        for own in range(4):

            @pl.when(place[SEAT] == own)
            def _():
                for seat, qv, up in (
                    (own, qv_mine_ref, up_mine_ref),
                    (own ^ 1, qv_near_ref, up_near_ref),
                ):
                    copy(qv, 0, 0, 0, seat * part, part)
                    copy(qv, 0, 2 * part, 0, width + seat * part, part)
                    for index in range(shards):
                        start = (index * 4 + seat) * block
                        copy(up, 0, index * block, 2, start, block)

    outs = (struct((6, width), jnp.float32), struct((shards, sum(sizes)), jnp.float32))
    return order.run(
        kernel, outs, attn, middle, mixed, down, qv_mine, qv_near, up_mine, up_near
    )


def add_sums(order, mods, biases, mods_far, biases_far):
    def kernel(place, mods_ref, biases_ref, mods_far_ref, biases_far_ref, mods_out, biases_out):
        mods_out[...] = mods_ref[...] + mods_far_ref[...]
        biases_out[...] = biases_ref[...] + biases_far_ref[...]

    outs = (struct(mods.shape, mods.dtype), struct(biases.shape, biases.dtype))
    return order.run(kernel, outs, mods, biases, mods_far, biases_far)


def sums_to_send(order, mods, biases, mods_near, biases_near):
    rows, width = mods.shape
    shards, columns = biases.shape

    def kernel(place, mods_ref, biases_ref, mods_near_ref, biases_near_ref, *refs):
        outs, (pair, total) = refs[:shards], refs[shards:]
        pair[place[CORE]] = wide(low(mods_ref[...]))
        pair[1 - place[CORE]] = wide(low(mods_near_ref[...]))
        total[...] = biases_ref[...] + biases_near_ref[...]
        shard = 2 * place[LINE] + place[PAIR]
        for step in range(shards):
            outs[step][:rows, :] = pair[0]
            outs[step][rows : 2 * rows, :] = pair[1]
            row = lax.rem(shard + step, shards)
            outs[step][2 * rows :, :] = jnp.zeros((HEAD - 2 * rows, width), jnp.float32)
            outs[step][2 * rows : 2 * rows + 1, :columns] = total[pl.ds(row, 1), :]

    outs = [struct((HEAD, width), jnp.float32)] * shards
    scratch = (
        pltpu.VMEM((2, rows, width), jnp.float32),
        pltpu.VMEM((shards, columns), jnp.float32),
    )
    return order.run(kernel, outs, mods, biases, mods_near, biases_near, scratch=scratch)


def modulation_back(order, received, mod_weight, hidden):
    shards, width = len(received), received[0].shape[1]
    rows, columns = mod_weight.shape
    sizes = (2 * width // shards, width // shards, hidden // shards, width // shards)

    def kernel(place, weight_ref, *refs):
        sources, refs = refs[:shards], refs[shards:]
        mod_all, biases, parts, (held, products) = refs[0], refs[1:5], refs[5:-2], refs[-2:]
        shard = 2 * place[LINE] + place[PAIR]
        total = jnp.zeros((1, sum(sizes)), jnp.float32)
        for step in range(shards):
            source = sources[step]
            index = lax.rem(shard + (shards - step), shards)
            for latent in range(2):
                for row in range(6):
                    held[pl.ds(2 * index + latent, 1), row * width : (row + 1) * width] = source[
                        6 * latent + row : 6 * latent + row + 1, :
                    ]
            total = total + source[12:13, : sum(sizes)]
        start = 0
        for target, size in zip(biases, sizes):
            target[...] = total[:, start : start + size]
            start += size
        mod_all[...] = low(held[...])
        products[...] = dot(mod_all[...], weight_ref[...], 1, 1)
        for step in range(shards):
            row = 2 * lax.rem(shard + step, shards)
            parts[step][0:1, :] = products[pl.ds(row, 1), :]
            parts[step][1:2, :] = products[pl.ds(row + 1, 1), :]

    outs = [struct((2 * shards, columns), jnp.bfloat16)]
    outs += [struct((1, size), jnp.float32) for size in sizes]
    outs += [struct((2, rows), jnp.float32)] * shards
    scratch = (
        pltpu.VMEM((2 * shards, columns), jnp.float32),
        pltpu.VMEM((2 * shards, rows), jnp.float32),
    )
    return order.run(kernel, outs, mod_weight, *received, scratch=scratch)


def condition_back(order, received, condition):
    shards, (micros, rows) = len(received), received[0].shape

    def kernel(place, condition_ref, *refs):
        out, held = refs[shards:]
        shard = 2 * place[LINE] + place[PAIR]
        for step in range(shards):
            held[lax.rem(shard + (shards - step), shards)] = refs[step][...]
        values = wide(condition_ref[...])
        sigma = 1.0 / (1.0 + jnp.exp(-values))
        slope = sigma * (1.0 + values * (1.0 - sigma))
        for index in range(shards):
            span = slice(index * rows, (index + 1) * rows)
            out[:, span] = held[index] * slope[:, span]

    outs = [struct(condition.shape, jnp.float32)]
    scratch = (pltpu.VMEM((shards, micros, rows), jnp.float32),)
    return order.run(kernel, outs, condition, *received, scratch=scratch)


def cut_feed(order, up_weight, down_weight, shards):
    hidden, width = down_weight.shape
    rows, columns = up_weight.shape

    def kernel(place, up_ref, down_ref, target):
        cut_columns(place, up_ref, target, 0, place[SEAT], 4, shards)
        target[:, columns // 4 :] = down_ref[place[SEAT]]

    shape = struct((rows, columns // 4 + width), up_weight.dtype)
    return order.run(
        kernel, [shape], up_weight, down_weight.reshape(4, hidden // 4, width)
    )


def cut_tokens(order, tokens):
    shape = struct(tokens.shape[1:], tokens.dtype)

    def kernel(place, source, mine, give):
        mine[...] = source[place[CORE]]
        give[...] = source[1 - place[CORE]]

    return order.run(kernel, [shape, shape], tokens)


def lay_columns(order, quarters, *parts):
    rows = quarters[0].shape[0]

    def kernel(place, *refs):
        for own in range(4):

            @pl.when(place[SEAT] == own)
            def _():
                offset = 0
                for target, (columns, groups) in zip(refs[4:], parts):
                    part = columns // groups
                    for group in range(groups):
                        for other in range(4):
                            start = (group * 4 + (own ^ other)) * part
                            block = refs[other][:, offset : offset + part]
                            target[:, start : start + part] = wide(block)
                        offset += part

    outs = [struct((rows, 4 * columns), jnp.float32) for columns, groups in parts]
    return order.run(kernel, outs, *quarters)


def lay_rows(order, quarters):
    rows, columns = quarters[0].shape

    def kernel(place, *refs):
        for other in range(4):
            refs[4][place[SEAT] ^ other] = wide(refs[other][...])

    result = order.run(kernel, [struct((4, rows, columns), jnp.float32)], *quarters)
    return result.reshape(4 * rows, columns)


def lay_tokens(order, *pairs):
    def kernel(place, *refs):
        for index in range(len(pairs)):
            target = refs[2 * len(pairs) + index]
            target[place[CORE]] = refs[2 * index][...]
            target[1 - place[CORE]] = refs[2 * index + 1][...]

    outs = [struct((2,) + mine.shape, mine.dtype) for mine, near in pairs]
    return order.run(kernel, outs, *(value for values in pairs for value in values))


def norm_tokens(order, pieces, parts, mod_bias):
    tokens, width = pieces[0].shape
    length = 4 * tokens

    def kernel(place, *refs):
        sources, refs = refs[: len(parts)], refs[len(parts) :]
        bias_ref, (mod, out, turned, means, inverses) = refs[0], refs[5:]
        for row in range(6):
            span = slice(row * width, (row + 1) * width)
            total = bias_ref[row : row + 1, :]
            for source in sources:
                total = total + source[:, span]
            mod[row : row + 1, :] = total
        for index in range(4):
            span = slice(index * tokens, (index + 1) * tokens)
            values = wide(refs[1 + index][...])
            mean = jnp.mean(values, axis=1, keepdims=True)
            centre = values - mean
            inverse = lax.rsqrt(jnp.mean(centre * centre, axis=1, keepdims=True) + 1e-06)
            result = centre * inverse * (1.0 + mod[1:2, :]) + mod[0:1, :]
            out[span, :] = low(result)
            turned[:, span] = low(result.T)
            means[span, :] = mean
            inverses[span, :] = inverse

    outs = (
        struct((6, width), jnp.float32),
        struct((length, width), jnp.bfloat16),
        struct((width, length), jnp.bfloat16),
        struct((length, 1), jnp.float32),
        struct((length, 1), jnp.float32),
    )
    return order.run(kernel, outs, *parts, mod_bias, *pieces)


def attend(order, attn_in, weight, bias):
    length = attn_in.shape[0]
    heads = H // 4

    def kernel(place, in_ref, weight_ref, bias_ref, parts, result):
        values = (dot(in_ref[...], weight_ref[...], 1, 0) + bias_ref[...]).T
        for index in range(3 * heads):
            parts[index] = low(values[index * HD : (index + 1) * HD])
        results = []
        for head in range(heads):
            probs = soft_columns(parts[head], parts[heads + head])
            results.append(dot(parts[2 * heads + head], low(probs), 1, 0))
        result[...] = low(jnp.concatenate(results, axis=0))

    outs = (
        struct((3 * heads, HD, length), jnp.bfloat16),
        struct((heads * HD, length), jnp.bfloat16),
    )
    return order.run(kernel, outs, attn_in, weight, bias)


def attend_back(order, other, parts, out_weight, grad_attn):
    length = grad_attn.shape[0]
    heads = H // 4
    part = heads * HD
    factor = HD ** (-0.5)

    def kernel(place, parts_ref, weight_ref, grad_ref, out, sums):
        rows = pl.ds(pl.multiple_of((place[SEAT] ^ other) * part, part), part)
        grad_heads = dot(weight_ref[rows, :], grad_ref[...], 1, 1)
        grads = [None] * (3 * heads)
        for head in range(heads):
            queries, keys = parts_ref[head], parts_ref[heads + head]
            contents = parts_ref[2 * heads + head]
            grad = low(grad_heads[head * HD : (head + 1) * HD])
            probs = soft_columns(queries, keys)
            grad_probs = dot(contents, grad, 0, 0)
            inner = jnp.sum(probs * grad_probs, axis=0, keepdims=True)
            grad_scores = low(probs * (grad_probs - inner))
            grads[head] = factor * dot(keys, grad_scores, 1, 0)
            grads[heads + head] = factor * dot(queries, grad_scores, 1, 1)
            grads[2 * heads + head] = dot(grad, low(probs), 1, 1)
        result = low(jnp.concatenate(grads, axis=0).T)
        out[...] = result
        sums[...] = jnp.sum(wide(result), axis=0, keepdims=True)

    outs = (
        struct((length, 3 * part), jnp.bfloat16),
        struct((1, 3 * part), jnp.float32),
    )
    return order.run(kernel, outs, parts, out_weight, grad_attn)


def attention_out(order, quarters, out_mine, out_near, out_bias, pieces, mod):
    tokens, width = pieces[0].shape
    half, length = 2 * tokens, 4 * tokens
    part = quarters[0].shape[0]
    columns = width // 2

    def kernel(place, *refs):
        out_mine_ref, out_near_ref, bias_ref = refs[4:7]
        mod_ref, heads, weight, branch, normed, inverses, mlp_in = refs[11:]
        for other in range(4):
            rows = pl.ds(pl.multiple_of((place[SEAT] ^ other) * part, part), part)
            if other < 2:
                heads[rows, :] = refs[other][...]
            else:
                heads[rows, :half] = refs[other][:, half:]
                heads[rows, half:] = refs[other][:, :half]
        for own in range(2):

            @pl.when(place[CORE] == own)
            def _():
                weight[:, own * columns : (own + 1) * columns] = out_mine_ref[...]
                weight[:, (1 - own) * columns : (2 - own) * columns] = out_near_ref[...]

        result = dot(heads[...], weight[...], 0, 0) + bias_ref[...]
        branch[...] = result[:half]
        shift, scale = mod_ref[3:4, :], 1.0 + mod_ref[4:5, :]
        for index in range(4):
            span = slice(index * tokens, (index + 1) * tokens)
            values = wide(refs[7 + index][...]) + mod_ref[2:3, :] * result[span]
            centre = values - jnp.mean(values, axis=1, keepdims=True)
            inverse = lax.rsqrt(jnp.mean(centre * centre, axis=1, keepdims=True) + 1e-06)
            centre = centre * inverse
            normed[span, :] = centre
            inverses[span, :] = inverse
            mlp_in[span, :] = low(centre * scale + shift)

    outs = (
        struct((width, length), jnp.bfloat16),
        struct((width, width), jnp.bfloat16),
        struct((half, width), jnp.float32),
        struct((length, width), jnp.float32),
        struct((length, 1), jnp.float32),
        struct((length, width), jnp.bfloat16),
    )
    return order.run(kernel, outs, *quarters, out_mine, out_near, out_bias, *pieces, mod)


def gate_grad(order, pieces, mod):
    tokens, width = pieces[0].shape

    def kernel(place, *refs):
        mod_ref, out, sums = refs[4:]
        total = jnp.zeros(sums.shape, jnp.float32)
        for index in range(4):
            result = low(mod_ref[5:6, :] * wide(refs[index][...]))
            out[index * tokens : (index + 1) * tokens, :] = result
            if index < 2:
                total = total + jnp.sum(wide(result), axis=0, keepdims=True)
        sums[...] = total

    outs = (struct((4 * tokens, width), jnp.bfloat16), struct((1, width), jnp.float32))
    return order.run(kernel, outs, *pieces, mod)


def feed(order, mlp_in, weight, bias):
    length, width = mlp_in.shape
    hidden = weight.shape[1]
    step = hidden // 3

    def kernel(place, in_ref, weight_ref, bias_ref, act, slope):
        pre_act = dot(in_ref[...], weight_ref[...], 1, 0) + bias_ref[...]
        squared = pre_act * pre_act
        bent = jnp.tanh(GELU_ROOT * pre_act * (1.0 + GELU_CUBE * squared))
        raised = 0.5 + 0.5 * bent
        act[...] = low(pre_act * raised)
        slope[...] = raised + pre_act * (1.0 - bent * bent) * (
            0.5 * GELU_ROOT + (1.5 * GELU_ROOT * GELU_CUBE) * squared
        )

    return order.run(
        kernel,
        (
            struct((length, hidden), jnp.bfloat16),
            struct((length, hidden), jnp.float32),
        ),
        mlp_in, weight, bias,
        grid=(3,),
        in_specs=[
            whole((length, width)),
            column_block((width, hidden), step),
            column_block((1, hidden), step),
        ],
        out_specs=(
            column_block((length, hidden), step),
            column_block((length, hidden), step),
        ),
    )


def feed_back(order, grad_mlp, weight, slope):
    length, width = grad_mlp.shape
    hidden = weight.shape[0]
    step = hidden // 3

    def kernel(place, grad_ref, weight_ref, slope_ref, out, sums):
        result = low(dot(grad_ref[...], weight_ref[...], 1, 1) * slope_ref[...])
        out[...] = result
        sums[...] = jnp.sum(wide(result), axis=0, keepdims=True)

    return order.run(
        kernel,
        (struct((length, hidden), jnp.bfloat16), struct((1, hidden), jnp.float32)),
        grad_mlp, weight, slope,
        grid=(3,),
        in_specs=[
            whole((length, width)),
            row_block((hidden, width), step),
            column_block((length, hidden), step),
        ],
        out_specs=(column_block((length, hidden), step), column_block((1, hidden), step)),
    )


def feed_in_back(order, pre_mine, up_mine, pre_near, up_near):
    length, hidden = pre_mine.shape
    width = up_mine.shape[0]
    step = width // 3

    def kernel(place, pre_mine_ref, up_mine_ref, pre_near_ref, up_near_ref, out):
        out[...] = low(
            dot(pre_mine_ref[...], up_mine_ref[...], 1, 1)
            + dot(pre_near_ref[...], up_near_ref[...], 1, 1)
        )

    return order.run(
        kernel,
        [struct((length, width), jnp.bfloat16)],
        pre_mine, up_mine, pre_near, up_near,
        grid=(3,),
        in_specs=[
            whole((length, hidden)),
            row_block((width, hidden), step),
            whole((length, hidden)),
            row_block((width, hidden), step),
        ],
        out_specs=[column_block((length, width), step)],
    )


def feed_out(order, act_mine, down_mine, act_near, down_near):
    length, hidden = act_mine.shape
    width = down_mine.shape[1]
    half, step = length // 2, width // 3

    def kernel(place, act_mine_ref, down_mine_ref, act_near_ref, down_near_ref, own, give):
        result = dot(act_mine_ref[...], down_mine_ref[...], 1, 0) + dot(
            act_near_ref[...], down_near_ref[...], 1, 0
        )
        own[...] = result[:half]
        give[...] = low(result[half:])

    return order.run(
        kernel,
        (struct((half, width), jnp.float32), struct((half, width), jnp.bfloat16)),
        act_mine, down_mine, act_near, down_near,
        grid=(3,),
        in_specs=[
            whole((length, hidden)),
            column_block((hidden, width), step),
            whole((length, hidden)),
            column_block((hidden, width), step),
        ],
        out_specs=(column_block((half, width), step), column_block((half, width), step)),
    )


def weight_grad(order, shards, left_side, right_side, chunks):
    length, rows = left_side.shape
    columns = right_side.shape[1]

    def kernel(place, left_ref, right_ref, *refs):
        total = low(dot(left_ref[...], right_ref[...], 0, 0))
        give_chunks(total, shards, refs, 0)

    return order.run(kernel, chunks_of(shards, rows, columns, chunks), left_side, right_side)


def chunks_of(shards, rows, columns, chunks):
    return [struct((shards // chunks, rows // shards, columns), jnp.bfloat16)] * chunks


def give_chunks(total, shards, refs, start):
    piece = total.shape[0] // shards
    share = shards // len(refs)
    span = slice(start, start + total.shape[1])
    for shard in range(shards):
        block = total[shard * piece : (shard + 1) * piece]
        refs[shard // share][shard % share, :, span] = block


def attention_grad(order, shards, attn_turned, qkv_grad, heads_out, grad_attn, chunks):
    rows = attn_turned.shape[0]
    columns, part = qkv_grad.shape[1], grad_attn.shape[1] // 4

    def kernel(place, turned_ref, qkv_ref, heads_ref, grad_ref, *refs):
        held = refs[chunks]
        take_quarter(place, grad_ref, held, 1)
        give_chunks(low(dot(turned_ref[...], qkv_ref[...], 1, 0)), shards, refs[:chunks], 0)
        total = low(dot(heads_ref[...], held[...], 1, 0))
        give_chunks(total, shards, refs[:chunks], columns)

    return order.run(
        kernel,
        chunks_of(shards, rows, columns + part, chunks),
        attn_turned,
        qkv_grad,
        heads_out,
        grad_attn,
        scratch=(pltpu.VMEM((grad_attn.shape[0], part), grad_attn.dtype),),
    )


def take_quarter(place, source, target, other):
    columns = target.shape[1]
    for index in range(4):

        @pl.when((place[SEAT] ^ other) == index)
        def _():
            target[...] = source[:, index * columns : (index + 1) * columns]


def split_pairs(place, total, shards, met_refs, start, write):
    piece = total.shape[0] // shards
    share = shards // len(met_refs)
    span = slice(start, start + total.shape[1])
    for own in range(2):

        @pl.when(place[PAIR] == own)
        def _():
            for shard in range(shards):
                part = total[shard * piece : (shard + 1) * piece]
                met = met_refs[shard // share][shard % share, :, span]
                write(shard // 2, shard % 2 == own, low(part + wide(met)))


def weight_sum(order, shards, left_side, right_side, met, join=False):
    rows, columns = left_side.shape[1], right_side.shape[1]
    piece = rows // shards

    def kernel(place, left_ref, right_ref, *refs):
        met_refs, outs = refs[: len(met)], refs[len(met) :]

        def write(line, mine, part):
            if join:
                start = piece if mine else 0
                outs[0][line, start : start + piece] = part
            else:
                outs[1 if mine else 0][line] = part

        total = dot(left_ref[...], right_ref[...], 0, 0)
        split_pairs(place, total, shards, met_refs, 0, write)

    if join:
        outs = (struct((shards // 2, 2 * piece, columns), jnp.bfloat16),)
    else:
        outs = (struct((shards // 2, piece, columns), jnp.bfloat16),) * 2
    return order.run(kernel, outs, left_side, right_side, *met)


def attention_sum(order, shards, attn_turned, qkv_grad, heads_out, grad_attn, met):
    rows = attn_turned.shape[0]
    columns, part = qkv_grad.shape[1], grad_attn.shape[1] // 4

    def kernel(place, turned_ref, qkv_ref, heads_ref, grad_ref, *refs):
        met_refs, (give, mine, held) = refs[: len(met)], refs[len(met) :]
        take_quarter(place, grad_ref, held, 0)
        for left, right, start in ((turned_ref, qkv_ref, 0), (heads_ref, held, columns)):
            total = dot(left[...], right[...], 1, 0)
            span = slice(start, start + total.shape[1])

            def write(line, own, block, span=span):
                target = mine if own else give
                target[line, :, span] = block

            split_pairs(place, total, shards, met_refs, start, write)

    outs = (struct((shards // 2, rows // shards, columns + part), jnp.bfloat16),) * 2
    return order.run(
        kernel,
        outs,
        attn_turned,
        qkv_grad,
        heads_out,
        grad_attn,
        *met,
        scratch=(pltpu.VMEM((grad_attn.shape[0], part), grad_attn.dtype),),
    )


def middle_back(order, part, far, normed, inverses, pieces, mod, branch):
    length, width = part.shape
    tokens = length // 4

    def kernel(place, part_ref, far_ref, normed_ref, inverse_ref, *refs):
        mod_ref, branch_ref, grad_attn, grad_middle, sums = refs[4:]
        gate, scale = mod_ref[2:3, :], 1.0 + mod_ref[4:5, :]
        totals = [jnp.zeros((1, width), jnp.float32)] * 4
        for index in range(4):
            span = slice(index * tokens, (index + 1) * tokens)
            other = slice((index ^ 2) * tokens, ((index ^ 2) + 1) * tokens)
            grad_in = wide(part_ref[span, :]) + wide(far_ref[other, :])
            values = normed_ref[span, :]
            grad = wide(refs[index][...]) + normalize_back(
                values, inverse_ref[span, :], grad_in * scale
            )
            result = low(gate * grad)
            grad_attn[span, :] = result
            if index < 2:
                grad_middle[span, :] = grad
                terms = (grad_in, grad_in * values, grad * branch_ref[span, :], wide(result))
                totals = [
                    total + jnp.sum(term, axis=0, keepdims=True)
                    for total, term in zip(totals, terms)
                ]
        for row, total in enumerate(totals):
            sums[row : row + 1, :] = total

    outs = (
        struct((length, width), jnp.bfloat16),
        struct((2 * tokens, width), jnp.float32),
        struct((4, width), jnp.float32),
    )
    return order.run(kernel, outs, part, far, normed, inverses, *pieces, mod, branch)


def attention_in_back(order, grad_mine, qkv_mine, grad_near, qkv_near, pieces, means, inverses):
    length, columns = grad_mine.shape
    width = qkv_mine.shape[0]
    tokens, half, step = length // 4, length // 2, width // 3

    def kernel(place, grad_mine_ref, qkv_mine_ref, grad_near_ref, qkv_near_ref, *refs):
        mean_ref, inverse_ref, own, give, sums = refs[4:]
        result = dot(grad_mine_ref[...], qkv_mine_ref[...], 1, 1) + dot(
            grad_near_ref[...], qkv_near_ref[...], 1, 1
        )
        own[...] = result[:half]
        give[...] = low(result[half:])
        scaled = jnp.zeros((1, step), jnp.float32)
        for index in range(4):
            span = slice(index * tokens, (index + 1) * tokens)
            normed = (wide(refs[index][...]) - mean_ref[span, :]) * inverse_ref[span, :]
            scaled = scaled + jnp.sum(result[span] * normed, axis=0, keepdims=True)
        sums[0:1, :] = jnp.sum(result, axis=0, keepdims=True)
        sums[1:2, :] = scaled

    outs = (
        struct((half, width), jnp.float32),
        struct((half, width), jnp.bfloat16),
        struct((2, width), jnp.float32),
    )
    weights = row_block((width, columns), step)
    grads = whole((length, columns))
    stats = whole((length, 1))
    return order.run(
        kernel,
        outs,
        grad_mine,
        qkv_mine,
        grad_near,
        qkv_near,
        *pieces,
        means,
        inverses,
        grid=(3,),
        in_specs=[grads, weights, grads, weights]
        + [column_block((tokens, width), step)] * 4
        + [stats, stats],
        out_specs=[
            column_block((half, width), step),
            column_block((half, width), step),
            column_block((2, width), step),
        ],
    )


def tokens_back(order, own, far, pieces, means, inverses, mod, grad_middle):
    half, width = own.shape
    tokens = half // 2

    def kernel(
        place, own_ref, far_ref, mine_ref, near_ref, mean_ref, inverse_ref, mod_ref, grad_ref,
        mine, give,
    ):
        for index, (source, target) in enumerate(((mine_ref, mine), (near_ref, give))):
            span = slice(index * tokens, (index + 1) * tokens)
            inverse = inverse_ref[span, :]
            normed = (wide(source[...]) - mean_ref[span, :]) * inverse
            grad = (own_ref[span, :] + wide(far_ref[span, :])) * (1.0 + mod_ref[1:2, :])
            target[...] = grad_ref[span, :] + normalize_back(normed, inverse, grad)

    outs = (struct((tokens, width), jnp.float32),) * 2
    return order.run(
        kernel, outs, own, far, pieces[0], pieces[1], means, inverses, mod, grad_middle
    )


def mix(order, own, far, down_bias, pieces, branch, grads, mod):
    half, width = own.shape
    tokens = half // 2

    def kernel(
        place, own_ref, far_ref, bias_ref, mine_ref, near_ref, branch_ref, grad_mine, grad_near,
        mod_ref, mine, give, sums,
    ):
        total = jnp.zeros((1, width), jnp.float32)
        sources = ((mine_ref, grad_mine, mine), (near_ref, grad_near, give))
        for index, (source, grad, target) in enumerate(sources):
            span = slice(index * tokens, (index + 1) * tokens)
            mlp_branch = own_ref[span, :] + wide(far_ref[span, :]) + bias_ref[...]
            middle = wide(source[...]) + mod_ref[2:3, :] * branch_ref[span, :]
            target[...] = low(middle + mod_ref[5:6, :] * mlp_branch)
            total = total + jnp.sum(wide(grad[...]) * mlp_branch, axis=0, keepdims=True)
        sums[...] = total

    outs = (struct((tokens, width), jnp.bfloat16),) * 2 + (struct((1, width), jnp.float32),)
    return order.run(
        kernel, outs, own, far, down_bias, pieces[0], pieces[1], branch, grads[0], grads[1], mod
    )


def per_device(
    latents,
    condition,
    mod_weight,
    mod_bias,
    qkv_weight,
    qv_bias,
    out_weight,
    out_bias,
    up_weight,
    up_bias,
    down_weight,
    down_bias,
    cotangent,
):
    here = Place()
    order = Order(here.place)
    shards, seat, core = here.shards, here.seat, here.core
    near_seat = seat ^ 1
    micros, tokens, width = latents.shape
    rows = width // shards
    hidden = up_weight.shape[1]
    heads = H // 4
    part = heads * HD
    block = hidden // shards // 4
    wait = order.wait

    hidden_part = shards * block
    attention_widths = (3 * part, width // 2)

    biases = jnp.concatenate([mod_bias, qv_bias, out_bias, up_bias, down_bias]).reshape(1, -1)
    ring = Gather(
        here, order, cut_attention(order, condition, biases, qkv_weight, out_weight), near=True
    )
    lat_mine, lat_give = cut_tokens(order, latents)
    lat_near, lat_far = here.to_core(lat_give), here.to_side(lat_mine)
    cot_mine, cot_give = cut_tokens(order, cotangent)
    cot_near, cot_far = here.to_core(cot_give), here.to_side(cot_mine)
    feed_piece = cut_feed(order, up_weight, down_weight, shards)
    ring.turn()
    lat_near, cot_near = wait(lat_near, cot_near)
    lat_far_near, cot_far_near = here.to_side(lat_near), here.to_side(cot_near)
    lat_far = wait(lat_far)
    ring.turn()
    cot_far, lat_far_near = wait(cot_far, lat_far_near)
    lats = (lat_mine, lat_near, lat_far, lat_far_near)
    ring.turn()
    feed_ring = Gather(here, order, wait(feed_piece), hold=True)
    qkv_mine, out_mine, heads_all = ring.finish(attention_widths, HEAD, True)
    feed_ring.release()
    (
        cond_rows,
        mod_bias,
        qkv_bias_mine,
        qkv_bias_near,
        out_bias,
        up_bias_mine,
        up_bias_near,
        down_bias,
        *mod_parts,
    ) = modulation_parts(order, heads_all, mod_weight, micros, width, hidden)
    mod_parts = here.exchange(mod_parts)
    qkv_near, out_near = ring.finish_near(attention_widths, HEAD)
    cots = (cot_mine, cot_near, cot_far, wait(cot_far_near))
    mod_parts = [mod_parts[0]] + list(wait(*mod_parts[1:]))
    feed_ring.turn()
    mod, attn_in, attn_turned, means_one, inverses_one = norm_tokens(
        order, lats, mod_parts, mod_bias
    )
    qkv_mine = qkv_mine.reshape(width, 3 * part)
    parts_mine, heads_mine = attend(order, attn_in, qkv_mine, qkv_bias_mine)
    heads_far = here.to_side(heads_mine)
    qkv_near = qkv_near.reshape(width, 3 * part)
    parts_near, heads_near = attend(order, attn_in, qkv_near, qkv_bias_near)
    heads_far_near = here.to_side(heads_near)
    heads_far = wait(heads_far)
    feed_ring.turn()
    quarters = (heads_mine, heads_near, heads_far, wait(heads_far_near))
    heads_out, out_full, branch, normed_two, inverses_two, mlp_in = attention_out(
        order,
        quarters,
        out_mine.reshape(width, width // 2),
        out_near.reshape(width, width // 2),
        out_bias,
        lats,
        mod,
    )
    grad_mlp, down_sums = gate_grad(order, cots, mod)
    feed_ring.turn()
    up_mine, down_mine = feed_ring.finish((hidden_part, width))
    up_near, down_near = here.to_core(up_mine), here.to_core(down_mine)
    up_mine = up_mine.reshape(width, hidden_part)
    down_mine = down_mine.reshape(hidden_part, width)
    act_mine, slope_mine = feed(order, mlp_in, up_mine, up_bias_mine)
    pre_mine, up_sums_mine = feed_back(order, grad_mlp, down_mine, slope_mine)
    up_near = wait(up_near).reshape(width, hidden_part)
    act_near, slope_near = feed(order, mlp_in, up_near, up_bias_near)
    down_near = wait(down_near).reshape(hidden_part, width)
    pre_near, up_sums_near = feed_back(order, grad_mlp, down_near, slope_near)

    mlp_part = feed_in_back(order, pre_mine, up_mine, pre_near, up_near)
    mlp_far = here.to_side(mlp_part)

    def to_core(chunks):
        return [here.to_core(chunk) for chunk in chunks]

    up_met = to_core(weight_grad(order, shards, mlp_in, pre_near, 8))
    down_met = to_core(weight_grad(order, shards, act_near, grad_mlp, 8))
    up_met = wait(*up_met)
    up_sum = ScatterLines(
        here, order, weight_sum(order, shards, mlp_in, pre_mine, up_met, join=True)
    )
    down_met = wait(*down_met)
    down_sum = Scatter(here, order, *weight_sum(order, shards, act_mine, grad_mlp, down_met))
    feed_own, feed_give = feed_out(order, act_mine, down_mine, act_near, down_near)
    feed_far = here.to_side(feed_give)

    mlp_far = wait(mlp_far)
    grad_attn, grad_middle, middle_sums = middle_back(
        order, mlp_part, mlp_far, normed_two, inverses_two, cots, mod, branch
    )
    qkv_grad_near, qv_sums_near = attend_back(order, 1, parts_near, out_full, grad_attn)
    met = to_core(
        attention_grad(order, shards, attn_turned, qkv_grad_near, heads_out, grad_attn, 4)
    )
    up_sum.turn()
    qkv_grad_mine, qv_sums_mine = attend_back(order, 0, parts_mine, out_full, grad_attn)
    down_sum.join()
    met = wait(*met)
    attention_total = Scatter(
        here,
        order,
        *attention_sum(order, shards, attn_turned, qkv_grad_mine, heads_out, grad_attn, met),
    )
    up_sum.turn()
    attn_own, attn_give, attn_sums = attention_in_back(
        order, qkv_grad_mine, qkv_mine, qkv_grad_near, qkv_near, lats, means_one, inverses_one
    )
    attn_far = here.to_side(attn_give)
    down_sum.turn()
    feed_far = wait(feed_far)
    mixed_mine, mixed_give, mix_sums = mix(
        order, feed_own, feed_far, down_bias, lats, branch, cots, mod
    )
    mixed_near = here.to_core(mixed_give)

    mods, biases = token_sums(
        order, shards, attn_sums, middle_sums, mix_sums, down_sums, qv_sums_mine, qv_sums_near,
        up_sums_mine, up_sums_near,
    )
    mods_far, biases_far = here.to_side(mods), here.to_side(biases)
    up_sum.join()
    mods_far, biases_far = wait(mods_far, biases_far)
    mods, biases = add_sums(order, mods, biases, mods_far, biases_far)
    mods_near, biases_near = here.to_core(mods), here.to_core(biases)
    down_sum.turn()
    attention_total.join()
    mods_near, biases_near = wait(mods_near, biases_near)
    received = here.exchange(sums_to_send(order, mods, biases, mods_near, biases_near))
    attention_total.turn()
    grad_down = down_sum.finish()
    down_far, down_near = here.to_side(grad_down), here.to_core(grad_down)
    received = [received[0]] + list(wait(*received[1:]))
    mod_all, grad_qv_bias, grad_out_bias, grad_up_bias, grad_down_bias, *grad_low = (
        modulation_back(order, received, mod_weight, hidden)
    )
    grad_low = here.exchange(grad_low)
    attention_total.turn()
    grad_up = up_sum.finish()
    up_far, up_near = here.to_side(grad_up), here.to_core(grad_up)
    grad_attention = attention_total.finish()
    attention_far = here.to_side(grad_attention)
    attention_near = here.to_core(grad_attention)
    down_far, down_near = wait(down_far, down_near)
    down_far_near = here.to_core(down_far)
    attn_far = wait(attn_far)
    tokens_mine, tokens_give = tokens_back(
        order, attn_own, attn_far, lats, means_one, inverses_one, mod, grad_middle
    )
    tokens_near = here.to_core(tokens_give)
    up_far, up_near = wait(up_far, up_near)
    up_far_near = here.to_core(up_far)
    down_far_near = wait(down_far_near)
    grad_down = lay_rows(order, (grad_down, down_near, down_far, down_far_near))
    attention_far, attention_near = wait(attention_far, attention_near)
    attention_far_near = here.to_core(attention_far)
    up_far_near = wait(up_far_near)
    grad_up = lay_columns(
        order, (grad_up, up_near, up_far, up_far_near), (hidden_part, shards)
    )
    attention_far_near = wait(attention_far_near)
    grad_qkv, grad_out = lay_columns(
        order,
        (grad_attention, attention_near, attention_far, attention_far_near),
        (3 * part, 3),
        (width // 4, 1),
    )
    grad_low = [grad_low[0]] + list(wait(*grad_low[1:]))
    grad_condition = condition_back(order, grad_low, condition)
    mixed_near, tokens_near = wait(mixed_near, tokens_near)
    mixed, grad_latents = lay_tokens(
        order, (mixed_mine, mixed_near), (tokens_mine, tokens_near)
    )
    mod_all = wait(mod_all)
    grad_mod_weight = wait(dot(cond_rows, mod_all, 0, 0))
    span = 6 * width // shards
    mod_span = lax.dynamic_slice_in_dim(mod_all, here.shard * span, span, 1)
    grad_mod_bias = jnp.sum(wide(mod_span), axis=0)
    grad_qv_bias, grad_out_bias, grad_up_bias, grad_down_bias = (
        vector.reshape(-1)
        for vector in (grad_qv_bias, grad_out_bias, grad_up_bias, grad_down_bias)
    )

    return (
        mixed,
        grad_latents,
        grad_condition,
        grad_mod_weight,
        grad_mod_bias,
        grad_qkv,
        grad_qv_bias,
        grad_out,
        grad_out_bias,
        grad_up,
        grad_up_bias,
        grad_down,
        grad_down_bias,
    )


def solution(mesh):
    tokens = P("fsdp", "seq", None)
    matrix = P("fsdp", None)
    vector = P("fsdp")
    parameters = (matrix, vector) * 5
    in_specs = (tokens, matrix) + parameters + (tokens,)
    out_specs = (tokens, tokens, matrix) + parameters
    return jax.shard_map(
        per_device, mesh=mesh, in_specs=in_specs, out_specs=out_specs, check_vma=False
    )
```

```python
import jax
import jax.numpy as jnp
from jax import lax
from jax.experimental import pallas as pl
from jax.experimental.pallas import tpu as pltpu
from jax.sharding import PartitionSpec as P

H = 16
HD = 72
GELU_ROOT = (2.0 / 3.141592653589793) ** 0.5
GELU_CUBE = 0.044715
SEAT, CORE, PAIR, LINE = range(4)
HEAD = 16

SCALARS = pl.BlockSpec(memory_space=pltpu.SMEM)
WHOLE = pl.BlockSpec(memory_space=pltpu.VMEM)
ANY = pl.BlockSpec(memory_space=pl.ANY)
ROOM = pltpu.CompilerParams(vmem_limit_bytes=20 << 20)
SHORT = pl.CostEstimate(flops=1, transcendentals=0, bytes_accessed=1)


def low(values):
    return values.astype(jnp.bfloat16)


def wide(values):
    return values.astype(jnp.float32)


def struct(shape, dtype):
    return jax.ShapeDtypeStruct(shape, dtype)


def whole(shape):
    return pl.BlockSpec(shape, lambda step: (0,) * len(shape))


def column_block(shape, columns):
    return pl.BlockSpec(shape[:-1] + (columns,), lambda step: (0,) * (len(shape) - 1) + (step,))


def row_block(shape, rows):
    return pl.BlockSpec((rows,) + shape[1:], lambda step: (step,) + (0,) * (len(shape) - 1))


def dot(left_side, right_side, left_dim, right_dim):
    return lax.dot_general(
        left_side,
        right_side,
        (((left_dim,), (right_dim,)), ((), ())),
        preferred_element_type=jnp.float32,
    )


def normalize_back(normed, inverse, grad):
    inner = jnp.mean(grad * normed, axis=-1, keepdims=True)
    return (grad - jnp.mean(grad, axis=-1, keepdims=True) - normed * inner) * inverse


def soft_columns(queries, keys):
    scores = dot(keys, queries, 0, 0) * HD ** (-0.5)
    raised = jnp.exp(scores - jnp.max(scores, axis=0, keepdims=True))
    return raised * (1.0 / jnp.sum(raised, axis=0, keepdims=True))


def pick(values, index, axis):
    return lax.dynamic_index_in_dim(values, index, axis, keepdims=False)


class Order:
    def __init__(self, place):
        self.place = place
        self.token = jnp.zeros((8, 128), jnp.float32)

    def wait(self, *values):
        self.token, values = lax.optimization_barrier((self.token, values))
        return values if len(values) > 1 else values[0]

    def run(self, kernel, outs, *args, grid=(), in_specs=None, out_specs=None, scratch=()):
        count, given = len(outs), len(args)

        def body(place, *refs):
            kernel(place, *refs[:given], *refs[given + 1 : given + 1 + count], *refs[given + 2 + count :])

        results = pl.pallas_call(
            body,
            out_shape=tuple(outs) + (struct(self.token.shape, self.token.dtype),),
            grid=grid,
            in_specs=[SCALARS] + list(in_specs or [WHOLE] * given) + [ANY],
            out_specs=tuple(out_specs or [WHOLE] * count) + (ANY,),
            scratch_shapes=scratch,
            input_output_aliases={given + 1: count},
            compiler_params=ROOM,
            cost_estimate=SHORT,
        )(self.place, *args, self.token)
        self.token = results[-1]
        return results[:-1] if count > 1 else results[0]

    def pass_on(self, blocks, step, sums):
        lines, rows, columns = blocks[0].shape
        count = len(blocks)

        def kernel(place, *refs):
            outs = refs[-1 - count : -1]
            for index in range(count):
                result = refs[index][0]
                if sums:
                    result = wide(result) + wide(refs[count + index][...])
                outs[index][...] = result.astype(outs[index].dtype)

        def block_at(unused, place):
            return (lax.rem(place[LINE] + (lines - step), lines), 0, 0)

        piece = pl.BlockSpec((rows, columns), lambda unused, place: (0, 0))
        spec = pltpu.PrefetchScalarGridSpec(
            num_scalar_prefetch=1,
            grid=(1,),
            in_specs=[pl.BlockSpec((1, rows, columns), block_at)] * count
            + [piece] * len(sums)
            + [ANY],
            out_specs=(piece,) * count + (ANY,),
        )
        results = pl.pallas_call(
            kernel,
            grid_spec=spec,
            out_shape=tuple(struct((rows, columns), block.dtype) for block in blocks)
            + (struct(self.token.shape, self.token.dtype),),
            input_output_aliases={1 + count + len(sums): count},
            compiler_params=ROOM,
            cost_estimate=SHORT,
        )(self.place, *blocks, *sums, self.token)
        self.token = results[-1]
        return results[:-1]


class Place:
    def __init__(self):
        self.shards = lax.axis_size("fsdp")
        self.seats = lax.axis_size("seq")
        self.line_size = self.shards // 2
        self.shard = lax.axis_index("fsdp")
        self.seat = lax.axis_index("seq")
        self.core = self.seat % 2
        places = [self.seat, self.core, self.shard % 2, self.shard // 2]
        self.place = jnp.stack(places).astype(jnp.int32)

    def to_core(self, values):
        return lax.ppermute(values, "seq", [(i, i ^ 1) for i in range(self.seats)])

    def to_side(self, values):
        return lax.ppermute(values, "seq", [(i, i ^ 2) for i in range(self.seats)])

    def to_pair(self, values):
        return lax.ppermute(values, "fsdp", [(i, i ^ 1) for i in range(self.shards)])

    def to_line(self, values, step=1):
        return lax.ppermute(
            values, "fsdp", [(i, (i + 2 * step) % self.shards) for i in range(self.shards)]
        )


def piece_shard(place, index, shards):
    lines = shards // 2
    near = index > 0 and (index % 2 == 0 or index == shards - 1)
    back = (index - 1) // 2 if near else (index + 1) // 2
    line = lax.rem(place[LINE] + (lines - back), lines)
    return 2 * line + (1 - place[PAIR] if near else place[PAIR])


class Gather:
    def __init__(self, here, order, piece, near=False, hold=False):
        self.here, self.order, self.near = here, order, near
        self.pieces, self.copies = [], []
        self.steps, self.pending = 0, []
        self.send([piece], hold)

    def send(self, pieces, hold=False):
        here = self.here
        self.pieces += pieces
        sent = []
        if self.steps < here.line_size:
            if self.steps + 1 < here.line_size:
                sent.append(here.to_line(pieces[0]))
            if not hold:
                sent.append(here.to_pair(pieces[0]))
        self.steps += 1
        self.copied = [here.to_core(piece) for piece in pieces] if self.near else []
        self.pending = sent

    def release(self):
        self.pending.append(self.here.to_pair(self.order.wait(self.pieces[0])))

    def turn(self):
        if self.pending:
            arrived = self.order.wait(*self.pending, *self.copied)
            arrived = list(arrived) if len(self.pending) + len(self.copied) > 1 else [arrived]
            count = len(self.pending)
            self.copies += arrived[count:]
            self.send(arrived[:count])

    def finish(self, widths, head=0, keep_head=False):
        while self.pending:
            self.turn()
        return self.place(self.pieces, widths, head, keep_head)

    def finish_near(self, widths, head=0):
        return self.place(self.copies + [self.order.wait(*self.copied)], widths, head, False)

    def place(self, pieces, widths, head, keep_head):
        shards = self.here.shards
        rows, total = pieces[0].shape
        rows -= head

        def kernel(place, *refs):
            targets = refs[shards:]
            for index in range(shards):
                shard = piece_shard(place, index, shards)
                start = 0
                for target, columns in zip(targets, widths):
                    target[shard] = refs[index][head:, start : start + columns]
                    start += columns
                if keep_head:
                    targets[-1][shard] = refs[index][:head, :]

        outs = [struct((shards, rows, columns), pieces[0].dtype) for columns in widths]
        if keep_head:
            outs.append(struct((shards, head, total), pieces[0].dtype))
        return self.order.run(kernel, outs, *pieces)


class Lines:
    def __init__(self, here, order, piece):
        self.here, self.order = here, order
        self.pieces = [piece] + [here.to_line(piece, step) for step in range(1, here.line_size)]

    def join(self):
        count = len(self.pieces)
        self.pieces[1:] = self.order.wait(*self.pieces[1:])

        def kernel(place, *refs):
            for index in range(count):
                refs[-1][index] = refs[index][...]

        shape = struct((count,) + self.pieces[0].shape, self.pieces[0].dtype)
        self.mine = self.order.run(kernel, [shape], *self.pieces)
        self.got = self.here.to_pair(self.mine)

    def finish(self):
        return self.mine, self.order.wait(self.got)


class LineSum:
    def __init__(self, here, order, parts):
        self.here, self.order = here, order
        self.parts = [parts[0]]
        self.parts += [here.to_line(parts[step], step) for step in range(1, here.line_size)]

    def join(self):
        count = len(self.parts)
        self.parts[1:] = self.order.wait(*self.parts[1:])

        def kernel(place, *refs):
            give, mine = refs[count:]
            total = refs[0][...]
            for index in range(1, count):
                total = total + refs[index][...]
            give[...] = total[0:1]
            mine[...] = total[1:2]

        row = struct((1, self.parts[0].shape[1]), self.parts[0].dtype)
        give, self.mine = self.order.run(kernel, [row, row], *self.parts)
        self.got = self.here.to_pair(give)

    def finish(self):
        return self.order.wait(self.got), self.mine


class Scatter:
    def __init__(self, here, order, *blocks):
        self.here, self.order, self.mine = here, order, blocks[-1]
        self.got = [here.to_pair(give) for give in blocks[:-1]]
        self.step = 0

    def join(self):
        got = [self.order.wait(part) for part in self.got]
        share = self.mine.shape[0] // len(got)

        def kernel(place, mine_ref, *refs):
            for index in range(len(got)):
                span = slice(index * share, (index + 1) * share)
                refs[-1][span] = low(wide(mine_ref[span]) + wide(refs[index][...]))

        shape = struct(self.mine.shape, jnp.bfloat16)
        self.kept = [self.order.run(kernel, [shape], self.mine, *got)]
        self.sums = []
        self.send()

    def send(self):
        self.step += 1
        sums = self.order.pass_on(self.kept, self.step, self.sums)
        if self.step < self.here.line_size:
            sums = [self.here.to_line(total) for total in sums]
        self.sums = sums

    def turn(self):
        if self.step < self.here.line_size:
            sums = self.order.wait(*self.sums)
            self.sums = list(sums) if len(self.kept) > 1 else [sums]
            self.send()

    def finish(self):
        while self.step < self.here.line_size:
            self.turn()
        return self.sums[0]


def cut_columns(place, source, target, offset, index, parts, groups):
    part = source.shape[1] // groups // parts
    for choice in range(parts):

        @pl.when(index == choice)
        def _():
            for group in range(groups):
                start = (group * parts + choice) * part
                goal = offset + group * part
                target[:, goal : goal + part] = source[:, start : start + part]


def cut_attention(order, condition, biases, qkv_weight, out_weight):
    rows, width = out_weight.shape
    columns = qkv_weight.shape[1] // 4
    total = columns + width // 2
    micros = condition.shape[0]

    def kernel(place, condition_ref, biases_ref, qkv_ref, out_ref, target, held):
        held[...] = jnp.zeros(held.shape, jnp.float32)
        held[:micros, :width] = wide(condition_ref[...])
        for row, start in enumerate(range(0, biases.shape[1], total)):
            count = min(total, biases.shape[1] - start)
            held[micros + row : micros + row + 1, :count] = wide(
                biases_ref[:, start : start + count]
            )
        target[:HEAD, :] = low(held[...])
        rest = target.at[HEAD:, :]
        cut_columns(place, qkv_ref, rest, 0, place[SEAT], 4, 3)
        cut_columns(place, out_ref, rest, columns, place[CORE], 2, 1)

    return order.run(
        kernel,
        [struct((HEAD + rows, total), qkv_weight.dtype)],
        condition,
        biases,
        qkv_weight,
        out_weight,
        scratch=(pltpu.VMEM((HEAD, total), jnp.float32),),
    )


def modulation_parts(order, heads, mod_weight, micros, width, hidden):
    shards, head, total = heads.shape
    rows, columns = mod_weight.shape
    part = H // 4 * HD
    block = hidden // shards // 4
    sizes = {"mod": columns, "qv": 2 * width, "out": width, "up": hidden, "down": width}

    def kernel(place, heads_ref, weight_ref, *refs):
        cond_rows, mod_bias, qkv_mine, qkv_near, out_bias, up_mine, up_near, down_bias = refs[:8]
        parts, (cond, mine, products) = refs[8:-3], refs[-3:]
        shard = 2 * place[LINE] + place[PAIR]
        for index in range(shards):
            values = wide(heads_ref[index, :micros, :width])
            values = wide(low(values / (1.0 + jnp.exp(-values))))
            cond[index * micros : (index + 1) * micros, :] = values
        for index in range(shards):

            @pl.when(shard == index)
            def _():
                mine[...] = low(cond[:, index * rows : (index + 1) * rows])

        cond_rows[...] = mine[...]
        products[...] = dot(mine[...], weight_ref[...], 1, 0)
        for step, target in enumerate(parts):
            line = lax.rem(place[LINE] + step, shards // 2)
            for row, pair in enumerate((1 - place[PAIR], place[PAIR])):
                source = (2 * line + pair) * micros + place[CORE]
                target[row : row + 1, :] = products[pl.ds(source, 1), :]

        def copy(target, row, column, name, start, count):
            base = 0
            for other, size in sizes.items():
                if other == name:
                    break
                base += size // shards
            share = sizes[name] // shards
            while count > 0:
                index, offset = divmod(start, share)
                line, lane = divmod(base + offset, total)
                length = min(count, share - offset, total - lane)
                source = heads_ref[index, micros + line : micros + line + 1, lane : lane + length]
                target[row : row + 1, column : column + length] = wide(source)
                start, column, count = start + length, column + length, count - length

        for row in range(6):
            copy(mod_bias, row, 0, "mod", row * width, width)
        copy(out_bias, 0, 0, "out", 0, width)
        copy(down_bias, 0, 0, "down", 0, width)
        for own in range(4):

            @pl.when(place[SEAT] == own)
            def _():
                for seat, qkv, up in ((own, qkv_mine, up_mine), (own ^ 1, qkv_near, up_near)):
                    copy(qkv, 0, 0, "qv", seat * part, part)
                    qkv[:, part : 2 * part] = jnp.zeros((1, part), jnp.float32)
                    copy(qkv, 0, 2 * part, "qv", width + seat * part, part)
                    for index in range(shards):
                        start = (index * 4 + seat) * block
                        copy(up, 0, index * block, "up", start, block)

    row = lambda count: struct((1, count), jnp.float32)
    outs = [
        struct((shards * micros, rows), jnp.bfloat16),
        struct((6, width), jnp.float32),
        row(3 * part),
        row(3 * part),
        row(width),
        row(shards * block),
        row(shards * block),
        row(width),
    ] + [struct((2, columns), jnp.float32)] * (shards // 2)
    scratch = (
        pltpu.VMEM((shards * micros, width), jnp.float32),
        pltpu.VMEM((shards * micros, rows), jnp.bfloat16),
        pltpu.VMEM((shards * micros, columns), jnp.float32),
    )
    return order.run(kernel, outs, heads, mod_weight, scratch=scratch)


def token_sums(order, shards, attn, middle, mixed, down, qv_mine, qv_near, up_mine, up_near):
    width = attn.shape[1]
    part = qv_mine.shape[1] // 3
    hidden = 4 * up_mine.shape[1]
    block = hidden // shards // 4
    sizes = (2 * width // shards, width // shards, hidden // shards, width // shards)
    starts = [sum(sizes[:index]) for index in range(4)]

    def kernel(
        place, attn_ref, middle_ref, mixed_ref, down_ref, qv_mine_ref, qv_near_ref, up_mine_ref,
        up_near_ref, out,
    ):
        out[0:2, :] = attn_ref[...]
        out[2:3, :] = middle_ref[2:3, :]
        out[3:5, :] = middle_ref[0:2, :]
        out[5:6, :] = mixed_ref[...]
        out[6:, :] = jnp.zeros((out.shape[0] - 6, width), jnp.float32)

        def copy(source, row, column, which, start, count):
            while count > 0:
                index, offset = divmod(start, sizes[which])
                line, goal = divmod(index * sum(sizes) + starts[which] + offset, width)
                length = min(count, sizes[which] - offset, width - goal)
                out[6 + line : 7 + line, goal : goal + length] = source[
                    row : row + 1, column : column + length
                ]
                start, column, count = start + length, column + length, count - length

        copy(middle_ref, 3, 0, 1, 0, width)
        copy(down_ref, 0, 0, 3, 0, width)
        for own in range(4):

            @pl.when(place[SEAT] == own)
            def _():
                for seat, qv, up in (
                    (own, qv_mine_ref, up_mine_ref),
                    (own ^ 1, qv_near_ref, up_near_ref),
                ):
                    copy(qv, 0, 0, 0, seat * part, part)
                    copy(qv, 0, 2 * part, 0, width + seat * part, part)
                    for index in range(shards):
                        start = (index * 4 + seat) * block
                        copy(up, 0, index * block, 2, start, block)

    outs = [struct((6 + sum(sizes) * shards // width, width), jnp.float32)]
    return order.run(
        kernel, outs, attn, middle, mixed, down, qv_mine, qv_near, up_mine, up_near
    )


def add_sums(order, sums, far):
    def kernel(place, sums_ref, far_ref, out):
        out[...] = sums_ref[...] + far_ref[...]

    return order.run(kernel, [struct(sums.shape, sums.dtype)], sums, far)


def join_sums(order, sums, near):
    rows, width = sums.shape

    def kernel(place, sums_ref, near_ref, out, held):
        held[...] = jnp.zeros(held.shape, jnp.float32)
        for own in range(2):

            @pl.when(place[CORE] == own)
            def _():
                held[6 * own : 6 * own + 6, :] = sums_ref[:6, :]
                held[6 - 6 * own : 12 - 6 * own, :] = near_ref[:6, :]

        held[12 : 6 + rows, :] = sums_ref[6:, :] + near_ref[6:, :]
        out[...] = low(held[...])

    total = 2 * HEAD
    return order.run(
        kernel,
        [struct((total, width), jnp.bfloat16)],
        sums,
        near,
        scratch=(pltpu.VMEM((total, width), jnp.float32),),
    )


def modulation_back(order, mine, near, mod_weight, hidden):
    lines, _, width = mine.shape
    shards = 2 * lines
    rows, columns = mod_weight.shape
    sizes = (2 * width // shards, width // shards, hidden // shards, width // shards)

    def kernel(place, weight_ref, mine_ref, near_ref, *refs):
        mod_all, biases, (products, held, total) = refs[0], refs[1:5], refs[5:]
        shard = 2 * place[LINE] + place[PAIR]
        total[...] = jnp.zeros(total.shape, jnp.float32)
        for index in range(shards):
            source = wide((near_ref if index % 2 else mine_ref)[index // 2])
            line = lax.rem(place[LINE] + (lines - index // 2), lines)
            owner = 2 * line + (1 - place[PAIR] if index % 2 else place[PAIR])
            for latent in range(2):
                for row in range(6):
                    held[pl.ds(2 * owner + latent, 1), row * width : (row + 1) * width] = source[
                        6 * latent + row : 6 * latent + row + 1, :
                    ]
            total[...] += source[12 : 12 + total.shape[0], :]
        for index in range(shards):

            @pl.when(shard == index)
            def _():
                line, start = divmod(index * sum(sizes), width)
                for target, size in zip(biases, sizes):
                    target[...] = total[line : line + 1, start : start + size]
                    start += size

        mod_all[...] = low(held[...])
        products[...] = dot(mod_all[...], weight_ref[...], 1, 1)

    outs = [struct((2 * shards, columns), jnp.bfloat16)]
    outs += [struct((1, size), jnp.float32) for size in sizes]
    outs.append(struct((2 * shards, rows), jnp.float32))
    scratch = (
        pltpu.VMEM((2 * shards, columns), jnp.float32),
        pltpu.VMEM((sum(sizes) * shards // width, width), jnp.float32),
    )
    return order.run(kernel, outs, mod_weight, mine, near, scratch=scratch)


def condition_back(order, mine, near, condition):
    micros, width = condition.shape
    lines, _, rows = mine.shape

    def kernel(place, condition_ref, mine_ref, near_ref, out, held):
        shard = 2 * place[LINE] + place[PAIR]
        for index in range(2 * lines):
            source = near_ref if index % 2 else mine_ref
            line = lax.rem(place[LINE] + (lines - index // 2), lines)
            owner = 2 * line + (1 - place[PAIR] if index % 2 else place[PAIR])
            for latent in range(micros):
                row = source[index // 2, pl.ds(micros * shard + latent, 1), :]
                held[owner, latent : latent + 1, :] = row
        values = wide(condition_ref[...])
        sigma = 1.0 / (1.0 + jnp.exp(-values))
        slope = sigma * (1.0 + values * (1.0 - sigma))
        for index in range(2 * lines):
            span = slice(index * rows, (index + 1) * rows)
            out[:, span] = held[index] * slope[:, span]

    outs = [struct(condition.shape, jnp.float32)]
    scratch = (pltpu.VMEM((2 * lines, micros, rows), jnp.float32),)
    return order.run(kernel, outs, condition, mine, near, scratch=scratch)


def cut_feed(order, up_weight, down_weight, shards):
    hidden, width = down_weight.shape
    rows, columns = up_weight.shape

    def kernel(place, up_ref, down_ref, target):
        cut_columns(place, up_ref, target, 0, place[SEAT], 4, shards)
        target[:, columns // 4 :] = down_ref[place[SEAT]]

    shape = struct((rows, columns // 4 + width), up_weight.dtype)
    return order.run(
        kernel, [shape], up_weight, down_weight.reshape(4, hidden // 4, width)
    )


def cut_tokens(order, tokens):
    shape = struct(tokens.shape[1:], tokens.dtype)

    def kernel(place, source, mine, give):
        mine[...] = source[place[CORE]]
        give[...] = source[1 - place[CORE]]

    return order.run(kernel, [shape, shape], tokens)


def lay_columns(order, quarters, *parts):
    rows = quarters[0].shape[0]

    def kernel(place, *refs):
        for own in range(4):

            @pl.when(place[SEAT] == own)
            def _():
                offset = 0
                for target, (columns, groups) in zip(refs[4:], parts):
                    part = columns // groups
                    for group in range(groups):
                        for other in range(4):
                            start = (group * 4 + (own ^ other)) * part
                            block = refs[other][:, offset : offset + part]
                            target[:, start : start + part] = wide(block)
                        offset += part

    outs = [struct((rows, 4 * columns), jnp.float32) for columns, groups in parts]
    return order.run(kernel, outs, *quarters)


def lay_rows(order, quarters):
    rows, columns = quarters[0].shape

    def kernel(place, *refs):
        for other in range(4):
            refs[4][place[SEAT] ^ other] = wide(refs[other][...])

    result = order.run(kernel, [struct((4, rows, columns), jnp.float32)], *quarters)
    return result.reshape(4 * rows, columns)


def lay_tokens(order, *pairs):
    def kernel(place, *refs):
        for index in range(len(pairs)):
            target = refs[2 * len(pairs) + index]
            target[place[CORE]] = refs[2 * index][...]
            target[1 - place[CORE]] = refs[2 * index + 1][...]

    outs = [struct((2,) + mine.shape, mine.dtype) for mine, near in pairs]
    return order.run(kernel, outs, *(value for values in pairs for value in values))


def norm_tokens(order, pieces, parts, mod_bias):
    tokens, width = pieces[0].shape
    length = 4 * tokens

    def kernel(place, *refs):
        sources, refs = refs[: len(parts)], refs[len(parts) :]
        bias_ref, (mod, out, turned, means, inverses) = refs[0], refs[5:]
        for row in range(6):
            span = slice(row * width, (row + 1) * width)
            total = bias_ref[row : row + 1, :]
            for source in sources:
                total = total + source[:, span]
            mod[row : row + 1, :] = total
        for index in range(4):
            span = slice(index * tokens, (index + 1) * tokens)
            values = wide(refs[1 + index][...])
            mean = jnp.mean(values, axis=1, keepdims=True)
            centre = values - mean
            inverse = lax.rsqrt(jnp.mean(centre * centre, axis=1, keepdims=True) + 1e-06)
            result = centre * inverse * (1.0 + mod[1:2, :]) + mod[0:1, :]
            out[span, :] = low(result)
            turned[:, span] = low(result.T)
            means[span, :] = mean
            inverses[span, :] = inverse

    outs = (
        struct((6, width), jnp.float32),
        struct((length, width), jnp.bfloat16),
        struct((width, length), jnp.bfloat16),
        struct((length, 1), jnp.float32),
        struct((length, 1), jnp.float32),
    )
    return order.run(kernel, outs, *parts, mod_bias, *pieces)


def attend(order, attn_in, weight, bias):
    length = attn_in.shape[0]
    heads = H // 4

    def kernel(place, in_ref, weight_ref, bias_ref, parts, result):
        values = (dot(in_ref[...], weight_ref[...], 1, 0) + bias_ref[...]).T
        for index in range(3 * heads):
            parts[index] = low(values[index * HD : (index + 1) * HD])
        results = []
        for head in range(heads):
            probs = soft_columns(parts[head], parts[heads + head])
            results.append(dot(parts[2 * heads + head], low(probs), 1, 0))
        result[...] = low(jnp.concatenate(results, axis=0))

    outs = (
        struct((3 * heads, HD, length), jnp.bfloat16),
        struct((heads * HD, length), jnp.bfloat16),
    )
    return order.run(kernel, outs, attn_in, weight, bias)


def attend_back(order, other, parts, out_weight, grad_attn):
    length = grad_attn.shape[0]
    heads = H // 4
    part = heads * HD
    factor = HD ** (-0.5)

    def kernel(place, parts_ref, weight_ref, grad_ref, out, sums):
        rows = pl.ds(pl.multiple_of((place[SEAT] ^ other) * part, part), part)
        grad_heads = dot(weight_ref[rows, :], grad_ref[...], 1, 1)
        grads = [None] * (3 * heads)
        for head in range(heads):
            queries, keys = parts_ref[head], parts_ref[heads + head]
            contents = parts_ref[2 * heads + head]
            grad = low(grad_heads[head * HD : (head + 1) * HD])
            probs = soft_columns(queries, keys)
            grad_probs = dot(contents, grad, 0, 0)
            inner = jnp.sum(probs * grad_probs, axis=0, keepdims=True)
            grad_scores = low(probs * (grad_probs - inner))
            grads[head] = factor * dot(keys, grad_scores, 1, 0)
            grads[heads + head] = factor * dot(queries, grad_scores, 1, 1)
            grads[2 * heads + head] = dot(grad, low(probs), 1, 1)
        result = low(jnp.concatenate(grads, axis=0).T)
        out[...] = result
        sums[...] = jnp.sum(wide(result), axis=0, keepdims=True)

    outs = (
        struct((length, 3 * part), jnp.bfloat16),
        struct((1, 3 * part), jnp.float32),
    )
    return order.run(kernel, outs, parts, out_weight, grad_attn)


def attention_out(order, quarters, out_mine, out_near, out_bias, pieces, mod):
    tokens, width = pieces[0].shape
    half, length = 2 * tokens, 4 * tokens
    part = quarters[0].shape[0]
    columns = width // 2

    def kernel(place, *refs):
        out_mine_ref, out_near_ref, bias_ref = refs[4:7]
        mod_ref, heads, weight, branch, normed, inverses, mlp_in = refs[11:]
        for other in range(4):
            rows = pl.ds(pl.multiple_of((place[SEAT] ^ other) * part, part), part)
            if other < 2:
                heads[rows, :] = refs[other][...]
            else:
                heads[rows, :half] = refs[other][:, half:]
                heads[rows, half:] = refs[other][:, :half]
        for own in range(2):

            @pl.when(place[CORE] == own)
            def _():
                weight[:, own * columns : (own + 1) * columns] = out_mine_ref[...]
                weight[:, (1 - own) * columns : (2 - own) * columns] = out_near_ref[...]

        result = dot(heads[...], weight[...], 0, 0) + bias_ref[...]
        branch[...] = result[:half]
        shift, scale = mod_ref[3:4, :], 1.0 + mod_ref[4:5, :]
        for index in range(4):
            span = slice(index * tokens, (index + 1) * tokens)
            values = wide(refs[7 + index][...]) + mod_ref[2:3, :] * result[span]
            centre = values - jnp.mean(values, axis=1, keepdims=True)
            inverse = lax.rsqrt(jnp.mean(centre * centre, axis=1, keepdims=True) + 1e-06)
            centre = centre * inverse
            normed[span, :] = centre
            inverses[span, :] = inverse
            mlp_in[span, :] = low(centre * scale + shift)

    outs = (
        struct((width, length), jnp.bfloat16),
        struct((width, width), jnp.bfloat16),
        struct((half, width), jnp.float32),
        struct((length, width), jnp.float32),
        struct((length, 1), jnp.float32),
        struct((length, width), jnp.bfloat16),
    )
    return order.run(kernel, outs, *quarters, out_mine, out_near, out_bias, *pieces, mod)


def gate_grad(order, pieces, mod):
    tokens, width = pieces[0].shape

    def kernel(place, *refs):
        mod_ref, out, sums = refs[4:]
        total = jnp.zeros(sums.shape, jnp.float32)
        for index in range(4):
            result = low(mod_ref[5:6, :] * wide(refs[index][...]))
            out[index * tokens : (index + 1) * tokens, :] = result
            if index < 2:
                total = total + jnp.sum(wide(result), axis=0, keepdims=True)
        sums[...] = total

    outs = (struct((4 * tokens, width), jnp.bfloat16), struct((1, width), jnp.float32))
    return order.run(kernel, outs, *pieces, mod)


def feed(order, mlp_in, weight, bias):
    length, width = mlp_in.shape
    hidden = weight.shape[1]
    step = hidden // 3

    def kernel(place, in_ref, weight_ref, bias_ref, act, slope):
        pre_act = dot(in_ref[...], weight_ref[...], 1, 0) + bias_ref[...]
        squared = pre_act * pre_act
        bent = jnp.tanh(GELU_ROOT * pre_act * (1.0 + GELU_CUBE * squared))
        raised = 0.5 + 0.5 * bent
        act[...] = low(pre_act * raised)
        slope[...] = raised + pre_act * (1.0 - bent * bent) * (
            0.5 * GELU_ROOT + (1.5 * GELU_ROOT * GELU_CUBE) * squared
        )

    return order.run(
        kernel,
        (
            struct((length, hidden), jnp.bfloat16),
            struct((length, hidden), jnp.float32),
        ),
        mlp_in, weight, bias,
        grid=(3,),
        in_specs=[
            whole((length, width)),
            column_block((width, hidden), step),
            column_block((1, hidden), step),
        ],
        out_specs=(
            column_block((length, hidden), step),
            column_block((length, hidden), step),
        ),
    )


def feed_back(order, grad_mlp, weight, slope):
    length, width = grad_mlp.shape
    hidden = weight.shape[0]
    step = hidden // 3

    def kernel(place, grad_ref, weight_ref, slope_ref, out, sums):
        result = low(dot(grad_ref[...], weight_ref[...], 1, 1) * slope_ref[...])
        out[...] = result
        sums[...] = jnp.sum(wide(result), axis=0, keepdims=True)

    return order.run(
        kernel,
        (struct((length, hidden), jnp.bfloat16), struct((1, hidden), jnp.float32)),
        grad_mlp, weight, slope,
        grid=(3,),
        in_specs=[
            whole((length, width)),
            row_block((hidden, width), step),
            column_block((length, hidden), step),
        ],
        out_specs=(column_block((length, hidden), step), column_block((1, hidden), step)),
    )


def feed_in_back(order, pre_mine, up_mine, pre_near, up_near):
    length, hidden = pre_mine.shape
    width = up_mine.shape[0]
    step = width // 3

    def kernel(place, pre_mine_ref, up_mine_ref, pre_near_ref, up_near_ref, out):
        out[...] = low(
            dot(pre_mine_ref[...], up_mine_ref[...], 1, 1)
            + dot(pre_near_ref[...], up_near_ref[...], 1, 1)
        )

    return order.run(
        kernel,
        [struct((length, width), jnp.bfloat16)],
        pre_mine, up_mine, pre_near, up_near,
        grid=(3,),
        in_specs=[
            whole((length, hidden)),
            row_block((width, hidden), step),
            whole((length, hidden)),
            row_block((width, hidden), step),
        ],
        out_specs=[column_block((length, width), step)],
    )


def feed_out(order, act_mine, down_mine, act_near, down_near):
    length, hidden = act_mine.shape
    width = down_mine.shape[1]
    half, step = length // 2, width // 3

    def kernel(place, act_mine_ref, down_mine_ref, act_near_ref, down_near_ref, own, give):
        result = dot(act_mine_ref[...], down_mine_ref[...], 1, 0) + dot(
            act_near_ref[...], down_near_ref[...], 1, 0
        )
        own[...] = result[:half]
        give[...] = low(result[half:])

    return order.run(
        kernel,
        (struct((half, width), jnp.float32), struct((half, width), jnp.bfloat16)),
        act_mine, down_mine, act_near, down_near,
        grid=(3,),
        in_specs=[
            whole((length, hidden)),
            column_block((hidden, width), step),
            whole((length, hidden)),
            column_block((hidden, width), step),
        ],
        out_specs=(column_block((half, width), step), column_block((half, width), step)),
    )


def weight_grad(order, shards, left_side, right_side, chunks):
    length, rows = left_side.shape
    columns = right_side.shape[1]

    def kernel(place, left_ref, right_ref, *refs):
        total = low(dot(left_ref[...], right_ref[...], 0, 0))
        give_chunks(total, shards, refs, 0)

    return order.run(kernel, chunks_of(shards, rows, columns, chunks), left_side, right_side)


def chunks_of(shards, rows, columns, chunks):
    return [struct((shards // chunks, rows // shards, columns), jnp.bfloat16)] * chunks


def give_chunks(total, shards, refs, start):
    piece = total.shape[0] // shards
    share = shards // len(refs)
    span = slice(start, start + total.shape[1])
    for shard in range(shards):
        block = total[shard * piece : (shard + 1) * piece]
        refs[shard // share][shard % share, :, span] = block


def attention_grad(order, shards, attn_turned, qkv_grad, heads_out, grad_attn, chunks):
    rows = attn_turned.shape[0]
    columns, part = qkv_grad.shape[1], grad_attn.shape[1] // 4

    def kernel(place, turned_ref, qkv_ref, heads_ref, grad_ref, *refs):
        held = refs[chunks]
        take_quarter(place, grad_ref, held, 1)
        give_chunks(low(dot(turned_ref[...], qkv_ref[...], 1, 0)), shards, refs[:chunks], 0)
        total = low(dot(heads_ref[...], held[...], 1, 0))
        give_chunks(total, shards, refs[:chunks], columns)

    return order.run(
        kernel,
        chunks_of(shards, rows, columns + part, chunks),
        attn_turned,
        qkv_grad,
        heads_out,
        grad_attn,
        scratch=(pltpu.VMEM((grad_attn.shape[0], part), grad_attn.dtype),),
    )


def take_quarter(place, source, target, other):
    columns = target.shape[1]
    for index in range(4):

        @pl.when((place[SEAT] ^ other) == index)
        def _():
            target[...] = source[:, index * columns : (index + 1) * columns]


def split_pairs(place, total, shards, met_refs, start, write):
    piece = total.shape[0] // shards
    share = shards // len(met_refs)
    span = slice(start, start + total.shape[1])
    for own in range(2):

        @pl.when(place[PAIR] == own)
        def _():
            for shard in range(shards):
                part = total[shard * piece : (shard + 1) * piece]
                met = met_refs[shard // share][shard % share, :, span]
                write(shard // 2, shard % 2 == own, low(part + wide(met)))


def weight_sum(order, shards, left_side, right_side, met, parts=1):
    rows, columns = left_side.shape[1], right_side.shape[1]
    lines = shards // 2
    share = lines // parts

    def kernel(place, left_ref, right_ref, *refs):
        met_refs, outs = refs[: len(met)], refs[len(met) :]

        def write(line, own, part):
            if own:
                outs[parts][line] = part
            else:
                outs[line // share][line % share] = part

        total = dot(left_ref[...], right_ref[...], 0, 0)
        split_pairs(place, total, shards, met_refs, 0, write)

    outs = [struct((share, rows // shards, columns), jnp.bfloat16)] * parts
    outs.append(struct((lines, rows // shards, columns), jnp.bfloat16))
    return order.run(kernel, outs, left_side, right_side, *met)


def attention_sum(order, shards, attn_turned, qkv_grad, heads_out, grad_attn, met):
    rows = attn_turned.shape[0]
    columns, part = qkv_grad.shape[1], grad_attn.shape[1] // 4

    def kernel(place, turned_ref, qkv_ref, heads_ref, grad_ref, *refs):
        met_refs, (give, mine, held) = refs[: len(met)], refs[len(met) :]
        take_quarter(place, grad_ref, held, 0)
        for left, right, start in ((turned_ref, qkv_ref, 0), (heads_ref, held, columns)):
            total = dot(left[...], right[...], 1, 0)
            span = slice(start, start + total.shape[1])

            def write(line, own, block, span=span):
                target = mine if own else give
                target[line, :, span] = block

            split_pairs(place, total, shards, met_refs, start, write)

    outs = (struct((shards // 2, rows // shards, columns + part), jnp.bfloat16),) * 2
    return order.run(
        kernel,
        outs,
        attn_turned,
        qkv_grad,
        heads_out,
        grad_attn,
        *met,
        scratch=(pltpu.VMEM((grad_attn.shape[0], part), grad_attn.dtype),),
    )


def middle_back(order, part, far, normed, inverses, pieces, mod, branch):
    length, width = part.shape
    tokens = length // 4

    def kernel(place, part_ref, far_ref, normed_ref, inverse_ref, *refs):
        mod_ref, branch_ref, grad_attn, grad_middle, sums = refs[4:]
        gate, scale = mod_ref[2:3, :], 1.0 + mod_ref[4:5, :]
        totals = [jnp.zeros((1, width), jnp.float32)] * 4
        for index in range(4):
            span = slice(index * tokens, (index + 1) * tokens)
            other = slice((index ^ 2) * tokens, ((index ^ 2) + 1) * tokens)
            grad_in = wide(part_ref[span, :]) + wide(far_ref[other, :])
            values = normed_ref[span, :]
            grad = wide(refs[index][...]) + normalize_back(
                values, inverse_ref[span, :], grad_in * scale
            )
            result = low(gate * grad)
            grad_attn[span, :] = result
            if index < 2:
                grad_middle[span, :] = grad
                terms = (grad_in, grad_in * values, grad * branch_ref[span, :], wide(result))
                totals = [
                    total + jnp.sum(term, axis=0, keepdims=True)
                    for total, term in zip(totals, terms)
                ]
        for row, total in enumerate(totals):
            sums[row : row + 1, :] = total

    outs = (
        struct((length, width), jnp.bfloat16),
        struct((2 * tokens, width), jnp.float32),
        struct((4, width), jnp.float32),
    )
    return order.run(kernel, outs, part, far, normed, inverses, *pieces, mod, branch)


def attention_in_back(order, grad_mine, qkv_mine, grad_near, qkv_near, pieces, means, inverses):
    length, columns = grad_mine.shape
    width = qkv_mine.shape[0]
    tokens, half, step = length // 4, length // 2, width // 3

    def kernel(place, grad_mine_ref, qkv_mine_ref, grad_near_ref, qkv_near_ref, *refs):
        mean_ref, inverse_ref, own, give, sums = refs[4:]
        result = dot(grad_mine_ref[...], qkv_mine_ref[...], 1, 1) + dot(
            grad_near_ref[...], qkv_near_ref[...], 1, 1
        )
        own[...] = result[:half]
        give[...] = low(result[half:])
        scaled = jnp.zeros((1, step), jnp.float32)
        for index in range(4):
            span = slice(index * tokens, (index + 1) * tokens)
            normed = (wide(refs[index][...]) - mean_ref[span, :]) * inverse_ref[span, :]
            scaled = scaled + jnp.sum(result[span] * normed, axis=0, keepdims=True)
        sums[0:1, :] = jnp.sum(result, axis=0, keepdims=True)
        sums[1:2, :] = scaled

    outs = (
        struct((half, width), jnp.float32),
        struct((half, width), jnp.bfloat16),
        struct((2, width), jnp.float32),
    )
    weights = row_block((width, columns), step)
    grads = whole((length, columns))
    stats = whole((length, 1))
    return order.run(
        kernel,
        outs,
        grad_mine,
        qkv_mine,
        grad_near,
        qkv_near,
        *pieces,
        means,
        inverses,
        grid=(3,),
        in_specs=[grads, weights, grads, weights]
        + [column_block((tokens, width), step)] * 4
        + [stats, stats],
        out_specs=[
            column_block((half, width), step),
            column_block((half, width), step),
            column_block((2, width), step),
        ],
    )


def tokens_back(order, own, far, pieces, means, inverses, mod, grad_middle):
    half, width = own.shape
    tokens = half // 2

    def kernel(
        place, own_ref, far_ref, mine_ref, near_ref, mean_ref, inverse_ref, mod_ref, grad_ref,
        mine, give,
    ):
        for index, (source, target) in enumerate(((mine_ref, mine), (near_ref, give))):
            span = slice(index * tokens, (index + 1) * tokens)
            inverse = inverse_ref[span, :]
            normed = (wide(source[...]) - mean_ref[span, :]) * inverse
            grad = (own_ref[span, :] + wide(far_ref[span, :])) * (1.0 + mod_ref[1:2, :])
            target[...] = grad_ref[span, :] + normalize_back(normed, inverse, grad)

    outs = (struct((tokens, width), jnp.float32),) * 2
    return order.run(
        kernel, outs, own, far, pieces[0], pieces[1], means, inverses, mod, grad_middle
    )


def mix(order, own, far, down_bias, pieces, branch, grads, mod):
    half, width = own.shape
    tokens = half // 2

    def kernel(
        place, own_ref, far_ref, bias_ref, mine_ref, near_ref, branch_ref, grad_mine, grad_near,
        mod_ref, mine, give, sums,
    ):
        total = jnp.zeros((1, width), jnp.float32)
        sources = ((mine_ref, grad_mine, mine), (near_ref, grad_near, give))
        for index, (source, grad, target) in enumerate(sources):
            span = slice(index * tokens, (index + 1) * tokens)
            mlp_branch = own_ref[span, :] + wide(far_ref[span, :]) + bias_ref[...]
            middle = wide(source[...]) + mod_ref[2:3, :] * branch_ref[span, :]
            target[...] = low(middle + mod_ref[5:6, :] * mlp_branch)
            total = total + jnp.sum(wide(grad[...]) * mlp_branch, axis=0, keepdims=True)
        sums[...] = total

    outs = (struct((tokens, width), jnp.bfloat16),) * 2 + (struct((1, width), jnp.float32),)
    return order.run(
        kernel, outs, own, far, down_bias, pieces[0], pieces[1], branch, grads[0], grads[1], mod
    )


def per_device(
    latents,
    condition,
    mod_weight,
    mod_bias,
    qkv_weight,
    qv_bias,
    out_weight,
    out_bias,
    up_weight,
    up_bias,
    down_weight,
    down_bias,
    cotangent,
):
    here = Place()
    order = Order(here.place)
    shards, seat, core = here.shards, here.seat, here.core
    near_seat = seat ^ 1
    micros, tokens, width = latents.shape
    rows = width // shards
    hidden = up_weight.shape[1]
    heads = H // 4
    part = heads * HD
    block = hidden // shards // 4
    wait = order.wait

    hidden_part = shards * block
    attention_widths = (3 * part, width // 2)

    biases = jnp.concatenate([mod_bias, qv_bias, out_bias, up_bias, down_bias]).reshape(1, -1)
    ring = Gather(
        here, order, cut_attention(order, condition, biases, qkv_weight, out_weight), near=True
    )
    lat_mine, lat_give = cut_tokens(order, latents)
    lat_near, lat_far = here.to_core(lat_give), here.to_side(lat_mine)
    cot_mine, cot_give = cut_tokens(order, cotangent)
    cot_near, cot_far = here.to_core(cot_give), here.to_side(cot_mine)
    feed_piece = cut_feed(order, up_weight, down_weight, shards)
    ring.turn()
    lat_near, cot_near = wait(lat_near, cot_near)
    lat_far_near, cot_far_near = here.to_side(lat_near), here.to_side(cot_near)
    lat_far = wait(lat_far)
    ring.turn()
    cot_far, lat_far_near = wait(cot_far, lat_far_near)
    lats = (lat_mine, lat_near, lat_far, lat_far_near)
    ring.turn()
    feed_ring = Gather(here, order, wait(feed_piece), hold=True)
    qkv_mine, out_mine, heads_all = ring.finish(attention_widths, HEAD, True)
    feed_ring.release()
    (
        cond_rows,
        mod_bias,
        qkv_bias_mine,
        qkv_bias_near,
        out_bias,
        up_bias_mine,
        up_bias_near,
        down_bias,
        *mod_parts,
    ) = modulation_parts(order, heads_all, mod_weight, micros, width, hidden)
    mod_sum = LineSum(here, order, mod_parts)
    mod_sum.join()
    mod_parts = mod_sum.finish()
    feed_ring.turn()
    qkv_near, out_near = ring.finish_near(attention_widths, HEAD)
    mod, attn_in, attn_turned, means_one, inverses_one = norm_tokens(
        order, lats, mod_parts, mod_bias
    )
    qkv_mine = qkv_mine.reshape(width, 3 * part)
    parts_mine, heads_mine = attend(order, attn_in, qkv_mine, qkv_bias_mine)
    heads_far = here.to_side(heads_mine)
    qkv_near = qkv_near.reshape(width, 3 * part)
    parts_near, heads_near = attend(order, attn_in, qkv_near, qkv_bias_near)
    heads_far_near = here.to_side(heads_near)
    heads_far = wait(heads_far)
    feed_ring.turn()
    quarters = (heads_mine, heads_near, heads_far, wait(heads_far_near))
    heads_out, out_full, branch, normed_two, inverses_two, mlp_in = attention_out(
        order,
        quarters,
        out_mine.reshape(width, width // 2),
        out_near.reshape(width, width // 2),
        out_bias,
        lats,
        mod,
    )
    cots = (cot_mine, cot_near, cot_far, wait(cot_far_near))
    grad_mlp, down_sums = gate_grad(order, cots, mod)
    feed_ring.turn()
    up_mine, down_mine = feed_ring.finish((hidden_part, width))
    up_near, down_near = here.to_core(up_mine), here.to_core(down_mine)
    up_mine = up_mine.reshape(width, hidden_part)
    down_mine = down_mine.reshape(hidden_part, width)
    act_mine, slope_mine = feed(order, mlp_in, up_mine, up_bias_mine)
    pre_mine, up_sums_mine = feed_back(order, grad_mlp, down_mine, slope_mine)
    up_near = wait(up_near).reshape(width, hidden_part)
    act_near, slope_near = feed(order, mlp_in, up_near, up_bias_near)
    down_near = wait(down_near).reshape(hidden_part, width)
    pre_near, up_sums_near = feed_back(order, grad_mlp, down_near, slope_near)

    mlp_part = feed_in_back(order, pre_mine, up_mine, pre_near, up_near)
    mlp_far = here.to_side(mlp_part)

    def to_core(chunks):
        return [here.to_core(chunk) for chunk in chunks]

    down_met = to_core(weight_grad(order, shards, act_near, grad_mlp, 8))
    up_met = to_core(weight_grad(order, shards, mlp_in, pre_near, 8))
    down_met = wait(*down_met)
    down_sum = Scatter(
        here, order, *weight_sum(order, shards, act_mine, grad_mlp, down_met, parts=2)
    )
    up_met = wait(*up_met)
    up_sum = Scatter(here, order, *weight_sum(order, shards, mlp_in, pre_mine, up_met))
    feed_own, feed_give = feed_out(order, act_mine, down_mine, act_near, down_near)
    feed_far = here.to_side(feed_give)

    mlp_far = wait(mlp_far)
    grad_attn, grad_middle, middle_sums = middle_back(
        order, mlp_part, mlp_far, normed_two, inverses_two, cots, mod, branch
    )
    qkv_grad_near, qv_sums_near = attend_back(order, 1, parts_near, out_full, grad_attn)
    met = to_core(
        attention_grad(order, shards, attn_turned, qkv_grad_near, heads_out, grad_attn, 8)
    )
    qkv_grad_mine, qv_sums_mine = attend_back(order, 0, parts_mine, out_full, grad_attn)
    down_sum.join()
    met = wait(*met)
    attention_total = Scatter(
        here,
        order,
        *attention_sum(order, shards, attn_turned, qkv_grad_mine, heads_out, grad_attn, met),
    )
    feed_far = wait(feed_far)
    mixed_mine, mixed_give, mix_sums = mix(
        order, feed_own, feed_far, down_bias, lats, branch, cots, mod
    )
    attn_own, attn_give, attn_sums = attention_in_back(
        order, qkv_grad_mine, qkv_mine, qkv_grad_near, qkv_near, lats, means_one, inverses_one
    )
    down_sum.turn()

    sums = token_sums(
        order, shards, attn_sums, middle_sums, mix_sums, down_sums, qv_sums_mine, qv_sums_near,
        up_sums_mine, up_sums_near,
    )
    sums_far = here.to_side(sums)
    up_sum.join()
    sums = add_sums(order, sums, wait(sums_far))
    sums_near = here.to_core(sums)
    down_sum.turn()
    sums = join_sums(order, sums, wait(sums_near))
    up_sum.turn()
    grad_down = down_sum.finish()
    sums_ring = Lines(here, order, sums)
    attn_far = here.to_side(wait(attn_give))
    up_sum.turn()
    sums_ring.join()
    down_far, down_near = here.to_side(grad_down), here.to_core(grad_down)
    grad_up = up_sum.finish()
    attention_total.join()
    attn_far = wait(attn_far)
    tokens_mine, tokens_give = tokens_back(
        order, attn_own, attn_far, lats, means_one, inverses_one, mod, grad_middle
    )
    mod_all, grad_qv_bias, grad_out_bias, grad_up_bias, grad_down_bias, grad_low = (
        modulation_back(order, *sums_ring.finish(), mod_weight, hidden)
    )
    low_ring = Lines(here, order, grad_low)
    attention_total.turn()
    low_ring.join()
    down_far, down_near = wait(down_far, down_near)
    down_far_near = here.to_core(down_far)
    up_far, up_near = here.to_side(grad_up), here.to_core(grad_up)
    attention_total.turn()
    grad_condition = condition_back(order, *low_ring.finish(), condition)
    down_far_near = wait(down_far_near)
    grad_down = lay_rows(order, (grad_down, down_near, down_far, down_far_near))
    up_far, up_near = wait(up_far, up_near)
    up_far_near = here.to_core(up_far)
    mod_all = wait(mod_all)
    grad_mod_weight = wait(dot(cond_rows, mod_all, 0, 0))
    grad_attention = attention_total.finish()
    attention_far = here.to_side(grad_attention)
    attention_near = here.to_core(grad_attention)
    up_far_near = wait(up_far_near)
    grad_up = lay_columns(
        order, (grad_up, up_near, up_far, up_far_near), (hidden_part, shards)
    )
    mixed_near, tokens_near = wait(here.to_core(mixed_give), here.to_core(tokens_give))
    mixed, grad_latents = lay_tokens(
        order, (mixed_mine, mixed_near), (tokens_mine, tokens_near)
    )
    attention_far, attention_near = wait(attention_far, attention_near)
    attention_far_near = wait(here.to_core(attention_far))
    grad_qkv, grad_out = lay_columns(
        order,
        (grad_attention, attention_near, attention_far, attention_far_near),
        (3 * part, 3),
        (width // 4, 1),
    )
    span = 6 * width // shards
    mod_span = lax.dynamic_slice_in_dim(mod_all, here.shard * span, span, 1)
    grad_mod_bias = jnp.sum(wide(mod_span), axis=0)
    grad_qv_bias, grad_out_bias, grad_up_bias, grad_down_bias = (
        vector.reshape(-1)
        for vector in (grad_qv_bias, grad_out_bias, grad_up_bias, grad_down_bias)
    )

    return (
        mixed,
        grad_latents,
        grad_condition,
        grad_mod_weight,
        grad_mod_bias,
        grad_qkv,
        grad_qv_bias,
        grad_out,
        grad_out_bias,
        grad_up,
        grad_up_bias,
        grad_down,
        grad_down_bias,
    )


def solution(mesh):
    tokens = P("fsdp", "seq", None)
    matrix = P("fsdp", None)
    vector = P("fsdp")
    parameters = (matrix, vector) * 5
    in_specs = (tokens, matrix) + parameters + (tokens,)
    out_specs = (tokens, tokens, matrix) + parameters
    return jax.shard_map(
        per_device, mesh=mesh, in_specs=in_specs, out_specs=out_specs, check_vma=False
    )
```

```python
import jax
import jax.numpy as jnp
from jax import lax
from jax.experimental import pallas as pl
from jax.experimental.pallas import tpu as pltpu
from jax.sharding import PartitionSpec as P

H = 16
HD = 72
GELU_ROOT = (2.0 / 3.141592653589793) ** 0.5
GELU_CUBE = 0.044715
SEAT, CORE, PAIR, LINE = range(4)
HEAD = 16

SCALARS = pl.BlockSpec(memory_space=pltpu.SMEM)
WHOLE = pl.BlockSpec(memory_space=pltpu.VMEM)
ANY = pl.BlockSpec(memory_space=pl.ANY)
ROOM = pltpu.CompilerParams(vmem_limit_bytes=20 << 20)
SHORT = pl.CostEstimate(flops=1, transcendentals=0, bytes_accessed=1)


def low(values):
    return values.astype(jnp.bfloat16)


def wide(values):
    return values.astype(jnp.float32)


def struct(shape, dtype):
    return jax.ShapeDtypeStruct(shape, dtype)


def whole(shape):
    return pl.BlockSpec(shape, lambda step: (0,) * len(shape))


def column_block(shape, columns):
    return pl.BlockSpec(shape[:-1] + (columns,), lambda step: (0,) * (len(shape) - 1) + (step,))


def row_block(shape, rows):
    return pl.BlockSpec((rows,) + shape[1:], lambda step: (step,) + (0,) * (len(shape) - 1))


def dot(left_side, right_side, left_dim, right_dim):
    return lax.dot_general(
        left_side,
        right_side,
        (((left_dim,), (right_dim,)), ((), ())),
        preferred_element_type=jnp.float32,
    )


def normalize_back(normed, inverse, grad):
    inner = jnp.mean(grad * normed, axis=-1, keepdims=True)
    return (grad - jnp.mean(grad, axis=-1, keepdims=True) - normed * inner) * inverse


def soft_columns(queries, keys):
    scores = dot(keys, queries, 0, 0) * HD ** (-0.5)
    raised = jnp.exp(scores - jnp.max(scores, axis=0, keepdims=True))
    return raised * (1.0 / jnp.sum(raised, axis=0, keepdims=True))


def pick(values, index, axis):
    return lax.dynamic_index_in_dim(values, index, axis, keepdims=False)


class Order:
    def __init__(self, place):
        self.place = place
        self.token = jnp.zeros((8, 128), jnp.float32)

    def wait(self, *values):
        self.token, values = lax.optimization_barrier((self.token, values))
        return values if len(values) > 1 else values[0]

    def run(self, kernel, outs, *args, grid=(), in_specs=None, out_specs=None, scratch=()):
        count, given = len(outs), len(args)

        def body(place, *refs):
            kernel(place, *refs[:given], *refs[given + 1 : given + 1 + count], *refs[given + 2 + count :])

        results = pl.pallas_call(
            body,
            out_shape=tuple(outs) + (struct(self.token.shape, self.token.dtype),),
            grid=grid,
            in_specs=[SCALARS] + list(in_specs or [WHOLE] * given) + [ANY],
            out_specs=tuple(out_specs or [WHOLE] * count) + (ANY,),
            scratch_shapes=scratch,
            input_output_aliases={given + 1: count},
            compiler_params=ROOM,
            cost_estimate=SHORT,
        )(self.place, *args, self.token)
        self.token = results[-1]
        return results[:-1] if count > 1 else results[0]


class Place:
    def __init__(self):
        self.shards = lax.axis_size("fsdp")
        self.seats = lax.axis_size("seq")
        self.line_size = self.shards // 2
        self.shard = lax.axis_index("fsdp")
        self.seat = lax.axis_index("seq")
        self.core = self.seat % 2
        places = [self.seat, self.core, self.shard % 2, self.shard // 2]
        self.place = jnp.stack(places).astype(jnp.int32)

    def to_core(self, values):
        return lax.ppermute(values, "seq", [(i, i ^ 1) for i in range(self.seats)])

    def to_side(self, values):
        return lax.ppermute(values, "seq", [(i, i ^ 2) for i in range(self.seats)])

    def to_pair(self, values):
        return lax.ppermute(values, "fsdp", [(i, i ^ 1) for i in range(self.shards)])

    def to_line(self, values, step=1):
        return lax.ppermute(
            values, "fsdp", [(i, (i + 2 * step) % self.shards) for i in range(self.shards)]
        )


def piece_shard(place, index, shards):
    lines = shards // 2
    near = index > 0 and (index % 2 == 0 or index == shards - 1)
    back = (index - 1) // 2 if near else (index + 1) // 2
    line = lax.rem(place[LINE] + (lines - back), lines)
    return 2 * line + (1 - place[PAIR] if near else place[PAIR])


class Gather:
    def __init__(self, here, order, piece, near=False, hold=False):
        self.here, self.order, self.near = here, order, near
        self.pieces, self.copies = [], []
        self.steps, self.pending = 0, []
        self.send([piece], hold)

    def send(self, pieces, hold=False):
        here = self.here
        self.pieces += pieces
        sent = []
        if self.steps < here.line_size:
            if self.steps + 1 < here.line_size:
                sent.append(here.to_line(pieces[0]))
            if not hold:
                sent.append(here.to_pair(pieces[0]))
        self.steps += 1
        self.copied = [here.to_core(piece) for piece in pieces] if self.near else []
        self.pending = sent

    def release(self):
        self.pending.append(self.here.to_pair(self.order.wait(self.pieces[0])))

    def turn(self):
        if self.pending:
            arrived = self.order.wait(*self.pending, *self.copied)
            arrived = list(arrived) if len(self.pending) + len(self.copied) > 1 else [arrived]
            count = len(self.pending)
            self.copies += arrived[count:]
            self.send(arrived[:count])

    def finish(self, widths, head=0, keep_head=False):
        while self.pending:
            self.turn()
        return self.place(self.pieces, widths, head, keep_head)

    def finish_near(self, widths, head=0):
        return self.place(self.copies + [self.order.wait(*self.copied)], widths, head, False)

    def place(self, pieces, widths, head, keep_head):
        shards = self.here.shards
        rows, total = pieces[0].shape
        rows -= head

        def kernel(place, *refs):
            targets = refs[shards:]
            for index in range(shards):
                shard = piece_shard(place, index, shards)
                start = 0
                for target, columns in zip(targets, widths):
                    target[shard] = refs[index][head:, start : start + columns]
                    start += columns
                if keep_head:
                    targets[-1][shard] = refs[index][:head, :]

        outs = [struct((shards, rows, columns), pieces[0].dtype) for columns in widths]
        if keep_head:
            outs.append(struct((shards, head, total), pieces[0].dtype))
        return self.order.run(kernel, outs, *pieces)


class Lines:
    def __init__(self, here, order, piece):
        self.here, self.order = here, order
        self.pieces = [piece] + [here.to_line(piece, step) for step in range(1, here.line_size)]

    def join(self):
        count = len(self.pieces)
        self.pieces[1:] = self.order.wait(*self.pieces[1:])

        def kernel(place, *refs):
            for index in range(count):
                refs[-1][index] = refs[index][...]

        shape = struct((count,) + self.pieces[0].shape, self.pieces[0].dtype)
        self.mine = self.order.run(kernel, [shape], *self.pieces)
        self.got = self.here.to_pair(self.mine)

    def finish(self):
        return self.mine, self.order.wait(self.got)


class LineSum:
    def __init__(self, here, order, parts):
        self.here, self.order = here, order
        self.parts = [parts[0]]
        self.parts += [here.to_line(parts[step], step) for step in range(1, here.line_size)]

    def join(self):
        count = len(self.parts)
        self.parts[1:] = self.order.wait(*self.parts[1:])

        def kernel(place, *refs):
            give, mine = refs[count:]
            total = refs[0][...]
            for index in range(1, count):
                total = total + refs[index][...]
            give[...] = total[0:1]
            mine[...] = total[1:2]

        row = struct((1, self.parts[0].shape[1]), self.parts[0].dtype)
        give, self.mine = self.order.run(kernel, [row, row], *self.parts)
        self.got = self.here.to_pair(give)

    def finish(self):
        return self.order.wait(self.got), self.mine


class Scatter:
    def __init__(self, here, order, blocks):
        count = here.line_size
        self.here, self.order, self.step = here, order, 0
        self.give, self.mine = blocks[:count], blocks[count:]
        self.under_way = [here.to_pair(self.give[1 % count])]

    def turn(self):
        here, count = self.here, self.here.line_size
        arrived = self.order.wait(*self.under_way)
        arrived = list(arrived) if len(self.under_way) > 1 else [arrived]
        self.step += 1
        own = self.mine[self.step % count]

        def kernel(place, *refs):
            total = wide(refs[0][...])
            for ref in refs[1:-1]:
                total = total + wide(ref[...])
            refs[-1][...] = low(total)

        total = self.order.run(kernel, [struct(own.shape, jnp.bfloat16)], own, *arrived)
        if self.step < count:
            back = (self.step + 1) % count
            self.under_way = [here.to_line(total), here.to_pair(self.give[back])]
        return total

    def finish(self):
        while self.step < self.here.line_size:
            total = self.turn()
        return total


def cut_columns(place, source, target, offset, index, parts, groups):
    part = source.shape[1] // groups // parts
    for choice in range(parts):

        @pl.when(index == choice)
        def _():
            for group in range(groups):
                start = (group * parts + choice) * part
                goal = offset + group * part
                target[:, goal : goal + part] = source[:, start : start + part]


def cut_attention(order, condition, biases, qkv_weight, out_weight):
    rows, width = out_weight.shape
    columns = qkv_weight.shape[1] // 4
    total = columns + width // 2
    micros = condition.shape[0]

    def kernel(place, condition_ref, biases_ref, qkv_ref, out_ref, target, held):
        held[...] = jnp.zeros(held.shape, jnp.float32)
        held[:micros, :width] = wide(condition_ref[...])
        for row, start in enumerate(range(0, biases.shape[1], total)):
            count = min(total, biases.shape[1] - start)
            held[micros + row : micros + row + 1, :count] = wide(
                biases_ref[:, start : start + count]
            )
        target[:HEAD, :] = low(held[...])
        rest = target.at[HEAD:, :]
        cut_columns(place, qkv_ref, rest, 0, place[SEAT], 4, 3)
        cut_columns(place, out_ref, rest, columns, place[CORE], 2, 1)

    return order.run(
        kernel,
        [struct((HEAD + rows, total), qkv_weight.dtype)],
        condition,
        biases,
        qkv_weight,
        out_weight,
        scratch=(pltpu.VMEM((HEAD, total), jnp.float32),),
    )


def modulation_parts(order, heads, mod_weight, micros, width, hidden):
    shards, head, total = heads.shape
    rows, columns = mod_weight.shape
    part = H // 4 * HD
    block = hidden // shards // 4
    sizes = {"mod": columns, "qv": 2 * width, "out": width, "up": hidden, "down": width}

    def kernel(place, heads_ref, weight_ref, *refs):
        cond_rows, mod_bias, qkv_mine, qkv_near, out_bias, up_mine, up_near, down_bias = refs[:8]
        parts, (cond, mine, products) = refs[8:-3], refs[-3:]
        shard = 2 * place[LINE] + place[PAIR]
        for index in range(shards):
            values = wide(heads_ref[index, :micros, :width])
            values = wide(low(values / (1.0 + jnp.exp(-values))))
            cond[index * micros : (index + 1) * micros, :] = values
        for index in range(shards):

            @pl.when(shard == index)
            def _():
                mine[...] = low(cond[:, index * rows : (index + 1) * rows])

        cond_rows[...] = mine[...]
        products[...] = dot(mine[...], weight_ref[...], 1, 0)
        for step, target in enumerate(parts):
            line = lax.rem(place[LINE] + step, shards // 2)
            for row, pair in enumerate((1 - place[PAIR], place[PAIR])):
                source = (2 * line + pair) * micros + place[CORE]
                target[row : row + 1, :] = products[pl.ds(source, 1), :]

        def copy(target, row, column, name, start, count):
            base = 0
            for other, size in sizes.items():
                if other == name:
                    break
                base += size // shards
            share = sizes[name] // shards
            while count > 0:
                index, offset = divmod(start, share)
                line, lane = divmod(base + offset, total)
                length = min(count, share - offset, total - lane)
                source = heads_ref[index, micros + line : micros + line + 1, lane : lane + length]
                target[row : row + 1, column : column + length] = wide(source)
                start, column, count = start + length, column + length, count - length

        for row in range(6):
            copy(mod_bias, row, 0, "mod", row * width, width)
        copy(out_bias, 0, 0, "out", 0, width)
        copy(down_bias, 0, 0, "down", 0, width)
        for own in range(4):

            @pl.when(place[SEAT] == own)
            def _():
                for seat, qkv, up in ((own, qkv_mine, up_mine), (own ^ 1, qkv_near, up_near)):
                    copy(qkv, 0, 0, "qv", seat * part, part)
                    qkv[:, part : 2 * part] = jnp.zeros((1, part), jnp.float32)
                    copy(qkv, 0, 2 * part, "qv", width + seat * part, part)
                    for index in range(shards):
                        start = (index * 4 + seat) * block
                        copy(up, 0, index * block, "up", start, block)

    row = lambda count: struct((1, count), jnp.float32)
    outs = [
        struct((shards * micros, rows), jnp.bfloat16),
        struct((6, width), jnp.float32),
        row(3 * part),
        row(3 * part),
        row(width),
        row(shards * block),
        row(shards * block),
        row(width),
    ] + [struct((2, columns), jnp.float32)] * (shards // 2)
    scratch = (
        pltpu.VMEM((shards * micros, width), jnp.float32),
        pltpu.VMEM((shards * micros, rows), jnp.bfloat16),
        pltpu.VMEM((shards * micros, columns), jnp.float32),
    )
    return order.run(kernel, outs, heads, mod_weight, scratch=scratch)


def token_sums(order, shards, attn, middle, mixed, down, qv_mine, qv_near, up_mine, up_near):
    width = attn.shape[1]
    part = qv_mine.shape[1] // 3
    hidden = 4 * up_mine.shape[1]
    block = hidden // shards // 4
    sizes = (2 * width // shards, width // shards, hidden // shards, width // shards)
    starts = [sum(sizes[:index]) for index in range(4)]

    def kernel(
        place, attn_ref, middle_ref, mixed_ref, down_ref, qv_mine_ref, qv_near_ref, up_mine_ref,
        up_near_ref, out,
    ):
        out[0:2, :] = attn_ref[...]
        out[2:3, :] = middle_ref[2:3, :]
        out[3:5, :] = middle_ref[0:2, :]
        out[5:6, :] = mixed_ref[...]
        out[6:, :] = jnp.zeros((out.shape[0] - 6, width), jnp.float32)

        def copy(source, row, column, which, start, count):
            while count > 0:
                index, offset = divmod(start, sizes[which])
                line, goal = divmod(index * sum(sizes) + starts[which] + offset, width)
                length = min(count, sizes[which] - offset, width - goal)
                out[6 + line : 7 + line, goal : goal + length] = source[
                    row : row + 1, column : column + length
                ]
                start, column, count = start + length, column + length, count - length

        copy(middle_ref, 3, 0, 1, 0, width)
        copy(down_ref, 0, 0, 3, 0, width)
        for own in range(4):

            @pl.when(place[SEAT] == own)
            def _():
                for seat, qv, up in (
                    (own, qv_mine_ref, up_mine_ref),
                    (own ^ 1, qv_near_ref, up_near_ref),
                ):
                    copy(qv, 0, 0, 0, seat * part, part)
                    copy(qv, 0, 2 * part, 0, width + seat * part, part)
                    for index in range(shards):
                        start = (index * 4 + seat) * block
                        copy(up, 0, index * block, 2, start, block)

    outs = [struct((6 + sum(sizes) * shards // width, width), jnp.float32)]
    return order.run(
        kernel, outs, attn, middle, mixed, down, qv_mine, qv_near, up_mine, up_near
    )


def add_sums(order, sums, far):
    rows, width = sums.shape

    def kernel(place, sums_ref, far_ref, out, held):
        held[...] = jnp.zeros(held.shape, jnp.float32)
        held[:rows, :] = sums_ref[...] + far_ref[...]
        out[...] = low(held[...])

    return order.run(
        kernel,
        [struct((HEAD, width), jnp.bfloat16)],
        sums,
        far,
        scratch=(pltpu.VMEM((HEAD, width), jnp.float32),),
    )


def modulation_back(order, mine, near, mine_far, near_far, mod_weight, hidden):
    lines, _, width = mine.shape
    shards = 2 * lines
    rows, columns = mod_weight.shape
    sizes = (2 * width // shards, width // shards, hidden // shards, width // shards)

    def kernel(place, weight_ref, mine_ref, near_ref, mine_far_ref, near_far_ref, *refs):
        mod_all, biases, (products, held, total) = refs[0], refs[1:5], refs[5:]
        shard = 2 * place[LINE] + place[PAIR]
        total[...] = jnp.zeros(total.shape, jnp.float32)
        sources = (
            (mine_ref, place[PAIR], place[CORE]),
            (near_ref, 1 - place[PAIR], place[CORE]),
            (mine_far_ref, place[PAIR], 1 - place[CORE]),
            (near_far_ref, 1 - place[PAIR], 1 - place[CORE]),
        )
        for back in range(lines):
            line = lax.rem(place[LINE] + (lines - back), lines)
            for source_ref, pair, core in sources:
                source = wide(source_ref[back])
                goal = 2 * (2 * line + pair) + core
                for row in range(6):
                    span = slice(row * width, (row + 1) * width)
                    held[pl.ds(goal, 1), span] = source[row : row + 1, :]
        for core in range(2):
            for back in range(lines):
                for source_ref in (mine_ref, near_ref, mine_far_ref, near_far_ref)[
                    2 * core : 2 * core + 2
                ]:
                    total[...] += wide(source_ref[back])[6 : 6 + total.shape[0], :]
        for index in range(shards):

            @pl.when(shard == index)
            def _():
                line, start = divmod(index * sum(sizes), width)
                for target, size in zip(biases, sizes):
                    target[...] = total[line : line + 1, start : start + size]
                    start += size

        mod_all[...] = low(held[...])
        products[...] = dot(mod_all[...], weight_ref[...], 1, 1)

    outs = [struct((2 * shards, columns), jnp.bfloat16)]
    outs += [struct((1, size), jnp.float32) for size in sizes]
    outs.append(struct((2 * shards, rows), jnp.float32))
    scratch = (
        pltpu.VMEM((2 * shards, columns), jnp.float32),
        pltpu.VMEM((sum(sizes) * shards // width, width), jnp.float32),
    )
    return order.run(
        kernel, outs, mod_weight, mine, near, mine_far, near_far, scratch=scratch
    )


def condition_back(order, mine, near, condition):
    micros, width = condition.shape
    lines, _, rows = mine.shape

    def kernel(place, condition_ref, mine_ref, near_ref, out, held):
        shard = 2 * place[LINE] + place[PAIR]
        for index in range(2 * lines):
            source = near_ref if index % 2 else mine_ref
            line = lax.rem(place[LINE] + (lines - index // 2), lines)
            owner = 2 * line + (1 - place[PAIR] if index % 2 else place[PAIR])
            for latent in range(micros):
                row = source[index // 2, pl.ds(micros * shard + latent, 1), :]
                held[owner, latent : latent + 1, :] = row
        values = wide(condition_ref[...])
        sigma = 1.0 / (1.0 + jnp.exp(-values))
        slope = sigma * (1.0 + values * (1.0 - sigma))
        for index in range(2 * lines):
            span = slice(index * rows, (index + 1) * rows)
            out[:, span] = held[index] * slope[:, span]

    outs = [struct(condition.shape, jnp.float32)]
    scratch = (pltpu.VMEM((2 * lines, micros, rows), jnp.float32),)
    return order.run(kernel, outs, condition, mine, near, scratch=scratch)


def cut_feed(order, up_weight, down_weight, shards):
    hidden, width = down_weight.shape
    rows, columns = up_weight.shape

    def kernel(place, up_ref, down_ref, target):
        cut_columns(place, up_ref, target, 0, place[SEAT], 4, shards)
        target[:, columns // 4 :] = down_ref[place[SEAT]]

    shape = struct((rows, columns // 4 + width), up_weight.dtype)
    return order.run(
        kernel, [shape], up_weight, down_weight.reshape(4, hidden // 4, width)
    )


def cut_tokens(order, tokens):
    shape = struct(tokens.shape[1:], tokens.dtype)

    def kernel(place, source, mine, give):
        mine[...] = source[place[CORE]]
        give[...] = source[1 - place[CORE]]

    return order.run(kernel, [shape, shape], tokens)


def lay_columns(order, quarters, *parts):
    rows = quarters[0].shape[0]

    def kernel(place, *refs):
        for own in range(4):

            @pl.when(place[SEAT] == own)
            def _():
                offset = 0
                for target, (columns, groups) in zip(refs[4:], parts):
                    part = columns // groups
                    for group in range(groups):
                        for other in range(4):
                            start = (group * 4 + (own ^ other)) * part
                            block = refs[other][:, offset : offset + part]
                            target[:, start : start + part] = wide(block)
                        offset += part

    outs = [struct((rows, 4 * columns), jnp.float32) for columns, groups in parts]
    return order.run(kernel, outs, *quarters)


def lay_rows(order, quarters):
    rows, columns = quarters[0].shape

    def kernel(place, *refs):
        for other in range(4):
            refs[4][place[SEAT] ^ other] = wide(refs[other][...])

    result = order.run(kernel, [struct((4, rows, columns), jnp.float32)], *quarters)
    return result.reshape(4 * rows, columns)


def lay_tokens(order, *pairs):
    def kernel(place, *refs):
        for index in range(len(pairs)):
            target = refs[2 * len(pairs) + index]
            target[place[CORE]] = refs[2 * index][...]
            target[1 - place[CORE]] = refs[2 * index + 1][...]

    outs = [struct((2,) + mine.shape, mine.dtype) for mine, near in pairs]
    return order.run(kernel, outs, *(value for values in pairs for value in values))


def norm_tokens(order, pieces, parts, mod_bias):
    tokens, width = pieces[0].shape
    length = 4 * tokens

    def kernel(place, *refs):
        sources, refs = refs[: len(parts)], refs[len(parts) :]
        bias_ref, (mod, out, turned, means, inverses) = refs[0], refs[5:]
        for row in range(6):
            span = slice(row * width, (row + 1) * width)
            total = bias_ref[row : row + 1, :]
            for source in sources:
                total = total + source[:, span]
            mod[row : row + 1, :] = total
        for index in range(4):
            span = slice(index * tokens, (index + 1) * tokens)
            values = wide(refs[1 + index][...])
            mean = jnp.mean(values, axis=1, keepdims=True)
            centre = values - mean
            inverse = lax.rsqrt(jnp.mean(centre * centre, axis=1, keepdims=True) + 1e-06)
            result = centre * inverse * (1.0 + mod[1:2, :]) + mod[0:1, :]
            out[span, :] = low(result)
            turned[:, span] = low(result.T)
            means[span, :] = mean
            inverses[span, :] = inverse

    outs = (
        struct((6, width), jnp.float32),
        struct((length, width), jnp.bfloat16),
        struct((width, length), jnp.bfloat16),
        struct((length, 1), jnp.float32),
        struct((length, 1), jnp.float32),
    )
    return order.run(kernel, outs, *parts, mod_bias, *pieces)


def attend(order, attn_in, weight, bias):
    length = attn_in.shape[0]
    heads = H // 4

    def kernel(place, in_ref, weight_ref, bias_ref, parts, result):
        values = (dot(in_ref[...], weight_ref[...], 1, 0) + bias_ref[...]).T
        for index in range(3 * heads):
            parts[index] = low(values[index * HD : (index + 1) * HD])
        results = []
        for head in range(heads):
            probs = soft_columns(parts[head], parts[heads + head])
            results.append(dot(parts[2 * heads + head], low(probs), 1, 0))
        result[...] = low(jnp.concatenate(results, axis=0))

    outs = (
        struct((3 * heads, HD, length), jnp.bfloat16),
        struct((heads * HD, length), jnp.bfloat16),
    )
    return order.run(kernel, outs, attn_in, weight, bias)


def attend_back(order, other, parts, out_weight, grad_attn):
    length = grad_attn.shape[0]
    heads = H // 4
    part = heads * HD
    factor = HD ** (-0.5)

    def kernel(place, parts_ref, weight_ref, grad_ref, out, sums):
        rows = pl.ds(pl.multiple_of((place[SEAT] ^ other) * part, part), part)
        grad_heads = dot(weight_ref[rows, :], grad_ref[...], 1, 1)
        grads = [None] * (3 * heads)
        for head in range(heads):
            queries, keys = parts_ref[head], parts_ref[heads + head]
            contents = parts_ref[2 * heads + head]
            grad = low(grad_heads[head * HD : (head + 1) * HD])
            probs = soft_columns(queries, keys)
            grad_probs = dot(contents, grad, 0, 0)
            inner = jnp.sum(probs * grad_probs, axis=0, keepdims=True)
            grad_scores = low(probs * (grad_probs - inner))
            grads[head] = factor * dot(keys, grad_scores, 1, 0)
            grads[heads + head] = factor * dot(queries, grad_scores, 1, 1)
            grads[2 * heads + head] = dot(grad, low(probs), 1, 1)
        result = low(jnp.concatenate(grads, axis=0).T)
        out[...] = result
        sums[...] = jnp.sum(wide(result), axis=0, keepdims=True)

    outs = (
        struct((length, 3 * part), jnp.bfloat16),
        struct((1, 3 * part), jnp.float32),
    )
    return order.run(kernel, outs, parts, out_weight, grad_attn)


def attention_out(order, quarters, out_mine, out_near, out_bias, pieces, mod):
    tokens, width = pieces[0].shape
    half, length = 2 * tokens, 4 * tokens
    part = quarters[0].shape[0]
    columns = width // 2

    def kernel(place, *refs):
        out_mine_ref, out_near_ref, bias_ref = refs[4:7]
        mod_ref, heads, weight, branch, normed, inverses, mlp_in = refs[11:]
        for other in range(4):
            rows = pl.ds(pl.multiple_of((place[SEAT] ^ other) * part, part), part)
            if other < 2:
                heads[rows, :] = refs[other][...]
            else:
                heads[rows, :half] = refs[other][:, half:]
                heads[rows, half:] = refs[other][:, :half]
        for own in range(2):

            @pl.when(place[CORE] == own)
            def _():
                weight[:, own * columns : (own + 1) * columns] = out_mine_ref[...]
                weight[:, (1 - own) * columns : (2 - own) * columns] = out_near_ref[...]

        result = dot(heads[...], weight[...], 0, 0) + bias_ref[...]
        branch[...] = result[:half]
        shift, scale = mod_ref[3:4, :], 1.0 + mod_ref[4:5, :]
        for index in range(4):
            span = slice(index * tokens, (index + 1) * tokens)
            values = wide(refs[7 + index][...]) + mod_ref[2:3, :] * result[span]
            centre = values - jnp.mean(values, axis=1, keepdims=True)
            inverse = lax.rsqrt(jnp.mean(centre * centre, axis=1, keepdims=True) + 1e-06)
            centre = centre * inverse
            normed[span, :] = centre
            inverses[span, :] = inverse
            mlp_in[span, :] = low(centre * scale + shift)

    outs = (
        struct((width, length), jnp.bfloat16),
        struct((width, width), jnp.bfloat16),
        struct((half, width), jnp.float32),
        struct((length, width), jnp.float32),
        struct((length, 1), jnp.float32),
        struct((length, width), jnp.bfloat16),
    )
    return order.run(kernel, outs, *quarters, out_mine, out_near, out_bias, *pieces, mod)


def gate_grad(order, pieces, mod):
    tokens, width = pieces[0].shape

    def kernel(place, *refs):
        mod_ref, out, sums = refs[4:]
        total = jnp.zeros(sums.shape, jnp.float32)
        for index in range(4):
            result = low(mod_ref[5:6, :] * wide(refs[index][...]))
            out[index * tokens : (index + 1) * tokens, :] = result
            if index < 2:
                total = total + jnp.sum(wide(result), axis=0, keepdims=True)
        sums[...] = total

    outs = (struct((4 * tokens, width), jnp.bfloat16), struct((1, width), jnp.float32))
    return order.run(kernel, outs, *pieces, mod)


def feed(order, mlp_in, weight, bias):
    length, width = mlp_in.shape
    hidden = weight.shape[1]
    step = hidden // 3

    def kernel(place, in_ref, weight_ref, bias_ref, act, slope):
        pre_act = dot(in_ref[...], weight_ref[...], 1, 0) + bias_ref[...]
        squared = pre_act * pre_act
        bent = jnp.tanh(GELU_ROOT * pre_act * (1.0 + GELU_CUBE * squared))
        raised = 0.5 + 0.5 * bent
        act[...] = low(pre_act * raised)
        slope[...] = raised + pre_act * (1.0 - bent * bent) * (
            0.5 * GELU_ROOT + (1.5 * GELU_ROOT * GELU_CUBE) * squared
        )

    return order.run(
        kernel,
        (
            struct((length, hidden), jnp.bfloat16),
            struct((length, hidden), jnp.float32),
        ),
        mlp_in, weight, bias,
        grid=(3,),
        in_specs=[
            whole((length, width)),
            column_block((width, hidden), step),
            column_block((1, hidden), step),
        ],
        out_specs=(
            column_block((length, hidden), step),
            column_block((length, hidden), step),
        ),
    )


def feed_back(order, grad_mlp, weight, slope):
    length, width = grad_mlp.shape
    hidden = weight.shape[0]
    step = hidden // 3

    def kernel(place, grad_ref, weight_ref, slope_ref, out, sums):
        result = low(dot(grad_ref[...], weight_ref[...], 1, 1) * slope_ref[...])
        out[...] = result
        sums[...] = jnp.sum(wide(result), axis=0, keepdims=True)

    return order.run(
        kernel,
        (struct((length, hidden), jnp.bfloat16), struct((1, hidden), jnp.float32)),
        grad_mlp, weight, slope,
        grid=(3,),
        in_specs=[
            whole((length, width)),
            row_block((hidden, width), step),
            column_block((length, hidden), step),
        ],
        out_specs=(column_block((length, hidden), step), column_block((1, hidden), step)),
    )


def feed_in_back(order, pre_mine, up_mine, pre_near, up_near):
    length, hidden = pre_mine.shape
    width = up_mine.shape[0]
    step = width // 3

    def kernel(place, pre_mine_ref, up_mine_ref, pre_near_ref, up_near_ref, out):
        out[...] = low(
            dot(pre_mine_ref[...], up_mine_ref[...], 1, 1)
            + dot(pre_near_ref[...], up_near_ref[...], 1, 1)
        )

    return order.run(
        kernel,
        [struct((length, width), jnp.bfloat16)],
        pre_mine, up_mine, pre_near, up_near,
        grid=(3,),
        in_specs=[
            whole((length, hidden)),
            row_block((width, hidden), step),
            whole((length, hidden)),
            row_block((width, hidden), step),
        ],
        out_specs=[column_block((length, width), step)],
    )


def feed_out(order, act_mine, down_mine, act_near, down_near):
    length, hidden = act_mine.shape
    width = down_mine.shape[1]
    half, step = length // 2, width // 3

    def kernel(place, act_mine_ref, down_mine_ref, act_near_ref, down_near_ref, own, give):
        result = dot(act_mine_ref[...], down_mine_ref[...], 1, 0) + dot(
            act_near_ref[...], down_near_ref[...], 1, 0
        )
        own[...] = result[:half]
        give[...] = low(result[half:])

    return order.run(
        kernel,
        (struct((half, width), jnp.float32), struct((half, width), jnp.bfloat16)),
        act_mine, down_mine, act_near, down_near,
        grid=(3,),
        in_specs=[
            whole((length, hidden)),
            column_block((hidden, width), step),
            whole((length, hidden)),
            column_block((hidden, width), step),
        ],
        out_specs=(column_block((half, width), step), column_block((half, width), step)),
    )


def weight_grad(order, shards, left_side, right_side, chunks):
    length, rows = left_side.shape
    columns = right_side.shape[1]

    def kernel(place, left_ref, right_ref, *refs):
        total = low(dot(left_ref[...], right_ref[...], 0, 0))
        give_chunks(total, shards, refs, 0)

    return order.run(kernel, chunks_of(shards, rows, columns, chunks), left_side, right_side)


def chunks_of(shards, rows, columns, chunks):
    return [struct((shards // chunks, rows // shards, columns), jnp.bfloat16)] * chunks


def give_chunks(total, shards, refs, start):
    piece = total.shape[0] // shards
    share = shards // len(refs)
    span = slice(start, start + total.shape[1])
    for shard in range(shards):
        block = total[shard * piece : (shard + 1) * piece]
        refs[shard // share][shard % share, :, span] = block


def attention_grad(order, shards, attn_turned, qkv_grad, heads_out, grad_attn, chunks):
    rows = attn_turned.shape[0]
    columns, part = qkv_grad.shape[1], grad_attn.shape[1] // 4

    def kernel(place, turned_ref, qkv_ref, heads_ref, grad_ref, *refs):
        held = refs[chunks]
        take_quarter(place, grad_ref, held, 1)
        give_chunks(low(dot(turned_ref[...], qkv_ref[...], 1, 0)), shards, refs[:chunks], 0)
        total = low(dot(heads_ref[...], held[...], 1, 0))
        give_chunks(total, shards, refs[:chunks], columns)

    return order.run(
        kernel,
        chunks_of(shards, rows, columns + part, chunks),
        attn_turned,
        qkv_grad,
        heads_out,
        grad_attn,
        scratch=(pltpu.VMEM((grad_attn.shape[0], part), grad_attn.dtype),),
    )


def take_quarter(place, source, target, other):
    columns = target.shape[1]
    for index in range(4):

        @pl.when((place[SEAT] ^ other) == index)
        def _():
            target[...] = source[:, index * columns : (index + 1) * columns]


def add_met(total, shards, met_refs, held, start):
    piece = total.shape[0] // shards
    share = shards // len(met_refs)
    span = slice(start, start + total.shape[1])
    for shard in range(shards):
        part = total[shard * piece : (shard + 1) * piece]
        met = met_refs[shard // share][shard % share, :, span]
        held[shard, :, span] = low(part + wide(met))


def give_blocks(place, shards, held, outs):
    lines = shards // 2
    for back in range(lines):
        line = lax.rem(place[LINE] + (lines - back), lines)
        outs[back][...] = held[2 * line + 1 - place[PAIR]]
        outs[lines + back][...] = held[2 * line + place[PAIR]]


def weight_sum(order, shards, left_side, right_side, met):
    rows, columns = left_side.shape[1], right_side.shape[1]
    piece = rows // shards

    def kernel(place, left_ref, right_ref, *refs):
        met_refs, outs, held = refs[: len(met)], refs[len(met) : -1], refs[-1]
        total = dot(left_ref[...], right_ref[...], 0, 0)
        add_met(total, shards, met_refs, held, 0)
        give_blocks(place, shards, held, outs)

    outs = [struct((piece, columns), jnp.bfloat16)] * shards
    scratch = (pltpu.VMEM((shards, piece, columns), jnp.bfloat16),)
    return order.run(kernel, outs, left_side, right_side, *met, scratch=scratch)


def attention_sum(order, shards, attn_turned, qkv_grad, heads_out, grad_attn, met):
    rows = attn_turned.shape[0]
    piece = rows // shards
    columns, part = qkv_grad.shape[1], grad_attn.shape[1] // 4

    def kernel(place, turned_ref, qkv_ref, heads_ref, grad_ref, *refs):
        met_refs, outs, (quarter, held) = refs[: len(met)], refs[len(met) : -2], refs[-2:]
        take_quarter(place, grad_ref, quarter, 0)
        for left, right, start in ((turned_ref, qkv_ref, 0), (heads_ref, quarter, columns)):
            add_met(dot(left[...], right[...], 1, 0), shards, met_refs, held, start)
        give_blocks(place, shards, held, outs)

    outs = [struct((piece, columns + part), jnp.bfloat16)] * shards
    scratch = (
        pltpu.VMEM((grad_attn.shape[0], part), grad_attn.dtype),
        pltpu.VMEM((shards, piece, columns + part), jnp.bfloat16),
    )
    return order.run(
        kernel, outs, attn_turned, qkv_grad, heads_out, grad_attn, *met, scratch=scratch
    )


def middle_back(order, part, far, normed, inverses, pieces, mod, branch):
    length, width = part.shape
    tokens = length // 4

    def kernel(place, part_ref, far_ref, normed_ref, inverse_ref, *refs):
        mod_ref, branch_ref, grad_attn, grad_middle, sums = refs[4:]
        gate, scale = mod_ref[2:3, :], 1.0 + mod_ref[4:5, :]
        totals = [jnp.zeros((1, width), jnp.float32)] * 4
        for index in range(4):
            span = slice(index * tokens, (index + 1) * tokens)
            other = slice((index ^ 2) * tokens, ((index ^ 2) + 1) * tokens)
            grad_in = wide(part_ref[span, :]) + wide(far_ref[other, :])
            values = normed_ref[span, :]
            grad = wide(refs[index][...]) + normalize_back(
                values, inverse_ref[span, :], grad_in * scale
            )
            result = low(gate * grad)
            grad_attn[span, :] = result
            if index < 2:
                grad_middle[span, :] = grad
                terms = (grad_in, grad_in * values, grad * branch_ref[span, :], wide(result))
                totals = [
                    total + jnp.sum(term, axis=0, keepdims=True)
                    for total, term in zip(totals, terms)
                ]
        for row, total in enumerate(totals):
            sums[row : row + 1, :] = total

    outs = (
        struct((length, width), jnp.bfloat16),
        struct((2 * tokens, width), jnp.float32),
        struct((4, width), jnp.float32),
    )
    return order.run(kernel, outs, part, far, normed, inverses, *pieces, mod, branch)


def attention_in_back(order, grad_mine, qkv_mine, grad_near, qkv_near, pieces, means, inverses):
    length, columns = grad_mine.shape
    width = qkv_mine.shape[0]
    tokens, half, step = length // 4, length // 2, width // 3

    def kernel(place, grad_mine_ref, qkv_mine_ref, grad_near_ref, qkv_near_ref, *refs):
        mean_ref, inverse_ref, own, give, sums = refs[4:]
        result = dot(grad_mine_ref[...], qkv_mine_ref[...], 1, 1) + dot(
            grad_near_ref[...], qkv_near_ref[...], 1, 1
        )
        own[...] = result[:half]
        give[...] = low(result[half:])
        scaled = jnp.zeros((1, step), jnp.float32)
        for index in range(4):
            span = slice(index * tokens, (index + 1) * tokens)
            normed = (wide(refs[index][...]) - mean_ref[span, :]) * inverse_ref[span, :]
            scaled = scaled + jnp.sum(result[span] * normed, axis=0, keepdims=True)
        sums[0:1, :] = jnp.sum(result, axis=0, keepdims=True)
        sums[1:2, :] = scaled

    outs = (
        struct((half, width), jnp.float32),
        struct((half, width), jnp.bfloat16),
        struct((2, width), jnp.float32),
    )
    weights = row_block((width, columns), step)
    grads = whole((length, columns))
    stats = whole((length, 1))
    return order.run(
        kernel,
        outs,
        grad_mine,
        qkv_mine,
        grad_near,
        qkv_near,
        *pieces,
        means,
        inverses,
        grid=(3,),
        in_specs=[grads, weights, grads, weights]
        + [column_block((tokens, width), step)] * 4
        + [stats, stats],
        out_specs=[
            column_block((half, width), step),
            column_block((half, width), step),
            column_block((2, width), step),
        ],
    )


def tokens_back(order, own, far, pieces, means, inverses, mod, grad_middle):
    half, width = own.shape
    tokens = half // 2

    def kernel(
        place, own_ref, far_ref, mine_ref, near_ref, mean_ref, inverse_ref, mod_ref, grad_ref,
        mine, give,
    ):
        for index, (source, target) in enumerate(((mine_ref, mine), (near_ref, give))):
            span = slice(index * tokens, (index + 1) * tokens)
            inverse = inverse_ref[span, :]
            normed = (wide(source[...]) - mean_ref[span, :]) * inverse
            grad = (own_ref[span, :] + wide(far_ref[span, :])) * (1.0 + mod_ref[1:2, :])
            target[...] = grad_ref[span, :] + normalize_back(normed, inverse, grad)

    outs = (struct((tokens, width), jnp.float32),) * 2
    return order.run(
        kernel, outs, own, far, pieces[0], pieces[1], means, inverses, mod, grad_middle
    )


def mix(order, own, far, down_bias, pieces, branch, grads, mod):
    half, width = own.shape
    tokens = half // 2

    def kernel(
        place, own_ref, far_ref, bias_ref, mine_ref, near_ref, branch_ref, grad_mine, grad_near,
        mod_ref, mine, give, sums,
    ):
        total = jnp.zeros((1, width), jnp.float32)
        sources = ((mine_ref, grad_mine, mine), (near_ref, grad_near, give))
        for index, (source, grad, target) in enumerate(sources):
            span = slice(index * tokens, (index + 1) * tokens)
            mlp_branch = own_ref[span, :] + wide(far_ref[span, :]) + bias_ref[...]
            middle = wide(source[...]) + mod_ref[2:3, :] * branch_ref[span, :]
            target[...] = low(middle + mod_ref[5:6, :] * mlp_branch)
            total = total + jnp.sum(wide(grad[...]) * mlp_branch, axis=0, keepdims=True)
        sums[...] = total

    outs = (struct((tokens, width), jnp.bfloat16),) * 2 + (struct((1, width), jnp.float32),)
    return order.run(
        kernel, outs, own, far, down_bias, pieces[0], pieces[1], branch, grads[0], grads[1], mod
    )


def per_device(
    latents,
    condition,
    mod_weight,
    mod_bias,
    qkv_weight,
    qv_bias,
    out_weight,
    out_bias,
    up_weight,
    up_bias,
    down_weight,
    down_bias,
    cotangent,
):
    here = Place()
    order = Order(here.place)
    shards, seat, core = here.shards, here.seat, here.core
    near_seat = seat ^ 1
    micros, tokens, width = latents.shape
    rows = width // shards
    hidden = up_weight.shape[1]
    heads = H // 4
    part = heads * HD
    block = hidden // shards // 4
    wait = order.wait

    hidden_part = shards * block
    attention_widths = (3 * part, width // 2)

    biases = jnp.concatenate([mod_bias, qv_bias, out_bias, up_bias, down_bias]).reshape(1, -1)
    ring = Gather(
        here, order, cut_attention(order, condition, biases, qkv_weight, out_weight), near=True
    )
    lat_mine, lat_give = cut_tokens(order, latents)
    lat_near, lat_far = here.to_core(lat_give), here.to_side(lat_mine)
    cot_mine, cot_give = cut_tokens(order, cotangent)
    cot_near, cot_far = here.to_core(cot_give), here.to_side(cot_mine)
    feed_piece = cut_feed(order, up_weight, down_weight, shards)
    ring.turn()
    lat_near, cot_near = wait(lat_near, cot_near)
    lat_far_near, cot_far_near = here.to_side(lat_near), here.to_side(cot_near)
    lat_far = wait(lat_far)
    ring.turn()
    cot_far, lat_far_near = wait(cot_far, lat_far_near)
    lats = (lat_mine, lat_near, lat_far, lat_far_near)
    ring.turn()
    feed_ring = Gather(here, order, wait(feed_piece), hold=True)
    qkv_mine, out_mine, heads_all = ring.finish(attention_widths, HEAD, True)
    feed_ring.release()
    (
        cond_rows,
        mod_bias,
        qkv_bias_mine,
        qkv_bias_near,
        out_bias,
        up_bias_mine,
        up_bias_near,
        down_bias,
        *mod_parts,
    ) = modulation_parts(order, heads_all, mod_weight, micros, width, hidden)
    mod_sum = LineSum(here, order, mod_parts)
    mod_sum.join()
    mod_parts = mod_sum.finish()
    feed_ring.turn()
    qkv_near, out_near = ring.finish_near(attention_widths, HEAD)
    mod, attn_in, attn_turned, means_one, inverses_one = norm_tokens(
        order, lats, mod_parts, mod_bias
    )
    qkv_mine = qkv_mine.reshape(width, 3 * part)
    parts_mine, heads_mine = attend(order, attn_in, qkv_mine, qkv_bias_mine)
    heads_far = here.to_side(heads_mine)
    qkv_near = qkv_near.reshape(width, 3 * part)
    parts_near, heads_near = attend(order, attn_in, qkv_near, qkv_bias_near)
    heads_far_near = here.to_side(heads_near)
    heads_far = wait(heads_far)
    feed_ring.turn()
    quarters = (heads_mine, heads_near, heads_far, wait(heads_far_near))
    heads_out, out_full, branch, normed_two, inverses_two, mlp_in = attention_out(
        order,
        quarters,
        out_mine.reshape(width, width // 2),
        out_near.reshape(width, width // 2),
        out_bias,
        lats,
        mod,
    )
    cots = (cot_mine, cot_near, cot_far, wait(cot_far_near))
    grad_mlp, down_sums = gate_grad(order, cots, mod)
    feed_ring.turn()
    up_mine, down_mine = feed_ring.finish((hidden_part, width))
    up_near, down_near = here.to_core(up_mine), here.to_core(down_mine)
    up_mine = up_mine.reshape(width, hidden_part)
    down_mine = down_mine.reshape(hidden_part, width)
    act_mine, slope_mine = feed(order, mlp_in, up_mine, up_bias_mine)
    pre_mine, up_sums_mine = feed_back(order, grad_mlp, down_mine, slope_mine)
    up_near = wait(up_near).reshape(width, hidden_part)
    act_near, slope_near = feed(order, mlp_in, up_near, up_bias_near)
    down_near = wait(down_near).reshape(hidden_part, width)
    pre_near, up_sums_near = feed_back(order, grad_mlp, down_near, slope_near)

    mlp_part = feed_in_back(order, pre_mine, up_mine, pre_near, up_near)
    mlp_far = here.to_side(mlp_part)

    def to_core(chunks):
        return [here.to_core(chunk) for chunk in chunks]

    down_met = to_core(weight_grad(order, shards, act_near, grad_mlp, 8))
    up_met = to_core(weight_grad(order, shards, mlp_in, pre_near, 8))
    down_met = wait(*down_met)
    down_sum = Scatter(here, order, weight_sum(order, shards, act_mine, grad_mlp, down_met))
    up_met = wait(*up_met)
    up_sum = Scatter(here, order, weight_sum(order, shards, mlp_in, pre_mine, up_met))
    down_sum.turn()
    feed_own, feed_give = feed_out(order, act_mine, down_mine, act_near, down_near)
    feed_far = here.to_side(feed_give)

    up_sum.turn()
    mlp_far = wait(mlp_far)
    grad_attn, grad_middle, middle_sums = middle_back(
        order, mlp_part, mlp_far, normed_two, inverses_two, cots, mod, branch
    )
    down_sum.turn()
    qkv_grad_near, qv_sums_near = attend_back(order, 1, parts_near, out_full, grad_attn)
    up_sum.turn()
    met = to_core(
        attention_grad(order, shards, attn_turned, qkv_grad_near, heads_out, grad_attn, 8)
    )
    met = wait(*met)
    down_sum.turn()
    qkv_grad_mine, qv_sums_mine = attend_back(order, 0, parts_mine, out_full, grad_attn)
    up_sum.turn()
    attention_total = Scatter(
        here,
        order,
        attention_sum(order, shards, attn_turned, qkv_grad_mine, heads_out, grad_attn, met),
    )
    grad_down = down_sum.finish()
    down_far, down_near = here.to_side(grad_down), here.to_core(grad_down)
    feed_far = wait(feed_far)
    mixed_mine, mixed_give, mix_sums = mix(
        order, feed_own, feed_far, down_bias, lats, branch, cots, mod
    )
    grad_up = up_sum.finish()
    attention_total.turn()
    down_far, down_near = wait(down_far, down_near)
    down_far_near = here.to_core(down_far)
    up_far, up_near = here.to_side(grad_up), here.to_core(grad_up)
    attn_own, attn_give, attn_sums = attention_in_back(
        order, qkv_grad_mine, qkv_mine, qkv_grad_near, qkv_near, lats, means_one, inverses_one
    )
    sums = token_sums(
        order, shards, attn_sums, middle_sums, mix_sums, down_sums, qv_sums_mine, qv_sums_near,
        up_sums_mine, up_sums_near,
    )
    sums_far = here.to_side(sums)
    attention_total.turn()
    sums = add_sums(order, sums, wait(sums_far))
    up_far, up_near, down_far_near = wait(up_far, up_near, down_far_near)
    sums_ring = Lines(here, order, sums)
    grad_down = lay_rows(order, (grad_down, down_near, down_far, down_far_near))
    attention_total.turn()
    sums_ring.join()
    up_far_near = here.to_core(up_far)
    attn_far = here.to_side(wait(attn_give))
    up_far_near = wait(up_far_near)
    grad_up = lay_columns(
        order, (grad_up, up_near, up_far, up_far_near), (hidden_part, shards)
    )
    sums_mine, sums_near = sums_ring.finish()
    sums_mine_far, sums_near_far = here.to_core(sums_mine), here.to_core(sums_near)
    grad_attention = attention_total.finish()
    attention_far = here.to_side(grad_attention)
    attention_near = here.to_core(grad_attention)
    sums_mine_far, sums_near_far = wait(sums_mine_far, sums_near_far)
    mod_all, grad_qv_bias, grad_out_bias, grad_up_bias, grad_down_bias, grad_low = (
        modulation_back(
            order, sums_mine, sums_near, sums_mine_far, sums_near_far, mod_weight, hidden
        )
    )
    low_ring = Lines(here, order, grad_low)
    attn_far = wait(attn_far)
    tokens_mine, tokens_give = tokens_back(
        order, attn_own, attn_far, lats, means_one, inverses_one, mod, grad_middle
    )
    attention_far, attention_near = wait(attention_far, attention_near)
    attention_far_near = here.to_core(attention_far)
    mixed_near, tokens_near = here.to_core(mixed_give), here.to_core(tokens_give)
    low_ring.join()
    attention_far_near = wait(attention_far_near)
    grad_qkv, grad_out = lay_columns(
        order,
        (grad_attention, attention_near, attention_far, attention_far_near),
        (3 * part, 3),
        (width // 4, 1),
    )
    mixed_near, tokens_near = wait(mixed_near, tokens_near)
    mixed, grad_latents = lay_tokens(
        order, (mixed_mine, mixed_near), (tokens_mine, tokens_near)
    )
    grad_condition = condition_back(order, *low_ring.finish(), condition)
    mod_all = wait(mod_all)
    grad_mod_weight = dot(cond_rows, mod_all, 0, 0)
    span = 6 * width // shards
    mod_span = lax.dynamic_slice_in_dim(mod_all, here.shard * span, span, 1)
    grad_mod_bias = jnp.sum(wide(mod_span), axis=0)
    grad_qv_bias, grad_out_bias, grad_up_bias, grad_down_bias = (
        vector.reshape(-1)
        for vector in (grad_qv_bias, grad_out_bias, grad_up_bias, grad_down_bias)
    )

    return (
        mixed,
        grad_latents,
        grad_condition,
        grad_mod_weight,
        grad_mod_bias,
        grad_qkv,
        grad_qv_bias,
        grad_out,
        grad_out_bias,
        grad_up,
        grad_up_bias,
        grad_down,
        grad_down_bias,
    )


def solution(mesh):
    tokens = P("fsdp", "seq", None)
    matrix = P("fsdp", None)
    vector = P("fsdp")
    parameters = (matrix, vector) * 5
    in_specs = (tokens, matrix) + parameters + (tokens,)
    out_specs = (tokens, tokens, matrix) + parameters
    return jax.shard_map(
        per_device, mesh=mesh, in_specs=in_specs, out_specs=out_specs, check_vma=False
    )
```

```python
import jax
import jax.numpy as jnp
from jax import lax
from jax.experimental import pallas as pl
from jax.experimental.pallas import tpu as pltpu
from jax.sharding import PartitionSpec as P

H = 16
HD = 72
GELU_ROOT = (2.0 / 3.141592653589793) ** 0.5
GELU_CUBE = 0.044715
SEAT, CORE, PAIR, LINE = range(4)
HEAD = 16

SCALARS = pl.BlockSpec(memory_space=pltpu.SMEM)
WHOLE = pl.BlockSpec(memory_space=pltpu.VMEM)
ANY = pl.BlockSpec(memory_space=pl.ANY)
ROOM = pltpu.CompilerParams(vmem_limit_bytes=14 << 20)
SHORT = pl.CostEstimate(flops=1, transcendentals=0, bytes_accessed=1)


def low(values):
    return values.astype(jnp.bfloat16)


def wide(values):
    return values.astype(jnp.float32)


def struct(shape, dtype):
    return jax.ShapeDtypeStruct(shape, dtype)


def whole(shape):
    return pl.BlockSpec(shape, lambda step: (0,) * len(shape))


def column_block(shape, columns):
    return pl.BlockSpec(shape[:-1] + (columns,), lambda step: (0,) * (len(shape) - 1) + (step,))


def row_block(shape, rows):
    return pl.BlockSpec((rows,) + shape[1:], lambda step: (step,) + (0,) * (len(shape) - 1))


def dot(left_side, right_side, left_dim, right_dim):
    return lax.dot_general(
        left_side,
        right_side,
        (((left_dim,), (right_dim,)), ((), ())),
        preferred_element_type=jnp.float32,
    )


def normalize_back(normed, inverse, grad):
    inner = jnp.mean(grad * normed, axis=-1, keepdims=True)
    return (grad - jnp.mean(grad, axis=-1, keepdims=True) - normed * inner) * inverse


def soft_columns(queries, keys):
    scores = dot(keys, queries, 0, 0) * HD ** (-0.5)
    raised = jnp.exp(scores - jnp.max(scores, axis=0, keepdims=True))
    return raised * (1.0 / jnp.sum(raised, axis=0, keepdims=True))


def pick(values, index, axis):
    return lax.dynamic_index_in_dim(values, index, axis, keepdims=False)


class Order:
    def __init__(self, place):
        self.place = place
        self.token = jnp.zeros((8, 128), jnp.float32)

    def wait(self, *values):
        self.token, values = lax.optimization_barrier((self.token, values))
        return values if len(values) > 1 else values[0]

    def run(self, kernel, outs, *args, grid=(), in_specs=None, out_specs=None, scratch=()):
        count, given = len(outs), len(args)

        def body(place, *refs):
            kernel(place, *refs[:given], *refs[given + 1 : given + 1 + count], *refs[given + 2 + count :])

        results = pl.pallas_call(
            body,
            out_shape=tuple(outs) + (struct(self.token.shape, self.token.dtype),),
            grid=grid,
            in_specs=[SCALARS] + list(in_specs or [WHOLE] * given) + [ANY],
            out_specs=tuple(out_specs or [WHOLE] * count) + (ANY,),
            scratch_shapes=scratch,
            input_output_aliases={given + 1: count},
            compiler_params=ROOM,
            cost_estimate=SHORT,
        )(self.place, *args, self.token)
        self.token = results[-1]
        return results[:-1] if count > 1 else results[0]


class Place:
    def __init__(self):
        self.shards = lax.axis_size("fsdp")
        self.seats = lax.axis_size("seq")
        self.line_size = self.shards // 2
        self.shard = lax.axis_index("fsdp")
        self.seat = lax.axis_index("seq")
        self.core = self.seat % 2
        places = [self.seat, self.core, self.shard % 2, self.shard // 2]
        self.place = jnp.stack(places).astype(jnp.int32)

    def to_core(self, values):
        return lax.ppermute(values, "seq", [(i, i ^ 1) for i in range(self.seats)])

    def to_side(self, values):
        return lax.ppermute(values, "seq", [(i, i ^ 2) for i in range(self.seats)])

    def to_pair(self, values):
        return lax.ppermute(values, "fsdp", [(i, i ^ 1) for i in range(self.shards)])

    def to_line(self, values, step=1):
        return lax.ppermute(
            values, "fsdp", [(i, (i + 2 * step) % self.shards) for i in range(self.shards)]
        )


def piece_shard(place, index, shards):
    lines = shards // 2
    near = index > 0 and (index % 2 == 0 or index == shards - 1)
    back = (index - 1) // 2 if near else (index + 1) // 2
    line = lax.rem(place[LINE] + (lines - back), lines)
    return 2 * line + (1 - place[PAIR] if near else place[PAIR])


class Gather:
    def __init__(self, here, order, piece, near=False, hold=False):
        self.here, self.order, self.near = here, order, near
        self.pieces, self.copies = [], []
        self.steps, self.pending = 0, []
        self.send([piece], hold)

    def send(self, pieces, hold=False):
        here = self.here
        self.pieces += pieces
        sent = []
        if self.steps < here.line_size:
            if self.steps + 1 < here.line_size:
                sent.append(here.to_line(pieces[0]))
            if not hold:
                sent.append(here.to_pair(pieces[0]))
        self.steps += 1
        self.copied = [here.to_core(piece) for piece in pieces] if self.near else []
        self.pending = sent

    def release(self):
        self.pending.append(self.here.to_pair(self.order.wait(self.pieces[0])))

    def turn(self):
        if self.pending:
            arrived = self.order.wait(*self.pending, *self.copied)
            arrived = list(arrived) if len(self.pending) + len(self.copied) > 1 else [arrived]
            count = len(self.pending)
            self.copies += arrived[count:]
            self.send(arrived[:count])

    def finish(self, widths, head=0, keep_head=False):
        while self.pending:
            self.turn()
        return self.place(self.pieces, widths, head, keep_head)

    def finish_near(self, widths, head=0):
        return self.place(self.copies + [self.order.wait(*self.copied)], widths, head, False)

    def place(self, pieces, widths, head, keep_head):
        shards = self.here.shards
        rows, total = pieces[0].shape
        rows -= head

        def kernel(place, *refs):
            targets = refs[shards:]
            for index in range(shards):
                shard = piece_shard(place, index, shards)
                start = 0
                for target, columns in zip(targets, widths):
                    target[shard] = refs[index][head:, start : start + columns]
                    start += columns
                if keep_head:
                    targets[-1][shard] = refs[index][:head, :]

        outs = [struct((shards, rows, columns), pieces[0].dtype) for columns in widths]
        if keep_head:
            outs.append(struct((shards, head, total), pieces[0].dtype))
        return self.order.run(kernel, outs, *pieces)


class Lines:
    def __init__(self, here, order, piece):
        self.here, self.order = here, order
        self.pieces = [piece] + [here.to_line(piece, step) for step in range(1, here.line_size)]

    def join(self):
        count = len(self.pieces)
        self.pieces[1:] = self.order.wait(*self.pieces[1:])

        def kernel(place, *refs):
            for index in range(count):
                refs[-1][index] = refs[index][...]

        shape = struct((count,) + self.pieces[0].shape, self.pieces[0].dtype)
        self.mine = self.order.run(kernel, [shape], *self.pieces)
        self.got = self.here.to_pair(self.mine)

    def finish(self):
        return self.mine, self.order.wait(self.got)


class LineSum:
    def __init__(self, here, order, parts):
        self.here, self.order = here, order
        self.parts = [parts[0]]
        self.parts += [here.to_line(parts[step], step) for step in range(1, here.line_size)]

    def join(self):
        count = len(self.parts)
        self.parts[1:] = self.order.wait(*self.parts[1:])

        def kernel(place, *refs):
            give, mine = refs[count:]
            total = refs[0][...]
            for index in range(1, count):
                total = total + refs[index][...]
            give[...] = total[0:1]
            mine[...] = total[1:2]

        row = struct((1, self.parts[0].shape[1]), self.parts[0].dtype)
        give, self.mine = self.order.run(kernel, [row, row], *self.parts)
        self.got = self.here.to_pair(give)

    def finish(self):
        return self.order.wait(self.got), self.mine


class Scatter:
    def __init__(self, here, order, blocks):
        count = here.line_size
        self.here, self.order, self.step = here, order, 0
        self.give, self.mine = blocks[:count], blocks[count:]
        self.under_way = [here.to_pair(self.give[1 % count])]

    def turn(self):
        here, count = self.here, self.here.line_size
        arrived = self.order.wait(*self.under_way)
        arrived = list(arrived) if len(self.under_way) > 1 else [arrived]
        self.step += 1
        own = self.mine[self.step % count]

        def kernel(place, *refs):
            total = wide(refs[0][...])
            for ref in refs[1:-1]:
                total = total + wide(ref[...])
            refs[-1][...] = low(total)

        total = self.order.run(kernel, [struct(own.shape, jnp.bfloat16)], own, *arrived)
        if self.step < count:
            back = (self.step + 1) % count
            self.under_way = [here.to_line(total), here.to_pair(self.give[back])]
        return total

    def finish(self):
        while self.step < self.here.line_size:
            total = self.turn()
        return total


def cut_columns(place, source, target, offset, index, parts, groups):
    part = source.shape[1] // groups // parts
    for choice in range(parts):

        @pl.when(index == choice)
        def _():
            for group in range(groups):
                start = (group * parts + choice) * part
                goal = offset + group * part
                target[:, goal : goal + part] = source[:, start : start + part]


def cut_attention(order, condition, biases, qkv_weight, out_weight):
    rows, width = out_weight.shape
    columns = qkv_weight.shape[1] // 4
    total = columns + width // 2
    micros = condition.shape[0]

    def kernel(place, condition_ref, biases_ref, qkv_ref, out_ref, target, held):
        held[...] = jnp.zeros(held.shape, jnp.float32)
        held[:micros, :width] = wide(condition_ref[...])
        for row, start in enumerate(range(0, biases.shape[1], total)):
            count = min(total, biases.shape[1] - start)
            held[micros + row : micros + row + 1, :count] = wide(
                biases_ref[:, start : start + count]
            )
        target[:HEAD, :] = low(held[...])
        rest = target.at[HEAD:, :]
        cut_columns(place, qkv_ref, rest, 0, place[SEAT], 4, 3)
        cut_columns(place, out_ref, rest, columns, place[CORE], 2, 1)

    return order.run(
        kernel,
        [struct((HEAD + rows, total), qkv_weight.dtype)],
        condition,
        biases,
        qkv_weight,
        out_weight,
        scratch=(pltpu.VMEM((HEAD, total), jnp.float32),),
    )


def modulation_parts(order, heads, mod_weight, micros, width, hidden):
    shards, head, total = heads.shape
    rows, columns = mod_weight.shape
    part = H // 4 * HD
    block = hidden // shards // 4
    sizes = {"mod": columns, "qv": 2 * width, "out": width, "up": hidden, "down": width}

    def kernel(place, heads_ref, weight_ref, *refs):
        cond_rows, mod_bias, qkv_mine, qkv_near, out_bias, up_mine, up_near, down_bias = refs[:8]
        parts, (cond, mine, products) = refs[8:-3], refs[-3:]
        shard = 2 * place[LINE] + place[PAIR]
        for index in range(shards):
            values = wide(heads_ref[index, :micros, :width])
            values = wide(low(values / (1.0 + jnp.exp(-values))))
            cond[index * micros : (index + 1) * micros, :] = values
        for index in range(shards):

            @pl.when(shard == index)
            def _():
                mine[...] = low(cond[:, index * rows : (index + 1) * rows])

        cond_rows[...] = mine[...]
        products[...] = dot(mine[...], weight_ref[...], 1, 0)
        for step, target in enumerate(parts):
            line = lax.rem(place[LINE] + step, shards // 2)
            for row, pair in enumerate((1 - place[PAIR], place[PAIR])):
                source = (2 * line + pair) * micros + place[CORE]
                target[row : row + 1, :] = products[pl.ds(source, 1), :]

        def copy(target, row, column, name, start, count):
            base = 0
            for other, size in sizes.items():
                if other == name:
                    break
                base += size // shards
            share = sizes[name] // shards
            while count > 0:
                index, offset = divmod(start, share)
                line, lane = divmod(base + offset, total)
                length = min(count, share - offset, total - lane)
                source = heads_ref[index, micros + line : micros + line + 1, lane : lane + length]
                target[row : row + 1, column : column + length] = wide(source)
                start, column, count = start + length, column + length, count - length

        for row in range(6):
            copy(mod_bias, row, 0, "mod", row * width, width)
        copy(out_bias, 0, 0, "out", 0, width)
        copy(down_bias, 0, 0, "down", 0, width)
        for own in range(4):

            @pl.when(place[SEAT] == own)
            def _():
                for seat, qkv, up in ((own, qkv_mine, up_mine), (own ^ 1, qkv_near, up_near)):
                    copy(qkv, 0, 0, "qv", seat * part, part)
                    qkv[:, part : 2 * part] = jnp.zeros((1, part), jnp.float32)
                    copy(qkv, 0, 2 * part, "qv", width + seat * part, part)
                    for index in range(shards):
                        start = (index * 4 + seat) * block
                        copy(up, 0, index * block, "up", start, block)

    row = lambda count: struct((1, count), jnp.float32)
    outs = [
        struct((shards * micros, rows), jnp.bfloat16),
        struct((6, width), jnp.float32),
        row(3 * part),
        row(3 * part),
        row(width),
        row(shards * block),
        row(shards * block),
        row(width),
    ] + [struct((2, columns), jnp.float32)] * (shards // 2)
    scratch = (
        pltpu.VMEM((shards * micros, width), jnp.float32),
        pltpu.VMEM((shards * micros, rows), jnp.bfloat16),
        pltpu.VMEM((shards * micros, columns), jnp.float32),
    )
    return order.run(kernel, outs, heads, mod_weight, scratch=scratch)


def token_sums(order, shards, attn, middle, mixed, down, qv_mine, qv_near, up_mine, up_near):
    width = attn.shape[1]
    part = qv_mine.shape[1] // 3
    hidden = 4 * up_mine.shape[1]
    block = hidden // shards // 4
    sizes = (2 * width // shards, width // shards, hidden // shards, width // shards)
    starts = [sum(sizes[:index]) for index in range(4)]

    def kernel(
        place, attn_ref, middle_ref, mixed_ref, down_ref, qv_mine_ref, qv_near_ref, up_mine_ref,
        up_near_ref, out,
    ):
        out[0:2, :] = attn_ref[...]
        out[2:3, :] = middle_ref[2:3, :]
        out[3:5, :] = middle_ref[0:2, :]
        out[5:6, :] = mixed_ref[...]
        out[6:, :] = jnp.zeros((out.shape[0] - 6, width), jnp.float32)

        def copy(source, row, column, which, start, count):
            while count > 0:
                index, offset = divmod(start, sizes[which])
                line, goal = divmod(index * sum(sizes) + starts[which] + offset, width)
                length = min(count, sizes[which] - offset, width - goal)
                out[6 + line : 7 + line, goal : goal + length] = source[
                    row : row + 1, column : column + length
                ]
                start, column, count = start + length, column + length, count - length

        copy(middle_ref, 3, 0, 1, 0, width)
        copy(down_ref, 0, 0, 3, 0, width)
        for own in range(4):

            @pl.when(place[SEAT] == own)
            def _():
                for seat, qv, up in (
                    (own, qv_mine_ref, up_mine_ref),
                    (own ^ 1, qv_near_ref, up_near_ref),
                ):
                    copy(qv, 0, 0, 0, seat * part, part)
                    copy(qv, 0, 2 * part, 0, width + seat * part, part)
                    for index in range(shards):
                        start = (index * 4 + seat) * block
                        copy(up, 0, index * block, 2, start, block)

    outs = [struct((6 + sum(sizes) * shards // width, width), jnp.float32)]
    return order.run(
        kernel, outs, attn, middle, mixed, down, qv_mine, qv_near, up_mine, up_near
    )


def add_sums(order, sums, far):
    rows, width = sums.shape

    def kernel(place, sums_ref, far_ref, out, held):
        held[...] = jnp.zeros(held.shape, jnp.float32)
        held[:rows, :] = sums_ref[...] + far_ref[...]
        out[...] = low(held[...])

    return order.run(
        kernel,
        [struct((HEAD, width), jnp.bfloat16)],
        sums,
        far,
        scratch=(pltpu.VMEM((HEAD, width), jnp.float32),),
    )


def modulation_back(order, mine, near, mine_far, near_far, mod_weight, hidden):
    lines, _, width = mine.shape
    shards = 2 * lines
    rows, columns = mod_weight.shape
    sizes = (2 * width // shards, width // shards, hidden // shards, width // shards)

    def kernel(place, weight_ref, mine_ref, near_ref, mine_far_ref, near_far_ref, *refs):
        mod_all, biases, (products, held, total) = refs[0], refs[1:5], refs[5:]
        shard = 2 * place[LINE] + place[PAIR]
        total[...] = jnp.zeros(total.shape, jnp.float32)
        sources = (
            (mine_ref, place[PAIR], place[CORE]),
            (near_ref, 1 - place[PAIR], place[CORE]),
            (mine_far_ref, place[PAIR], 1 - place[CORE]),
            (near_far_ref, 1 - place[PAIR], 1 - place[CORE]),
        )
        for back in range(lines):
            line = lax.rem(place[LINE] + (lines - back), lines)
            for source_ref, pair, core in sources:
                source = wide(source_ref[back])
                goal = 2 * (2 * line + pair) + core
                for row in range(6):
                    span = slice(row * width, (row + 1) * width)
                    held[pl.ds(goal, 1), span] = source[row : row + 1, :]
        for core in range(2):
            for back in range(lines):
                for source_ref in (mine_ref, near_ref, mine_far_ref, near_far_ref)[
                    2 * core : 2 * core + 2
                ]:
                    total[...] += wide(source_ref[back])[6 : 6 + total.shape[0], :]
        for index in range(shards):

            @pl.when(shard == index)
            def _():
                line, start = divmod(index * sum(sizes), width)
                for target, size in zip(biases, sizes):
                    target[...] = total[line : line + 1, start : start + size]
                    start += size

        mod_all[...] = low(held[...])
        products[...] = dot(mod_all[...], weight_ref[...], 1, 1)

    outs = [struct((2 * shards, columns), jnp.bfloat16)]
    outs += [struct((1, size), jnp.float32) for size in sizes]
    outs.append(struct((2 * shards, rows), jnp.float32))
    scratch = (
        pltpu.VMEM((2 * shards, columns), jnp.float32),
        pltpu.VMEM((sum(sizes) * shards // width, width), jnp.float32),
    )
    return order.run(
        kernel, outs, mod_weight, mine, near, mine_far, near_far, scratch=scratch
    )


def condition_back(order, mine, near, condition):
    micros, width = condition.shape
    lines, _, rows = mine.shape

    def kernel(place, condition_ref, mine_ref, near_ref, out, held):
        shard = 2 * place[LINE] + place[PAIR]
        for index in range(2 * lines):
            source = near_ref if index % 2 else mine_ref
            line = lax.rem(place[LINE] + (lines - index // 2), lines)
            owner = 2 * line + (1 - place[PAIR] if index % 2 else place[PAIR])
            for latent in range(micros):
                row = source[index // 2, pl.ds(micros * shard + latent, 1), :]
                held[owner, latent : latent + 1, :] = row
        values = wide(condition_ref[...])
        sigma = 1.0 / (1.0 + jnp.exp(-values))
        slope = sigma * (1.0 + values * (1.0 - sigma))
        for index in range(2 * lines):
            span = slice(index * rows, (index + 1) * rows)
            out[:, span] = held[index] * slope[:, span]

    outs = [struct(condition.shape, jnp.float32)]
    scratch = (pltpu.VMEM((2 * lines, micros, rows), jnp.float32),)
    return order.run(kernel, outs, condition, mine, near, scratch=scratch)


def cut_feed(order, up_weight, down_weight, shards):
    hidden, width = down_weight.shape
    rows, columns = up_weight.shape

    def kernel(place, up_ref, down_ref, target):
        cut_columns(place, up_ref, target, 0, place[SEAT], 4, shards)
        target[:, columns // 4 :] = down_ref[place[SEAT]]

    shape = struct((rows, columns // 4 + width), up_weight.dtype)
    return order.run(
        kernel, [shape], up_weight, down_weight.reshape(4, hidden // 4, width)
    )


def cut_tokens(order, tokens):
    shape = struct(tokens.shape[1:], tokens.dtype)

    def kernel(place, source, mine, give):
        mine[...] = source[place[CORE]]
        give[...] = source[1 - place[CORE]]

    return order.run(kernel, [shape, shape], tokens)


def lay_columns(order, quarters, *parts):
    rows = quarters[0].shape[0]

    def kernel(place, *refs):
        for own in range(4):

            @pl.when(place[SEAT] == own)
            def _():
                offset = 0
                for target, (columns, groups) in zip(refs[4:], parts):
                    part = columns // groups
                    for group in range(groups):
                        for other in range(4):
                            start = (group * 4 + (own ^ other)) * part
                            block = refs[other][:, offset : offset + part]
                            target[:, start : start + part] = wide(block)
                        offset += part

    outs = [struct((rows, 4 * columns), jnp.float32) for columns, groups in parts]
    return order.run(kernel, outs, *quarters)


def lay_rows(order, quarters):
    rows, columns = quarters[0].shape

    def kernel(place, *refs):
        for other in range(4):
            refs[4][place[SEAT] ^ other] = wide(refs[other][...])

    result = order.run(kernel, [struct((4, rows, columns), jnp.float32)], *quarters)
    return result.reshape(4 * rows, columns)


def lay_tokens(order, *pairs):
    def kernel(place, *refs):
        for index in range(len(pairs)):
            target = refs[2 * len(pairs) + index]
            target[place[CORE]] = refs[2 * index][...]
            target[1 - place[CORE]] = refs[2 * index + 1][...]

    outs = [struct((2,) + mine.shape, mine.dtype) for mine, near in pairs]
    return order.run(kernel, outs, *(value for values in pairs for value in values))


def norm_tokens(order, pieces, parts, mod_bias):
    tokens, width = pieces[0].shape
    length = 4 * tokens

    def kernel(place, *refs):
        sources, refs = refs[: len(parts)], refs[len(parts) :]
        bias_ref, (mod, out, turned, means, inverses) = refs[0], refs[5:]
        for row in range(6):
            span = slice(row * width, (row + 1) * width)
            total = bias_ref[row : row + 1, :]
            for source in sources:
                total = total + source[:, span]
            mod[row : row + 1, :] = total
        for index in range(4):
            span = slice(index * tokens, (index + 1) * tokens)
            values = wide(refs[1 + index][...])
            mean = jnp.mean(values, axis=1, keepdims=True)
            centre = values - mean
            inverse = lax.rsqrt(jnp.mean(centre * centre, axis=1, keepdims=True) + 1e-06)
            result = centre * inverse * (1.0 + mod[1:2, :]) + mod[0:1, :]
            out[span, :] = low(result)
            turned[:, span] = low(result.T)
            means[span, :] = mean
            inverses[span, :] = inverse

    outs = (
        struct((6, width), jnp.float32),
        struct((length, width), jnp.bfloat16),
        struct((width, length), jnp.bfloat16),
        struct((length, 1), jnp.float32),
        struct((length, 1), jnp.float32),
    )
    return order.run(kernel, outs, *parts, mod_bias, *pieces)


def attend(order, attn_in, weight, bias):
    length = attn_in.shape[0]
    heads = H // 4

    def kernel(place, in_ref, weight_ref, bias_ref, parts, result):
        values = (dot(in_ref[...], weight_ref[...], 1, 0) + bias_ref[...]).T
        for index in range(3 * heads):
            parts[index] = low(values[index * HD : (index + 1) * HD])
        results = []
        for head in range(heads):
            probs = soft_columns(parts[head], parts[heads + head])
            results.append(dot(parts[2 * heads + head], low(probs), 1, 0))
        result[...] = low(jnp.concatenate(results, axis=0))

    outs = (
        struct((3 * heads, HD, length), jnp.bfloat16),
        struct((heads * HD, length), jnp.bfloat16),
    )
    return order.run(kernel, outs, attn_in, weight, bias)


def attend_back(order, other, parts, out_weight, grad_attn):
    length = grad_attn.shape[0]
    heads = H // 4
    part = heads * HD
    factor = HD ** (-0.5)

    def kernel(place, parts_ref, weight_ref, grad_ref, out, sums):
        rows = pl.ds(pl.multiple_of((place[SEAT] ^ other) * part, part), part)
        grad_heads = dot(weight_ref[rows, :], grad_ref[...], 1, 1)
        grads = [None] * (3 * heads)
        for head in range(heads):
            queries, keys = parts_ref[head], parts_ref[heads + head]
            contents = parts_ref[2 * heads + head]
            grad = low(grad_heads[head * HD : (head + 1) * HD])
            probs = soft_columns(queries, keys)
            grad_probs = dot(contents, grad, 0, 0)
            inner = jnp.sum(probs * grad_probs, axis=0, keepdims=True)
            grad_scores = low(probs * (grad_probs - inner))
            grads[head] = factor * dot(keys, grad_scores, 1, 0)
            grads[heads + head] = factor * dot(queries, grad_scores, 1, 1)
            grads[2 * heads + head] = dot(grad, low(probs), 1, 1)
        result = low(jnp.concatenate(grads, axis=0).T)
        out[...] = result
        sums[...] = jnp.sum(wide(result), axis=0, keepdims=True)

    outs = (
        struct((length, 3 * part), jnp.bfloat16),
        struct((1, 3 * part), jnp.float32),
    )
    return order.run(kernel, outs, parts, out_weight, grad_attn)


def attention_out(order, quarters, out_mine, out_near, out_bias, pieces, mod):
    tokens, width = pieces[0].shape
    half, length = 2 * tokens, 4 * tokens
    part = quarters[0].shape[0]
    columns = width // 2

    def kernel(place, *refs):
        out_mine_ref, out_near_ref, bias_ref = refs[4:7]
        mod_ref, heads, weight, branch, normed, inverses, mlp_in = refs[11:]
        for other in range(4):
            rows = pl.ds(pl.multiple_of((place[SEAT] ^ other) * part, part), part)
            if other < 2:
                heads[rows, :] = refs[other][...]
            else:
                heads[rows, :half] = refs[other][:, half:]
                heads[rows, half:] = refs[other][:, :half]
        for own in range(2):

            @pl.when(place[CORE] == own)
            def _():
                weight[:, own * columns : (own + 1) * columns] = out_mine_ref[...]
                weight[:, (1 - own) * columns : (2 - own) * columns] = out_near_ref[...]

        result = dot(heads[...], weight[...], 0, 0) + bias_ref[...]
        branch[...] = result[:half]
        shift, scale = mod_ref[3:4, :], 1.0 + mod_ref[4:5, :]
        for index in range(4):
            span = slice(index * tokens, (index + 1) * tokens)
            values = wide(refs[7 + index][...]) + mod_ref[2:3, :] * result[span]
            centre = values - jnp.mean(values, axis=1, keepdims=True)
            inverse = lax.rsqrt(jnp.mean(centre * centre, axis=1, keepdims=True) + 1e-06)
            centre = centre * inverse
            normed[span, :] = centre
            inverses[span, :] = inverse
            mlp_in[span, :] = low(centre * scale + shift)

    outs = (
        struct((width, length), jnp.bfloat16),
        struct((width, width), jnp.bfloat16),
        struct((half, width), jnp.float32),
        struct((length, width), jnp.float32),
        struct((length, 1), jnp.float32),
        struct((length, width), jnp.bfloat16),
    )
    return order.run(kernel, outs, *quarters, out_mine, out_near, out_bias, *pieces, mod)


def gate_grad(order, pieces, mod):
    tokens, width = pieces[0].shape

    def kernel(place, *refs):
        mod_ref, out, sums = refs[4:]
        total = jnp.zeros(sums.shape, jnp.float32)
        for index in range(4):
            result = low(mod_ref[5:6, :] * wide(refs[index][...]))
            out[index * tokens : (index + 1) * tokens, :] = result
            if index < 2:
                total = total + jnp.sum(wide(result), axis=0, keepdims=True)
        sums[...] = total

    outs = (struct((4 * tokens, width), jnp.bfloat16), struct((1, width), jnp.float32))
    return order.run(kernel, outs, *pieces, mod)


def feed(order, mlp_in, weight, bias):
    length, width = mlp_in.shape
    hidden = weight.shape[1]
    step = hidden // 3

    def kernel(place, in_ref, weight_ref, bias_ref, act, slope):
        pre_act = dot(in_ref[...], weight_ref[...], 1, 0) + bias_ref[...]
        squared = pre_act * pre_act
        bent = jnp.tanh(GELU_ROOT * pre_act * (1.0 + GELU_CUBE * squared))
        raised = 0.5 + 0.5 * bent
        act[...] = low(pre_act * raised)
        slope[...] = raised + pre_act * (1.0 - bent * bent) * (
            0.5 * GELU_ROOT + (1.5 * GELU_ROOT * GELU_CUBE) * squared
        )

    return order.run(
        kernel,
        (
            struct((length, hidden), jnp.bfloat16),
            struct((length, hidden), jnp.float32),
        ),
        mlp_in, weight, bias,
        grid=(3,),
        in_specs=[
            whole((length, width)),
            column_block((width, hidden), step),
            column_block((1, hidden), step),
        ],
        out_specs=(
            column_block((length, hidden), step),
            column_block((length, hidden), step),
        ),
    )


def feed_back(order, grad_mlp, weight, slope):
    length, width = grad_mlp.shape
    hidden = weight.shape[0]
    step = hidden // 3

    def kernel(place, grad_ref, weight_ref, slope_ref, out, sums):
        result = low(dot(grad_ref[...], weight_ref[...], 1, 1) * slope_ref[...])
        out[...] = result
        sums[...] = jnp.sum(wide(result), axis=0, keepdims=True)

    return order.run(
        kernel,
        (struct((length, hidden), jnp.bfloat16), struct((1, hidden), jnp.float32)),
        grad_mlp, weight, slope,
        grid=(3,),
        in_specs=[
            whole((length, width)),
            row_block((hidden, width), step),
            column_block((length, hidden), step),
        ],
        out_specs=(column_block((length, hidden), step), column_block((1, hidden), step)),
    )


def feed_in_back(order, pre_mine, up_mine, pre_near, up_near):
    length, hidden = pre_mine.shape
    width = up_mine.shape[0]
    step = width // 3

    def kernel(place, pre_mine_ref, up_mine_ref, pre_near_ref, up_near_ref, out):
        out[...] = low(
            dot(pre_mine_ref[...], up_mine_ref[...], 1, 1)
            + dot(pre_near_ref[...], up_near_ref[...], 1, 1)
        )

    return order.run(
        kernel,
        [struct((length, width), jnp.bfloat16)],
        pre_mine, up_mine, pre_near, up_near,
        grid=(3,),
        in_specs=[
            whole((length, hidden)),
            row_block((width, hidden), step),
            whole((length, hidden)),
            row_block((width, hidden), step),
        ],
        out_specs=[column_block((length, width), step)],
    )


def feed_out(order, act_mine, down_mine, act_near, down_near):
    length, hidden = act_mine.shape
    width = down_mine.shape[1]
    half, step = length // 2, width // 3

    def kernel(place, act_mine_ref, down_mine_ref, act_near_ref, down_near_ref, own, give):
        result = dot(act_mine_ref[...], down_mine_ref[...], 1, 0) + dot(
            act_near_ref[...], down_near_ref[...], 1, 0
        )
        own[...] = result[:half]
        give[...] = low(result[half:])

    return order.run(
        kernel,
        (struct((half, width), jnp.float32), struct((half, width), jnp.bfloat16)),
        act_mine, down_mine, act_near, down_near,
        grid=(3,),
        in_specs=[
            whole((length, hidden)),
            column_block((hidden, width), step),
            whole((length, hidden)),
            column_block((hidden, width), step),
        ],
        out_specs=(column_block((half, width), step), column_block((half, width), step)),
    )


def weight_grad(order, shards, left_side, right_side, chunks):
    length, rows = left_side.shape
    columns = right_side.shape[1]

    def kernel(place, left_ref, right_ref, *refs):
        total = low(dot(left_ref[...], right_ref[...], 0, 0))
        give_chunks(total, shards, refs, 0)

    return order.run(kernel, chunks_of(shards, rows, columns, chunks), left_side, right_side)


def chunks_of(shards, rows, columns, chunks):
    return [struct((shards // chunks, rows // shards, columns), jnp.bfloat16)] * chunks


def give_chunks(total, shards, refs, start):
    piece = total.shape[0] // shards
    share = shards // len(refs)
    span = slice(start, start + total.shape[1])
    for shard in range(shards):
        block = total[shard * piece : (shard + 1) * piece]
        refs[shard // share][shard % share, :, span] = block


def attention_grad(order, shards, attn_turned, qkv_grad, heads_out, grad_attn, chunks):
    rows = attn_turned.shape[0]
    columns, part = qkv_grad.shape[1], grad_attn.shape[1] // 4

    def kernel(place, turned_ref, qkv_ref, heads_ref, grad_ref, *refs):
        held = refs[chunks]
        take_quarter(place, grad_ref, held, 1)
        give_chunks(low(dot(turned_ref[...], qkv_ref[...], 1, 0)), shards, refs[:chunks], 0)
        total = low(dot(heads_ref[...], held[...], 1, 0))
        give_chunks(total, shards, refs[:chunks], columns)

    return order.run(
        kernel,
        chunks_of(shards, rows, columns + part, chunks),
        attn_turned,
        qkv_grad,
        heads_out,
        grad_attn,
        scratch=(pltpu.VMEM((grad_attn.shape[0], part), grad_attn.dtype),),
    )


def take_quarter(place, source, target, other):
    columns = target.shape[1]
    for index in range(4):

        @pl.when((place[SEAT] ^ other) == index)
        def _():
            target[...] = source[:, index * columns : (index + 1) * columns]


def add_met(total, shards, met_refs, held, start):
    piece = total.shape[0] // shards
    share = shards // len(met_refs)
    span = slice(start, start + total.shape[1])
    for shard in range(shards):
        part = total[shard * piece : (shard + 1) * piece]
        met = met_refs[shard // share][shard % share, :, span]
        held[shard, :, span] = low(part + wide(met))


def give_blocks(place, shards, held, outs):
    lines = shards // 2
    for back in range(lines):
        line = lax.rem(place[LINE] + (lines - back), lines)
        outs[back][...] = held[2 * line + 1 - place[PAIR]]
        outs[lines + back][...] = held[2 * line + place[PAIR]]


def weight_sum(order, shards, left_side, right_side, met):
    rows, columns = left_side.shape[1], right_side.shape[1]
    piece = rows // shards

    def kernel(place, left_ref, right_ref, *refs):
        met_refs, outs, held = refs[: len(met)], refs[len(met) : -1], refs[-1]
        total = dot(left_ref[...], right_ref[...], 0, 0)
        add_met(total, shards, met_refs, held, 0)
        give_blocks(place, shards, held, outs)

    outs = [struct((piece, columns), jnp.bfloat16)] * shards
    scratch = (pltpu.VMEM((shards, piece, columns), jnp.bfloat16),)
    return order.run(kernel, outs, left_side, right_side, *met, scratch=scratch)


def attention_sum(order, shards, attn_turned, qkv_grad, heads_out, grad_attn, met):
    rows = attn_turned.shape[0]
    piece = rows // shards
    columns, part = qkv_grad.shape[1], grad_attn.shape[1] // 4

    def kernel(place, turned_ref, qkv_ref, heads_ref, grad_ref, *refs):
        met_refs, outs, (quarter, held) = refs[: len(met)], refs[len(met) : -2], refs[-2:]
        take_quarter(place, grad_ref, quarter, 0)
        for left, right, start in ((turned_ref, qkv_ref, 0), (heads_ref, quarter, columns)):
            add_met(dot(left[...], right[...], 1, 0), shards, met_refs, held, start)
        give_blocks(place, shards, held, outs)

    outs = [struct((piece, columns + part), jnp.bfloat16)] * shards
    scratch = (
        pltpu.VMEM((grad_attn.shape[0], part), grad_attn.dtype),
        pltpu.VMEM((shards, piece, columns + part), jnp.bfloat16),
    )
    return order.run(
        kernel, outs, attn_turned, qkv_grad, heads_out, grad_attn, *met, scratch=scratch
    )


def middle_back(order, part, far, normed, inverses, pieces, mod, branch):
    length, width = part.shape
    tokens = length // 4

    def kernel(place, part_ref, far_ref, normed_ref, inverse_ref, *refs):
        mod_ref, branch_ref, grad_attn, grad_middle, sums = refs[4:]
        gate, scale = mod_ref[2:3, :], 1.0 + mod_ref[4:5, :]
        totals = [jnp.zeros((1, width), jnp.float32)] * 4
        for index in range(4):
            span = slice(index * tokens, (index + 1) * tokens)
            other = slice((index ^ 2) * tokens, ((index ^ 2) + 1) * tokens)
            grad_in = wide(part_ref[span, :]) + wide(far_ref[other, :])
            values = normed_ref[span, :]
            grad = wide(refs[index][...]) + normalize_back(
                values, inverse_ref[span, :], grad_in * scale
            )
            result = low(gate * grad)
            grad_attn[span, :] = result
            if index < 2:
                grad_middle[span, :] = grad
                terms = (grad_in, grad_in * values, grad * branch_ref[span, :], wide(result))
                totals = [
                    total + jnp.sum(term, axis=0, keepdims=True)
                    for total, term in zip(totals, terms)
                ]
        for row, total in enumerate(totals):
            sums[row : row + 1, :] = total

    outs = (
        struct((length, width), jnp.bfloat16),
        struct((2 * tokens, width), jnp.float32),
        struct((4, width), jnp.float32),
    )
    return order.run(kernel, outs, part, far, normed, inverses, *pieces, mod, branch)


def attention_in_back(order, grad_mine, qkv_mine, grad_near, qkv_near, pieces, means, inverses):
    length, columns = grad_mine.shape
    width = qkv_mine.shape[0]
    tokens, half, step = length // 4, length // 2, width // 3

    def kernel(place, grad_mine_ref, qkv_mine_ref, grad_near_ref, qkv_near_ref, *refs):
        mean_ref, inverse_ref, own, give, sums = refs[4:]
        result = dot(grad_mine_ref[...], qkv_mine_ref[...], 1, 1) + dot(
            grad_near_ref[...], qkv_near_ref[...], 1, 1
        )
        own[...] = result[:half]
        give[...] = low(result[half:])
        scaled = jnp.zeros((1, step), jnp.float32)
        for index in range(4):
            span = slice(index * tokens, (index + 1) * tokens)
            normed = (wide(refs[index][...]) - mean_ref[span, :]) * inverse_ref[span, :]
            scaled = scaled + jnp.sum(result[span] * normed, axis=0, keepdims=True)
        sums[0:1, :] = jnp.sum(result, axis=0, keepdims=True)
        sums[1:2, :] = scaled

    outs = (
        struct((half, width), jnp.float32),
        struct((half, width), jnp.bfloat16),
        struct((2, width), jnp.float32),
    )
    weights = row_block((width, columns), step)
    grads = whole((length, columns))
    stats = whole((length, 1))
    return order.run(
        kernel,
        outs,
        grad_mine,
        qkv_mine,
        grad_near,
        qkv_near,
        *pieces,
        means,
        inverses,
        grid=(3,),
        in_specs=[grads, weights, grads, weights]
        + [column_block((tokens, width), step)] * 4
        + [stats, stats],
        out_specs=[
            column_block((half, width), step),
            column_block((half, width), step),
            column_block((2, width), step),
        ],
    )


def tokens_back(order, own, far, pieces, means, inverses, mod, grad_middle):
    half, width = own.shape
    tokens = half // 2

    def kernel(
        place, own_ref, far_ref, mine_ref, near_ref, mean_ref, inverse_ref, mod_ref, grad_ref,
        mine, give,
    ):
        for index, (source, target) in enumerate(((mine_ref, mine), (near_ref, give))):
            span = slice(index * tokens, (index + 1) * tokens)
            inverse = inverse_ref[span, :]
            normed = (wide(source[...]) - mean_ref[span, :]) * inverse
            grad = (own_ref[span, :] + wide(far_ref[span, :])) * (1.0 + mod_ref[1:2, :])
            target[...] = grad_ref[span, :] + normalize_back(normed, inverse, grad)

    outs = (struct((tokens, width), jnp.float32),) * 2
    return order.run(
        kernel, outs, own, far, pieces[0], pieces[1], means, inverses, mod, grad_middle
    )


def mix(order, own, far, down_bias, pieces, branch, grads, mod):
    half, width = own.shape
    tokens = half // 2

    def kernel(
        place, own_ref, far_ref, bias_ref, mine_ref, near_ref, branch_ref, grad_mine, grad_near,
        mod_ref, mine, give, sums,
    ):
        total = jnp.zeros((1, width), jnp.float32)
        sources = ((mine_ref, grad_mine, mine), (near_ref, grad_near, give))
        for index, (source, grad, target) in enumerate(sources):
            span = slice(index * tokens, (index + 1) * tokens)
            mlp_branch = own_ref[span, :] + wide(far_ref[span, :]) + bias_ref[...]
            middle = wide(source[...]) + mod_ref[2:3, :] * branch_ref[span, :]
            target[...] = low(middle + mod_ref[5:6, :] * mlp_branch)
            total = total + jnp.sum(wide(grad[...]) * mlp_branch, axis=0, keepdims=True)
        sums[...] = total

    outs = (struct((tokens, width), jnp.bfloat16),) * 2 + (struct((1, width), jnp.float32),)
    return order.run(
        kernel, outs, own, far, down_bias, pieces[0], pieces[1], branch, grads[0], grads[1], mod
    )


def per_device(
    latents,
    condition,
    mod_weight,
    mod_bias,
    qkv_weight,
    qv_bias,
    out_weight,
    out_bias,
    up_weight,
    up_bias,
    down_weight,
    down_bias,
    cotangent,
):
    here = Place()
    order = Order(here.place)
    shards, seat, core = here.shards, here.seat, here.core
    near_seat = seat ^ 1
    micros, tokens, width = latents.shape
    rows = width // shards
    hidden = up_weight.shape[1]
    heads = H // 4
    part = heads * HD
    block = hidden // shards // 4
    wait = order.wait

    hidden_part = shards * block
    attention_widths = (3 * part, width // 2)

    biases = jnp.concatenate([mod_bias, qv_bias, out_bias, up_bias, down_bias]).reshape(1, -1)
    ring = Gather(
        here, order, cut_attention(order, condition, biases, qkv_weight, out_weight), near=True
    )
    lat_mine, lat_give = cut_tokens(order, latents)
    lat_near, lat_far = here.to_core(lat_give), here.to_side(lat_mine)
    cot_mine, cot_give = cut_tokens(order, cotangent)
    cot_near, cot_far = here.to_core(cot_give), here.to_side(cot_mine)
    feed_piece = cut_feed(order, up_weight, down_weight, shards)
    ring.turn()
    lat_near, cot_near = wait(lat_near, cot_near)
    lat_far_near, cot_far_near = here.to_side(lat_near), here.to_side(cot_near)
    lat_far = wait(lat_far)
    ring.turn()
    cot_far, lat_far_near = wait(cot_far, lat_far_near)
    lats = (lat_mine, lat_near, lat_far, lat_far_near)
    ring.turn()
    feed_ring = Gather(here, order, wait(feed_piece), hold=True)
    qkv_mine, out_mine, heads_all = ring.finish(attention_widths, HEAD, True)
    feed_ring.release()
    (
        cond_rows,
        mod_bias,
        qkv_bias_mine,
        qkv_bias_near,
        out_bias,
        up_bias_mine,
        up_bias_near,
        down_bias,
        *mod_parts,
    ) = modulation_parts(order, heads_all, mod_weight, micros, width, hidden)
    mod_sum = LineSum(here, order, mod_parts)
    mod_sum.join()
    mod_parts = mod_sum.finish()
    feed_ring.turn()
    qkv_near, out_near = ring.finish_near(attention_widths, HEAD)
    mod, attn_in, attn_turned, means_one, inverses_one = norm_tokens(
        order, lats, mod_parts, mod_bias
    )
    qkv_mine = qkv_mine.reshape(width, 3 * part)
    parts_mine, heads_mine = attend(order, attn_in, qkv_mine, qkv_bias_mine)
    heads_far = here.to_side(heads_mine)
    qkv_near = qkv_near.reshape(width, 3 * part)
    parts_near, heads_near = attend(order, attn_in, qkv_near, qkv_bias_near)
    heads_far_near = here.to_side(heads_near)
    heads_far = wait(heads_far)
    feed_ring.turn()
    quarters = (heads_mine, heads_near, heads_far, wait(heads_far_near))
    heads_out, out_full, branch, normed_two, inverses_two, mlp_in = attention_out(
        order,
        quarters,
        out_mine.reshape(width, width // 2),
        out_near.reshape(width, width // 2),
        out_bias,
        lats,
        mod,
    )
    cots = (cot_mine, cot_near, cot_far, wait(cot_far_near))
    grad_mlp, down_sums = gate_grad(order, cots, mod)
    feed_ring.turn()
    up_mine, down_mine = feed_ring.finish((hidden_part, width))
    up_near, down_near = here.to_core(up_mine), here.to_core(down_mine)
    up_mine = up_mine.reshape(width, hidden_part)
    down_mine = down_mine.reshape(hidden_part, width)
    act_mine, slope_mine = feed(order, mlp_in, up_mine, up_bias_mine)
    pre_mine, up_sums_mine = feed_back(order, grad_mlp, down_mine, slope_mine)
    up_near = wait(up_near).reshape(width, hidden_part)
    act_near, slope_near = feed(order, mlp_in, up_near, up_bias_near)
    down_near = wait(down_near).reshape(hidden_part, width)
    pre_near, up_sums_near = feed_back(order, grad_mlp, down_near, slope_near)

    mlp_part = feed_in_back(order, pre_mine, up_mine, pre_near, up_near)
    mlp_far = here.to_side(mlp_part)

    def to_core(chunks):
        return [here.to_core(chunk) for chunk in chunks]

    down_met = to_core(weight_grad(order, shards, act_near, grad_mlp, 2))
    up_met = to_core(weight_grad(order, shards, mlp_in, pre_near, 2))
    down_met = wait(*down_met)
    down_sum = Scatter(here, order, weight_sum(order, shards, act_mine, grad_mlp, down_met))
    up_met = wait(*up_met)
    up_sum = Scatter(here, order, weight_sum(order, shards, mlp_in, pre_mine, up_met))
    down_sum.turn()
    feed_own, feed_give = feed_out(order, act_mine, down_mine, act_near, down_near)
    feed_far = here.to_side(feed_give)

    up_sum.turn()
    mlp_far = wait(mlp_far)
    grad_attn, grad_middle, middle_sums = middle_back(
        order, mlp_part, mlp_far, normed_two, inverses_two, cots, mod, branch
    )
    down_sum.turn()
    qkv_grad_near, qv_sums_near = attend_back(order, 1, parts_near, out_full, grad_attn)
    up_sum.turn()
    met = to_core(
        attention_grad(order, shards, attn_turned, qkv_grad_near, heads_out, grad_attn, 8)
    )
    met = wait(*met)
    qkv_grad_mine, qv_sums_mine = attend_back(order, 0, parts_mine, out_full, grad_attn)
    down_sum.turn()
    attention_total = Scatter(
        here,
        order,
        attention_sum(order, shards, attn_turned, qkv_grad_mine, heads_out, grad_attn, met),
    )
    up_sum.turn()
    grad_down = down_sum.finish()
    down_far, down_near = here.to_side(grad_down), here.to_core(grad_down)
    feed_far = wait(feed_far)
    mixed_mine, mixed_give, mix_sums = mix(
        order, feed_own, feed_far, down_bias, lats, branch, cots, mod
    )
    grad_up = up_sum.finish()
    attention_total.turn()
    down_far, down_near = wait(down_far, down_near)
    down_far_near = here.to_core(down_far)
    up_far, up_near = here.to_side(grad_up), here.to_core(grad_up)
    attn_own, attn_give, attn_sums = attention_in_back(
        order, qkv_grad_mine, qkv_mine, qkv_grad_near, qkv_near, lats, means_one, inverses_one
    )
    sums = token_sums(
        order, shards, attn_sums, middle_sums, mix_sums, down_sums, qv_sums_mine, qv_sums_near,
        up_sums_mine, up_sums_near,
    )
    sums_far = here.to_side(sums)
    attention_total.turn()
    sums = add_sums(order, sums, wait(sums_far))
    up_far, up_near, down_far_near = wait(up_far, up_near, down_far_near)
    sums_ring = Lines(here, order, sums)
    grad_down = lay_rows(order, (grad_down, down_near, down_far, down_far_near))
    attention_total.turn()
    sums_ring.join()
    up_far_near = here.to_core(up_far)
    attn_far = here.to_side(wait(attn_give))
    up_far_near = wait(up_far_near)
    grad_up = lay_columns(
        order, (grad_up, up_near, up_far, up_far_near), (hidden_part, shards)
    )
    sums_mine, sums_near = sums_ring.finish()
    sums_mine_far, sums_near_far = here.to_core(sums_mine), here.to_core(sums_near)
    grad_attention = attention_total.finish()
    attention_far = here.to_side(grad_attention)
    attention_near = here.to_core(grad_attention)
    sums_mine_far, sums_near_far = wait(sums_mine_far, sums_near_far)
    mod_all, grad_qv_bias, grad_out_bias, grad_up_bias, grad_down_bias, grad_low = (
        modulation_back(
            order, sums_mine, sums_near, sums_mine_far, sums_near_far, mod_weight, hidden
        )
    )
    low_ring = Lines(here, order, grad_low)
    attn_far = wait(attn_far)
    tokens_mine, tokens_give = tokens_back(
        order, attn_own, attn_far, lats, means_one, inverses_one, mod, grad_middle
    )
    attention_far, attention_near = wait(attention_far, attention_near)
    attention_far_near = here.to_core(attention_far)
    mixed_near, tokens_near = here.to_core(mixed_give), here.to_core(tokens_give)
    low_ring.join()
    attention_far_near = wait(attention_far_near)
    grad_qkv, grad_out = lay_columns(
        order,
        (grad_attention, attention_near, attention_far, attention_far_near),
        (3 * part, 3),
        (width // 4, 1),
    )
    mixed_near, tokens_near = wait(mixed_near, tokens_near)
    mixed, grad_latents = lay_tokens(
        order, (mixed_mine, mixed_near), (tokens_mine, tokens_near)
    )
    grad_condition = condition_back(order, *low_ring.finish(), condition)
    mod_all = wait(mod_all)
    grad_mod_weight = dot(cond_rows, mod_all, 0, 0)
    span = 6 * width // shards
    mod_span = lax.dynamic_slice_in_dim(mod_all, here.shard * span, span, 1)
    grad_mod_bias = jnp.sum(wide(mod_span), axis=0)
    grad_qv_bias, grad_out_bias, grad_up_bias, grad_down_bias = (
        vector.reshape(-1)
        for vector in (grad_qv_bias, grad_out_bias, grad_up_bias, grad_down_bias)
    )

    return (
        mixed,
        grad_latents,
        grad_condition,
        grad_mod_weight,
        grad_mod_bias,
        grad_qkv,
        grad_qv_bias,
        grad_out,
        grad_out_bias,
        grad_up,
        grad_up_bias,
        grad_down,
        grad_down_bias,
    )


def solution(mesh):
    tokens = P("fsdp", "seq", None)
    matrix = P("fsdp", None)
    vector = P("fsdp")
    parameters = (matrix, vector) * 5
    in_specs = (tokens, matrix) + parameters + (tokens,)
    out_specs = (tokens, tokens, matrix) + parameters
    return jax.shard_map(
        per_device, mesh=mesh, in_specs=in_specs, out_specs=out_specs, check_vma=False
    )
```

```python
import jax
import jax.numpy as jnp
from jax import lax
from jax.experimental import pallas as pl
from jax.experimental.pallas import tpu as pltpu
from jax.sharding import PartitionSpec as P

H = 16
HD = 72
GELU_ROOT = (2.0 / 3.141592653589793) ** 0.5
GELU_CUBE = 0.044715
SEAT, CORE, PAIR, LINE = range(4)
HEAD = 16

SCALARS = pl.BlockSpec(memory_space=pltpu.SMEM)
WHOLE = pl.BlockSpec(memory_space=pltpu.VMEM)
ANY = pl.BlockSpec(memory_space=pl.ANY)
ROOM = pltpu.CompilerParams(vmem_limit_bytes=14 << 20)
SHORT = pl.CostEstimate(flops=1, transcendentals=0, bytes_accessed=1)


def low(values):
    return values.astype(jnp.bfloat16)


def wide(values):
    return values.astype(jnp.float32)


def struct(shape, dtype):
    return jax.ShapeDtypeStruct(shape, dtype)


def whole(shape):
    return pl.BlockSpec(shape, lambda step: (0,) * len(shape))


def column_block(shape, columns):
    return pl.BlockSpec(shape[:-1] + (columns,), lambda step: (0,) * (len(shape) - 1) + (step,))


def row_block(shape, rows):
    return pl.BlockSpec((rows,) + shape[1:], lambda step: (step,) + (0,) * (len(shape) - 1))


def dot(left_side, right_side, left_dim, right_dim):
    return lax.dot_general(
        left_side,
        right_side,
        (((left_dim,), (right_dim,)), ((), ())),
        preferred_element_type=jnp.float32,
    )


def normalize_back(normed, inverse, grad):
    inner = jnp.mean(grad * normed, axis=-1, keepdims=True)
    return (grad - jnp.mean(grad, axis=-1, keepdims=True) - normed * inner) * inverse


def soft_columns(queries, keys):
    scores = dot(keys, queries, 0, 0) * HD ** (-0.5)
    raised = jnp.exp(scores - jnp.max(scores, axis=0, keepdims=True))
    return raised * (1.0 / jnp.sum(raised, axis=0, keepdims=True))


def pick(values, index, axis):
    return lax.dynamic_index_in_dim(values, index, axis, keepdims=False)


class Order:
    def __init__(self, place):
        self.place = place
        self.token = jnp.zeros((8, 128), jnp.float32)

    def wait(self, *values):
        self.token, values = lax.optimization_barrier((self.token, values))
        return values if len(values) > 1 else values[0]

    def run(self, kernel, outs, *args, grid=(), in_specs=None, out_specs=None, scratch=()):
        count, given = len(outs), len(args)

        def body(place, *refs):
            kernel(place, *refs[:given], *refs[given + 1 : given + 1 + count], *refs[given + 2 + count :])

        results = pl.pallas_call(
            body,
            out_shape=tuple(outs) + (struct(self.token.shape, self.token.dtype),),
            grid=grid,
            in_specs=[SCALARS] + list(in_specs or [WHOLE] * given) + [ANY],
            out_specs=tuple(out_specs or [WHOLE] * count) + (ANY,),
            scratch_shapes=scratch,
            input_output_aliases={given + 1: count},
            compiler_params=ROOM,
            cost_estimate=SHORT,
        )(self.place, *args, self.token)
        self.token = results[-1]
        return results[:-1] if count > 1 else results[0]


class Place:
    def __init__(self):
        self.shards = lax.axis_size("fsdp")
        self.seats = lax.axis_size("seq")
        self.line_size = self.shards // 2
        self.shard = lax.axis_index("fsdp")
        self.seat = lax.axis_index("seq")
        self.core = self.seat % 2
        places = [self.seat, self.core, self.shard % 2, self.shard // 2]
        self.place = jnp.stack(places).astype(jnp.int32)

    def to_core(self, values):
        return lax.ppermute(values, "seq", [(i, i ^ 1) for i in range(self.seats)])

    def to_side(self, values):
        return lax.ppermute(values, "seq", [(i, i ^ 2) for i in range(self.seats)])

    def to_pair(self, values):
        return lax.ppermute(values, "fsdp", [(i, i ^ 1) for i in range(self.shards)])

    def to_line(self, values, step=1):
        return lax.ppermute(
            values, "fsdp", [(i, (i + 2 * step) % self.shards) for i in range(self.shards)]
        )


def piece_shard(place, index, shards):
    lines = shards // 2
    near = index > 0 and (index % 2 == 0 or index == shards - 1)
    back = (index - 1) // 2 if near else (index + 1) // 2
    line = lax.rem(place[LINE] + (lines - back), lines)
    return 2 * line + (1 - place[PAIR] if near else place[PAIR])


class Gather:
    def __init__(self, here, order, piece, near=False, hold=False):
        self.here, self.order, self.near = here, order, near
        self.pieces, self.copies = [], []
        self.steps, self.pending = 0, []
        self.send([piece], hold)

    def send(self, pieces, hold=False):
        here = self.here
        self.pieces += pieces
        sent = []
        if self.steps < here.line_size:
            if self.steps + 1 < here.line_size:
                sent.append(here.to_line(pieces[0]))
            if not hold:
                sent.append(here.to_pair(pieces[0]))
        self.steps += 1
        self.copied = [here.to_core(piece) for piece in pieces] if self.near else []
        self.pending = sent

    def release(self):
        self.pending.append(self.here.to_pair(self.order.wait(self.pieces[0])))

    def turn(self):
        if self.pending:
            arrived = self.order.wait(*self.pending, *self.copied)
            arrived = list(arrived) if len(self.pending) + len(self.copied) > 1 else [arrived]
            count = len(self.pending)
            self.copies += arrived[count:]
            self.send(arrived[:count])

    def finish(self, widths, keep_rest=False):
        while self.pending:
            self.turn()
        return self.place(self.pieces, widths, keep_rest)

    def finish_near(self, widths):
        return self.place(self.copies + [self.order.wait(*self.copied)], widths, False)

    def place(self, pieces, widths, keep_rest):
        shards = self.here.shards
        rows, total = pieces[0].shape

        def kernel(place, *refs):
            targets = refs[shards:]
            for index in range(shards):
                shard = piece_shard(place, index, shards)
                start = 0
                for target, columns in zip(targets, widths):
                    target[shard] = refs[index][:, start : start + columns]
                    start += columns
                if keep_rest:
                    targets[-1][shard] = refs[index][:, start:]

        outs = [struct((shards, rows, columns), pieces[0].dtype) for columns in widths]
        if keep_rest:
            outs.append(struct((shards, rows, total - sum(widths)), pieces[0].dtype))
        return self.order.run(kernel, outs, *pieces)


class Lines:
    def __init__(self, here, order, piece):
        self.here, self.order = here, order
        self.pieces = [piece] + [here.to_line(piece, step) for step in range(1, here.line_size)]

    def join(self):
        count = len(self.pieces)
        self.pieces[1:] = self.order.wait(*self.pieces[1:])

        def kernel(place, *refs):
            for index in range(count):
                refs[-1][index] = refs[index][...]

        shape = struct((count,) + self.pieces[0].shape, self.pieces[0].dtype)
        self.mine = self.order.run(kernel, [shape], *self.pieces)
        self.got = self.here.to_pair(self.mine)

    def finish(self):
        return self.mine, self.order.wait(self.got)


class LineSum:
    def __init__(self, here, order, parts):
        self.here, self.order = here, order
        self.parts = [parts[0]]
        self.parts += [here.to_line(parts[step], step) for step in range(1, here.line_size)]

    def join(self):
        count = len(self.parts)
        self.parts[1:] = self.order.wait(*self.parts[1:])

        def kernel(place, *refs):
            give, mine = refs[count:]
            total = refs[0][...]
            for index in range(1, count):
                total = total + refs[index][...]
            give[...] = total[0:1]
            mine[...] = total[1:2]

        row = struct((1, self.parts[0].shape[1]), self.parts[0].dtype)
        give, self.mine = self.order.run(kernel, [row, row], *self.parts)
        self.got = self.here.to_pair(give)

    def finish(self):
        return self.order.wait(self.got), self.mine


class Scatter:
    def __init__(self, here, order, blocks):
        count = here.line_size
        self.here, self.order, self.step = here, order, 0
        self.give, self.mine = blocks[:count], blocks[count:]
        self.under_way = [here.to_pair(self.give[1 % count])]

    def turn(self):
        here, count = self.here, self.here.line_size
        arrived = self.order.wait(*self.under_way)
        arrived = list(arrived) if len(self.under_way) > 1 else [arrived]
        self.step += 1
        own = self.mine[self.step % count]

        def kernel(place, *refs):
            total = wide(refs[0][...])
            for ref in refs[1:-1]:
                total = total + wide(ref[...])
            refs[-1][...] = low(total)

        total = self.order.run(kernel, [struct(own.shape, jnp.bfloat16)], own, *arrived)
        if self.step < count:
            back = (self.step + 1) % count
            self.under_way = [here.to_line(total), here.to_pair(self.give[back])]
        return total

    def finish(self):
        while self.step < self.here.line_size:
            total = self.turn()
        return total


def cut_columns(place, source, target, offset, index, parts, groups):
    part = source.shape[1] // groups // parts
    for choice in range(parts):

        @pl.when(index == choice)
        def _():
            for group in range(groups):
                start = (group * parts + choice) * part
                goal = offset + group * part
                target[:, goal : goal + part] = source[:, start : start + part]


def cut_attention(order, condition, biases, qkv_weight, out_weight):
    rows, width = out_weight.shape
    columns = qkv_weight.shape[1] // 4
    total = columns + width // 2
    lanes = -total % 128
    micros = condition.shape[0]

    def kernel(place, condition_ref, biases_ref, qkv_ref, out_ref, target, held):
        held[...] = jnp.zeros(held.shape, jnp.float32)
        row = 0
        for source, index in [(condition_ref, micro) for micro in range(micros)] + [(biases_ref, 0)]:
            size = source.shape[1]
            for start in range(0, size, lanes):
                count = min(lanes, size - start)
                held[row : row + 1, :count] = wide(source[index : index + 1, start : start + count])
                row += 1
        target[:, total:] = low(held[...])
        cut_columns(place, qkv_ref, target, 0, place[SEAT], 4, 3)
        cut_columns(place, out_ref, target, columns, place[CORE], 2, 1)

    return order.run(
        kernel,
        [struct((rows, total + lanes), qkv_weight.dtype)],
        condition,
        biases,
        qkv_weight,
        out_weight,
        scratch=(pltpu.VMEM((rows, lanes), jnp.float32),),
    )


def modulation_parts(order, heads, mod_weight, micros, width, hidden):
    shards, _, lanes = heads.shape
    rows, columns = mod_weight.shape
    share_rows = width // lanes
    part = H // 4 * HD
    block = hidden // shards // 4
    sizes = {"mod": columns, "qv": 2 * width, "out": width, "up": hidden, "down": width}

    def kernel(place, heads_ref, weight_ref, *refs):
        cond_rows, mod_bias, qkv_mine, qkv_near, out_bias, up_mine, up_near, down_bias = refs[:8]
        parts, (cond, mine, products) = refs[8:-3], refs[-3:]
        shard = 2 * place[LINE] + place[PAIR]
        for index in range(shards):
            for micro in range(micros):
                goal = index * micros + micro
                for part_row in range(share_rows):
                    source = micro * share_rows + part_row
                    cond[goal : goal + 1, part_row * lanes : (part_row + 1) * lanes] = wide(
                        heads_ref[index, source : source + 1, :]
                    )
        values = cond[...]
        cond[...] = wide(low(values / (1.0 + jnp.exp(-values))))
        for index in range(shards):

            @pl.when(shard == index)
            def _():
                mine[...] = low(cond[:, index * rows : (index + 1) * rows])

        cond_rows[...] = mine[...]
        products[...] = dot(mine[...], weight_ref[...], 1, 0)
        for step, target in enumerate(parts):
            line = lax.rem(place[LINE] + step, shards // 2)
            for row, pair in enumerate((1 - place[PAIR], place[PAIR])):
                source = (2 * line + pair) * micros + place[CORE]
                target[row : row + 1, :] = products[pl.ds(source, 1), :]

        def copy(target, row, column, name, start, count):
            base = 0
            for other, size in sizes.items():
                if other == name:
                    break
                base += size // shards
            share = sizes[name] // shards
            while count > 0:
                index, offset = divmod(start, share)
                line, lane = divmod(base + offset, lanes)
                line += micros * share_rows
                length = min(count, share - offset, lanes - lane)
                source = heads_ref[index, line : line + 1, lane : lane + length]
                target[row : row + 1, column : column + length] = wide(source)
                start, column, count = start + length, column + length, count - length

        for row in range(6):
            copy(mod_bias, row, 0, "mod", row * width, width)
        copy(out_bias, 0, 0, "out", 0, width)
        copy(down_bias, 0, 0, "down", 0, width)
        for own in range(4):

            @pl.when(place[SEAT] == own)
            def _():
                for seat, qkv, up in ((own, qkv_mine, up_mine), (own ^ 1, qkv_near, up_near)):
                    copy(qkv, 0, 0, "qv", seat * part, part)
                    qkv[:, part : 2 * part] = jnp.zeros((1, part), jnp.float32)
                    copy(qkv, 0, 2 * part, "qv", width + seat * part, part)
                    for index in range(shards):
                        start = (index * 4 + seat) * block
                        copy(up, 0, index * block, "up", start, block)

    row = lambda count: struct((1, count), jnp.float32)
    outs = [
        struct((shards * micros, rows), jnp.bfloat16),
        struct((6, width), jnp.float32),
        row(3 * part),
        row(3 * part),
        row(width),
        row(shards * block),
        row(shards * block),
        row(width),
    ] + [struct((2, columns), jnp.float32)] * (shards // 2)
    scratch = (
        pltpu.VMEM((shards * micros, width), jnp.float32),
        pltpu.VMEM((shards * micros, rows), jnp.bfloat16),
        pltpu.VMEM((shards * micros, columns), jnp.float32),
    )
    return order.run(kernel, outs, heads, mod_weight, scratch=scratch)


def token_sums(order, shards, attn, middle, mixed, down, qv_mine, qv_near, up_mine, up_near):
    width = attn.shape[1]
    part = qv_mine.shape[1] // 3
    hidden = 4 * up_mine.shape[1]
    block = hidden // shards // 4
    sizes = (2 * width // shards, width // shards, hidden // shards, width // shards)
    starts = [sum(sizes[:index]) for index in range(4)]

    def kernel(
        place, attn_ref, middle_ref, mixed_ref, down_ref, qv_mine_ref, qv_near_ref, up_mine_ref,
        up_near_ref, out,
    ):
        out[0:2, :] = attn_ref[...]
        out[2:3, :] = middle_ref[2:3, :]
        out[3:5, :] = middle_ref[0:2, :]
        out[5:6, :] = mixed_ref[...]
        out[6:, :] = jnp.zeros((out.shape[0] - 6, width), jnp.float32)

        def copy(source, row, column, which, start, count):
            while count > 0:
                index, offset = divmod(start, sizes[which])
                line, goal = divmod(index * sum(sizes) + starts[which] + offset, width)
                length = min(count, sizes[which] - offset, width - goal)
                out[6 + line : 7 + line, goal : goal + length] = source[
                    row : row + 1, column : column + length
                ]
                start, column, count = start + length, column + length, count - length

        copy(middle_ref, 3, 0, 1, 0, width)
        copy(down_ref, 0, 0, 3, 0, width)
        for own in range(4):

            @pl.when(place[SEAT] == own)
            def _():
                for seat, qv, up in (
                    (own, qv_mine_ref, up_mine_ref),
                    (own ^ 1, qv_near_ref, up_near_ref),
                ):
                    copy(qv, 0, 0, 0, seat * part, part)
                    copy(qv, 0, 2 * part, 0, width + seat * part, part)
                    for index in range(shards):
                        start = (index * 4 + seat) * block
                        copy(up, 0, index * block, 2, start, block)

    outs = [struct((6 + sum(sizes) * shards // width, width), jnp.float32)]
    return order.run(
        kernel, outs, attn, middle, mixed, down, qv_mine, qv_near, up_mine, up_near
    )


def add_sums(order, sums, far):
    rows, width = sums.shape

    def kernel(place, sums_ref, far_ref, out, held):
        held[...] = jnp.zeros(held.shape, jnp.float32)
        held[:rows, :] = sums_ref[...] + far_ref[...]
        out[...] = low(held[...])

    return order.run(
        kernel,
        [struct((HEAD, width), jnp.bfloat16)],
        sums,
        far,
        scratch=(pltpu.VMEM((HEAD, width), jnp.float32),),
    )


def modulation_back(order, mine, near, mine_far, near_far, mod_weight, hidden):
    lines, _, width = mine.shape
    shards = 2 * lines
    rows, columns = mod_weight.shape
    sizes = (2 * width // shards, width // shards, hidden // shards, width // shards)

    def kernel(place, weight_ref, mine_ref, near_ref, mine_far_ref, near_far_ref, *refs):
        mod_all, biases, (products, held, total) = refs[0], refs[1:5], refs[5:]
        shard = 2 * place[LINE] + place[PAIR]
        total[...] = jnp.zeros(total.shape, jnp.float32)
        sources = (
            (mine_ref, place[PAIR], place[CORE]),
            (near_ref, 1 - place[PAIR], place[CORE]),
            (mine_far_ref, place[PAIR], 1 - place[CORE]),
            (near_far_ref, 1 - place[PAIR], 1 - place[CORE]),
        )
        for back in range(lines):
            line = lax.rem(place[LINE] + (lines - back), lines)
            for source_ref, pair, core in sources:
                source = wide(source_ref[back])
                goal = 2 * (2 * line + pair) + core
                for row in range(6):
                    span = slice(row * width, (row + 1) * width)
                    held[pl.ds(goal, 1), span] = source[row : row + 1, :]
        for core in range(2):
            for back in range(lines):
                for source_ref in (mine_ref, near_ref, mine_far_ref, near_far_ref)[
                    2 * core : 2 * core + 2
                ]:
                    total[...] += wide(source_ref[back])[6 : 6 + total.shape[0], :]
        for index in range(shards):

            @pl.when(shard == index)
            def _():
                line, start = divmod(index * sum(sizes), width)
                for target, size in zip(biases, sizes):
                    target[...] = total[line : line + 1, start : start + size]
                    start += size

        mod_all[...] = low(held[...])
        products[...] = dot(mod_all[...], weight_ref[...], 1, 1)

    outs = [struct((2 * shards, columns), jnp.bfloat16)]
    outs += [struct((1, size), jnp.float32) for size in sizes]
    outs.append(struct((2 * shards, rows), jnp.float32))
    scratch = (
        pltpu.VMEM((2 * shards, columns), jnp.float32),
        pltpu.VMEM((sum(sizes) * shards // width, width), jnp.float32),
    )
    return order.run(
        kernel, outs, mod_weight, mine, near, mine_far, near_far, scratch=scratch
    )


def condition_back(order, mine, near, condition):
    micros, width = condition.shape
    lines, _, rows = mine.shape

    def kernel(place, condition_ref, mine_ref, near_ref, out, held):
        shard = 2 * place[LINE] + place[PAIR]
        for index in range(2 * lines):
            source = near_ref if index % 2 else mine_ref
            line = lax.rem(place[LINE] + (lines - index // 2), lines)
            owner = 2 * line + (1 - place[PAIR] if index % 2 else place[PAIR])
            for latent in range(micros):
                row = source[index // 2, pl.ds(micros * shard + latent, 1), :]
                held[owner, latent : latent + 1, :] = row
        values = wide(condition_ref[...])
        sigma = 1.0 / (1.0 + jnp.exp(-values))
        slope = sigma * (1.0 + values * (1.0 - sigma))
        for index in range(2 * lines):
            span = slice(index * rows, (index + 1) * rows)
            out[:, span] = held[index] * slope[:, span]

    outs = [struct(condition.shape, jnp.float32)]
    scratch = (pltpu.VMEM((2 * lines, micros, rows), jnp.float32),)
    return order.run(kernel, outs, condition, mine, near, scratch=scratch)


def cut_feed(order, up_weight, down_weight, shards):
    hidden, width = down_weight.shape
    rows, columns = up_weight.shape

    def kernel(place, up_ref, down_ref, target):
        cut_columns(place, up_ref, target, 0, place[SEAT], 4, shards)
        target[:, columns // 4 :] = down_ref[place[SEAT]]

    shape = struct((rows, columns // 4 + width), up_weight.dtype)
    return order.run(
        kernel, [shape], up_weight, down_weight.reshape(4, hidden // 4, width)
    )


def cut_tokens(order, tokens):
    shape = struct(tokens.shape[1:], tokens.dtype)

    def kernel(place, source, mine, give):
        mine[...] = source[place[CORE]]
        give[...] = source[1 - place[CORE]]

    return order.run(kernel, [shape, shape], tokens)


def lay_columns(order, quarters, *parts):
    rows = quarters[0].shape[0]

    def kernel(place, *refs):
        for own in range(4):

            @pl.when(place[SEAT] == own)
            def _():
                offset = 0
                for target, (columns, groups) in zip(refs[4:], parts):
                    part = columns // groups
                    for group in range(groups):
                        for other in range(4):
                            start = (group * 4 + (own ^ other)) * part
                            block = refs[other][:, offset : offset + part]
                            target[:, start : start + part] = wide(block)
                        offset += part

    outs = [struct((rows, 4 * columns), jnp.float32) for columns, groups in parts]
    return order.run(kernel, outs, *quarters)


def lay_rows(order, quarters):
    rows, columns = quarters[0].shape

    def kernel(place, *refs):
        for other in range(4):
            refs[4][place[SEAT] ^ other] = wide(refs[other][...])

    result = order.run(kernel, [struct((4, rows, columns), jnp.float32)], *quarters)
    return result.reshape(4 * rows, columns)


def lay_tokens(order, *pairs):
    def kernel(place, *refs):
        for index in range(len(pairs)):
            target = refs[2 * len(pairs) + index]
            target[place[CORE]] = refs[2 * index][...]
            target[1 - place[CORE]] = refs[2 * index + 1][...]

    outs = [struct((2,) + mine.shape, mine.dtype) for mine, near in pairs]
    return order.run(kernel, outs, *(value for values in pairs for value in values))


def norm_tokens(order, pieces, parts, mod_bias):
    tokens, width = pieces[0].shape
    length = 4 * tokens

    def kernel(place, *refs):
        sources, refs = refs[: len(parts)], refs[len(parts) :]
        bias_ref, (mod, out, turned, means, inverses) = refs[0], refs[5:]
        for row in range(6):
            span = slice(row * width, (row + 1) * width)
            total = bias_ref[row : row + 1, :]
            for source in sources:
                total = total + source[:, span]
            mod[row : row + 1, :] = total
        for index in range(4):
            span = slice(index * tokens, (index + 1) * tokens)
            values = wide(refs[1 + index][...])
            mean = jnp.mean(values, axis=1, keepdims=True)
            centre = values - mean
            inverse = lax.rsqrt(jnp.mean(centre * centre, axis=1, keepdims=True) + 1e-06)
            result = centre * inverse * (1.0 + mod[1:2, :]) + mod[0:1, :]
            out[span, :] = low(result)
            turned[:, span] = low(result.T)
            means[span, :] = mean
            inverses[span, :] = inverse

    outs = (
        struct((6, width), jnp.float32),
        struct((length, width), jnp.bfloat16),
        struct((width, length), jnp.bfloat16),
        struct((length, 1), jnp.float32),
        struct((length, 1), jnp.float32),
    )
    return order.run(kernel, outs, *parts, mod_bias, *pieces)


def attend(order, attn_in, weight, bias):
    length = attn_in.shape[0]
    heads = H // 4

    def kernel(place, in_ref, weight_ref, bias_ref, parts, result):
        values = (dot(in_ref[...], weight_ref[...], 1, 0) + bias_ref[...]).T
        for index in range(3 * heads):
            parts[index] = low(values[index * HD : (index + 1) * HD])
        results = []
        for head in range(heads):
            probs = soft_columns(parts[head], parts[heads + head])
            results.append(dot(parts[2 * heads + head], low(probs), 1, 0))
        result[...] = low(jnp.concatenate(results, axis=0))

    outs = (
        struct((3 * heads, HD, length), jnp.bfloat16),
        struct((heads * HD, length), jnp.bfloat16),
    )
    return order.run(kernel, outs, attn_in, weight, bias)


def attend_back(order, other, parts, out_weight, grad_attn):
    length = grad_attn.shape[0]
    heads = H // 4
    part = heads * HD
    factor = HD ** (-0.5)

    def kernel(place, parts_ref, weight_ref, grad_ref, out, sums):
        rows = pl.ds(pl.multiple_of((place[SEAT] ^ other) * part, part), part)
        grad_heads = dot(weight_ref[rows, :], grad_ref[...], 1, 1)
        grads = [None] * (3 * heads)
        for head in range(heads):
            queries, keys = parts_ref[head], parts_ref[heads + head]
            contents = parts_ref[2 * heads + head]
            grad = low(grad_heads[head * HD : (head + 1) * HD])
            probs = soft_columns(queries, keys)
            grad_probs = dot(contents, grad, 0, 0)
            inner = jnp.sum(probs * grad_probs, axis=0, keepdims=True)
            grad_scores = low(probs * (grad_probs - inner))
            grads[head] = factor * dot(keys, grad_scores, 1, 0)
            grads[heads + head] = factor * dot(queries, grad_scores, 1, 1)
            grads[2 * heads + head] = dot(grad, low(probs), 1, 1)
        result = low(jnp.concatenate(grads, axis=0).T)
        out[...] = result
        sums[...] = jnp.sum(wide(result), axis=0, keepdims=True)

    outs = (
        struct((length, 3 * part), jnp.bfloat16),
        struct((1, 3 * part), jnp.float32),
    )
    return order.run(kernel, outs, parts, out_weight, grad_attn)


def attention_out(order, quarters, out_mine, out_near, out_bias, pieces, mod):
    tokens, width = pieces[0].shape
    half, length = 2 * tokens, 4 * tokens
    part = quarters[0].shape[0]
    columns = width // 2

    def kernel(place, *refs):
        out_mine_ref, out_near_ref, bias_ref = refs[4:7]
        mod_ref, heads, weight, branch, normed, inverses, mlp_in = refs[11:]
        for other in range(4):
            rows = pl.ds(pl.multiple_of((place[SEAT] ^ other) * part, part), part)
            if other < 2:
                heads[rows, :] = refs[other][...]
            else:
                heads[rows, :half] = refs[other][:, half:]
                heads[rows, half:] = refs[other][:, :half]
        for own in range(2):

            @pl.when(place[CORE] == own)
            def _():
                weight[:, own * columns : (own + 1) * columns] = out_mine_ref[...]
                weight[:, (1 - own) * columns : (2 - own) * columns] = out_near_ref[...]

        result = dot(heads[...], weight[...], 0, 0) + bias_ref[...]
        branch[...] = result[:half]
        shift, scale = mod_ref[3:4, :], 1.0 + mod_ref[4:5, :]
        for index in range(4):
            span = slice(index * tokens, (index + 1) * tokens)
            values = wide(refs[7 + index][...]) + mod_ref[2:3, :] * result[span]
            centre = values - jnp.mean(values, axis=1, keepdims=True)
            inverse = lax.rsqrt(jnp.mean(centre * centre, axis=1, keepdims=True) + 1e-06)
            centre = centre * inverse
            normed[span, :] = centre
            inverses[span, :] = inverse
            mlp_in[span, :] = low(centre * scale + shift)

    outs = (
        struct((width, length), jnp.bfloat16),
        struct((width, width), jnp.bfloat16),
        struct((half, width), jnp.float32),
        struct((length, width), jnp.float32),
        struct((length, 1), jnp.float32),
        struct((length, width), jnp.bfloat16),
    )
    return order.run(kernel, outs, *quarters, out_mine, out_near, out_bias, *pieces, mod)


def gate_grad(order, pieces, mod):
    tokens, width = pieces[0].shape

    def kernel(place, *refs):
        mod_ref, out, sums = refs[4:]
        total = jnp.zeros(sums.shape, jnp.float32)
        for index in range(4):
            result = low(mod_ref[5:6, :] * wide(refs[index][...]))
            out[index * tokens : (index + 1) * tokens, :] = result
            if index < 2:
                total = total + jnp.sum(wide(result), axis=0, keepdims=True)
        sums[...] = total

    outs = (struct((4 * tokens, width), jnp.bfloat16), struct((1, width), jnp.float32))
    return order.run(kernel, outs, *pieces, mod)


def feed(order, mlp_in, weight, bias):
    length, width = mlp_in.shape
    hidden = weight.shape[1]
    step = hidden // 3

    def kernel(place, in_ref, weight_ref, bias_ref, act, slope):
        pre_act = dot(in_ref[...], weight_ref[...], 1, 0) + bias_ref[...]
        squared = pre_act * pre_act
        bent = jnp.tanh(GELU_ROOT * pre_act * (1.0 + GELU_CUBE * squared))
        raised = 0.5 + 0.5 * bent
        act[...] = low(pre_act * raised)
        slope[...] = raised + pre_act * (1.0 - bent * bent) * (
            0.5 * GELU_ROOT + (1.5 * GELU_ROOT * GELU_CUBE) * squared
        )

    return order.run(
        kernel,
        (
            struct((length, hidden), jnp.bfloat16),
            struct((length, hidden), jnp.float32),
        ),
        mlp_in, weight, bias,
        grid=(3,),
        in_specs=[
            whole((length, width)),
            column_block((width, hidden), step),
            column_block((1, hidden), step),
        ],
        out_specs=(
            column_block((length, hidden), step),
            column_block((length, hidden), step),
        ),
    )


def feed_back(order, grad_mlp, weight, slope):
    length, width = grad_mlp.shape
    hidden = weight.shape[0]
    step = hidden // 3

    def kernel(place, grad_ref, weight_ref, slope_ref, out, sums):
        result = low(dot(grad_ref[...], weight_ref[...], 1, 1) * slope_ref[...])
        out[...] = result
        sums[...] = jnp.sum(wide(result), axis=0, keepdims=True)

    return order.run(
        kernel,
        (struct((length, hidden), jnp.bfloat16), struct((1, hidden), jnp.float32)),
        grad_mlp, weight, slope,
        grid=(3,),
        in_specs=[
            whole((length, width)),
            row_block((hidden, width), step),
            column_block((length, hidden), step),
        ],
        out_specs=(column_block((length, hidden), step), column_block((1, hidden), step)),
    )


def feed_in_back(order, pre_mine, up_mine, pre_near, up_near):
    length, hidden = pre_mine.shape
    width = up_mine.shape[0]
    step = width // 3

    def kernel(place, pre_mine_ref, up_mine_ref, pre_near_ref, up_near_ref, out):
        out[...] = low(
            dot(pre_mine_ref[...], up_mine_ref[...], 1, 1)
            + dot(pre_near_ref[...], up_near_ref[...], 1, 1)
        )

    return order.run(
        kernel,
        [struct((length, width), jnp.bfloat16)],
        pre_mine, up_mine, pre_near, up_near,
        grid=(3,),
        in_specs=[
            whole((length, hidden)),
            row_block((width, hidden), step),
            whole((length, hidden)),
            row_block((width, hidden), step),
        ],
        out_specs=[column_block((length, width), step)],
    )


def feed_out(order, act_mine, down_mine, act_near, down_near):
    length, hidden = act_mine.shape
    width = down_mine.shape[1]
    half, step = length // 2, width // 3

    def kernel(place, act_mine_ref, down_mine_ref, act_near_ref, down_near_ref, own, give):
        result = dot(act_mine_ref[...], down_mine_ref[...], 1, 0) + dot(
            act_near_ref[...], down_near_ref[...], 1, 0
        )
        own[...] = result[:half]
        give[...] = low(result[half:])

    return order.run(
        kernel,
        (struct((half, width), jnp.float32), struct((half, width), jnp.bfloat16)),
        act_mine, down_mine, act_near, down_near,
        grid=(3,),
        in_specs=[
            whole((length, hidden)),
            column_block((hidden, width), step),
            whole((length, hidden)),
            column_block((hidden, width), step),
        ],
        out_specs=(column_block((half, width), step), column_block((half, width), step)),
    )


def weight_grad(order, shards, left_side, right_side, chunks):
    length, rows = left_side.shape
    columns = right_side.shape[1]

    def kernel(place, left_ref, right_ref, *refs):
        total = low(dot(left_ref[...], right_ref[...], 0, 0))
        give_chunks(total, shards, refs, 0)

    return order.run(kernel, chunks_of(shards, rows, columns, chunks), left_side, right_side)


def chunks_of(shards, rows, columns, chunks):
    return [struct((shards // chunks, rows // shards, columns), jnp.bfloat16)] * chunks


def give_chunks(total, shards, refs, start):
    piece = total.shape[0] // shards
    share = shards // len(refs)
    span = slice(start, start + total.shape[1])
    for shard in range(shards):
        block = total[shard * piece : (shard + 1) * piece]
        refs[shard // share][shard % share, :, span] = block


def attention_grad(order, shards, attn_turned, qkv_grad, heads_out, grad_attn, chunks):
    rows = attn_turned.shape[0]
    columns, part = qkv_grad.shape[1], grad_attn.shape[1] // 4

    def kernel(place, turned_ref, qkv_ref, heads_ref, grad_ref, *refs):
        held = refs[chunks]
        take_quarter(place, grad_ref, held, 1)
        give_chunks(low(dot(turned_ref[...], qkv_ref[...], 1, 0)), shards, refs[:chunks], 0)
        total = low(dot(heads_ref[...], held[...], 1, 0))
        give_chunks(total, shards, refs[:chunks], columns)

    return order.run(
        kernel,
        chunks_of(shards, rows, columns + part, chunks),
        attn_turned,
        qkv_grad,
        heads_out,
        grad_attn,
        scratch=(pltpu.VMEM((grad_attn.shape[0], part), grad_attn.dtype),),
    )


def take_quarter(place, source, target, other):
    columns = target.shape[1]
    for index in range(4):

        @pl.when((place[SEAT] ^ other) == index)
        def _():
            target[...] = source[:, index * columns : (index + 1) * columns]


def add_met(total, shards, met_refs, held, start):
    piece = total.shape[0] // shards
    share = shards // len(met_refs)
    span = slice(start, start + total.shape[1])
    for shard in range(shards):
        part = total[shard * piece : (shard + 1) * piece]
        met = met_refs[shard // share][shard % share, :, span]
        held[shard, :, span] = low(part + wide(met))


def give_blocks(place, shards, held, outs):
    lines = shards // 2
    for back in range(lines):
        line = lax.rem(place[LINE] + (lines - back), lines)
        outs[back][...] = held[2 * line + 1 - place[PAIR]]
        outs[lines + back][...] = held[2 * line + place[PAIR]]


def weight_sum(order, shards, left_side, right_side, met):
    rows, columns = left_side.shape[1], right_side.shape[1]
    piece = rows // shards

    def kernel(place, left_ref, right_ref, *refs):
        met_refs, outs, held = refs[: len(met)], refs[len(met) : -1], refs[-1]
        total = dot(left_ref[...], right_ref[...], 0, 0)
        add_met(total, shards, met_refs, held, 0)
        give_blocks(place, shards, held, outs)

    outs = [struct((piece, columns), jnp.bfloat16)] * shards
    scratch = (pltpu.VMEM((shards, piece, columns), jnp.bfloat16),)
    return order.run(kernel, outs, left_side, right_side, *met, scratch=scratch)


def attention_sum(order, shards, attn_turned, qkv_grad, heads_out, grad_attn, met):
    rows = attn_turned.shape[0]
    piece = rows // shards
    columns, part = qkv_grad.shape[1], grad_attn.shape[1] // 4

    def kernel(place, turned_ref, qkv_ref, heads_ref, grad_ref, *refs):
        met_refs, outs, (quarter, held) = refs[: len(met)], refs[len(met) : -2], refs[-2:]
        take_quarter(place, grad_ref, quarter, 0)
        for left, right, start in ((turned_ref, qkv_ref, 0), (heads_ref, quarter, columns)):
            add_met(dot(left[...], right[...], 1, 0), shards, met_refs, held, start)
        give_blocks(place, shards, held, outs)

    outs = [struct((piece, columns + part), jnp.bfloat16)] * shards
    scratch = (
        pltpu.VMEM((grad_attn.shape[0], part), grad_attn.dtype),
        pltpu.VMEM((shards, piece, columns + part), jnp.bfloat16),
    )
    return order.run(
        kernel, outs, attn_turned, qkv_grad, heads_out, grad_attn, *met, scratch=scratch
    )


def middle_back(order, part, far, normed, inverses, pieces, mod, branch):
    length, width = part.shape
    tokens = length // 4

    def kernel(place, part_ref, far_ref, normed_ref, inverse_ref, *refs):
        mod_ref, branch_ref, grad_attn, grad_middle, sums = refs[4:]
        gate, scale = mod_ref[2:3, :], 1.0 + mod_ref[4:5, :]
        totals = [jnp.zeros((1, width), jnp.float32)] * 4
        for index in range(4):
            span = slice(index * tokens, (index + 1) * tokens)
            other = slice((index ^ 2) * tokens, ((index ^ 2) + 1) * tokens)
            grad_in = wide(part_ref[span, :]) + wide(far_ref[other, :])
            values = normed_ref[span, :]
            grad = wide(refs[index][...]) + normalize_back(
                values, inverse_ref[span, :], grad_in * scale
            )
            result = low(gate * grad)
            grad_attn[span, :] = result
            if index < 2:
                grad_middle[span, :] = grad
                terms = (grad_in, grad_in * values, grad * branch_ref[span, :], wide(result))
                totals = [
                    total + jnp.sum(term, axis=0, keepdims=True)
                    for total, term in zip(totals, terms)
                ]
        for row, total in enumerate(totals):
            sums[row : row + 1, :] = total

    outs = (
        struct((length, width), jnp.bfloat16),
        struct((2 * tokens, width), jnp.float32),
        struct((4, width), jnp.float32),
    )
    return order.run(kernel, outs, part, far, normed, inverses, *pieces, mod, branch)


def attention_in_back(order, grad_mine, qkv_mine, grad_near, qkv_near, pieces, means, inverses):
    length, columns = grad_mine.shape
    width = qkv_mine.shape[0]
    tokens, half, step = length // 4, length // 2, width // 3

    def kernel(place, grad_mine_ref, qkv_mine_ref, grad_near_ref, qkv_near_ref, *refs):
        mean_ref, inverse_ref, own, give, sums = refs[4:]
        result = dot(grad_mine_ref[...], qkv_mine_ref[...], 1, 1) + dot(
            grad_near_ref[...], qkv_near_ref[...], 1, 1
        )
        own[...] = result[:half]
        give[...] = low(result[half:])
        scaled = jnp.zeros((1, step), jnp.float32)
        for index in range(4):
            span = slice(index * tokens, (index + 1) * tokens)
            normed = (wide(refs[index][...]) - mean_ref[span, :]) * inverse_ref[span, :]
            scaled = scaled + jnp.sum(result[span] * normed, axis=0, keepdims=True)
        sums[0:1, :] = jnp.sum(result, axis=0, keepdims=True)
        sums[1:2, :] = scaled

    outs = (
        struct((half, width), jnp.float32),
        struct((half, width), jnp.bfloat16),
        struct((2, width), jnp.float32),
    )
    weights = row_block((width, columns), step)
    grads = whole((length, columns))
    stats = whole((length, 1))
    return order.run(
        kernel,
        outs,
        grad_mine,
        qkv_mine,
        grad_near,
        qkv_near,
        *pieces,
        means,
        inverses,
        grid=(3,),
        in_specs=[grads, weights, grads, weights]
        + [column_block((tokens, width), step)] * 4
        + [stats, stats],
        out_specs=[
            column_block((half, width), step),
            column_block((half, width), step),
            column_block((2, width), step),
        ],
    )


def tokens_back(order, own, far, pieces, means, inverses, mod, grad_middle):
    half, width = own.shape
    tokens = half // 2

    def kernel(
        place, own_ref, far_ref, mine_ref, near_ref, mean_ref, inverse_ref, mod_ref, grad_ref,
        mine, give,
    ):
        for index, (source, target) in enumerate(((mine_ref, mine), (near_ref, give))):
            span = slice(index * tokens, (index + 1) * tokens)
            inverse = inverse_ref[span, :]
            normed = (wide(source[...]) - mean_ref[span, :]) * inverse
            grad = (own_ref[span, :] + wide(far_ref[span, :])) * (1.0 + mod_ref[1:2, :])
            target[...] = grad_ref[span, :] + normalize_back(normed, inverse, grad)

    outs = (struct((tokens, width), jnp.float32),) * 2
    return order.run(
        kernel, outs, own, far, pieces[0], pieces[1], means, inverses, mod, grad_middle
    )


def mix(order, own, far, down_bias, pieces, branch, grads, mod):
    half, width = own.shape
    tokens = half // 2

    def kernel(
        place, own_ref, far_ref, bias_ref, mine_ref, near_ref, branch_ref, grad_mine, grad_near,
        mod_ref, mine, give, sums,
    ):
        total = jnp.zeros((1, width), jnp.float32)
        sources = ((mine_ref, grad_mine, mine), (near_ref, grad_near, give))
        for index, (source, grad, target) in enumerate(sources):
            span = slice(index * tokens, (index + 1) * tokens)
            mlp_branch = own_ref[span, :] + wide(far_ref[span, :]) + bias_ref[...]
            middle = wide(source[...]) + mod_ref[2:3, :] * branch_ref[span, :]
            target[...] = low(middle + mod_ref[5:6, :] * mlp_branch)
            total = total + jnp.sum(wide(grad[...]) * mlp_branch, axis=0, keepdims=True)
        sums[...] = total

    outs = (struct((tokens, width), jnp.bfloat16),) * 2 + (struct((1, width), jnp.float32),)
    return order.run(
        kernel, outs, own, far, down_bias, pieces[0], pieces[1], branch, grads[0], grads[1], mod
    )


def per_device(
    latents,
    condition,
    mod_weight,
    mod_bias,
    qkv_weight,
    qv_bias,
    out_weight,
    out_bias,
    up_weight,
    up_bias,
    down_weight,
    down_bias,
    cotangent,
):
    here = Place()
    order = Order(here.place)
    shards, seat, core = here.shards, here.seat, here.core
    near_seat = seat ^ 1
    micros, tokens, width = latents.shape
    rows = width // shards
    hidden = up_weight.shape[1]
    heads = H // 4
    part = heads * HD
    block = hidden // shards // 4
    wait = order.wait

    hidden_part = shards * block
    attention_widths = (3 * part, width // 2)

    biases = jnp.concatenate([mod_bias, qv_bias, out_bias, up_bias, down_bias]).reshape(1, -1)
    ring = Gather(
        here, order, cut_attention(order, condition, biases, qkv_weight, out_weight), near=True
    )
    lat_mine, lat_give = cut_tokens(order, latents)
    lat_near, lat_far = here.to_core(lat_give), here.to_side(lat_mine)
    cot_mine, cot_give = cut_tokens(order, cotangent)
    cot_near, cot_far = here.to_core(cot_give), here.to_side(cot_mine)
    feed_piece = cut_feed(order, up_weight, down_weight, shards)
    ring.turn()
    lat_near, cot_near = wait(lat_near, cot_near)
    lat_far_near, cot_far_near = here.to_side(lat_near), here.to_side(cot_near)
    lat_far = wait(lat_far)
    ring.turn()
    cot_far, lat_far_near = wait(cot_far, lat_far_near)
    lats = (lat_mine, lat_near, lat_far, lat_far_near)
    ring.turn()
    feed_ring = Gather(here, order, wait(feed_piece), hold=True)
    qkv_mine, out_mine, heads_all = ring.finish(attention_widths, True)
    feed_ring.release()
    (
        cond_rows,
        mod_bias,
        qkv_bias_mine,
        qkv_bias_near,
        out_bias,
        up_bias_mine,
        up_bias_near,
        down_bias,
        *mod_parts,
    ) = modulation_parts(order, heads_all, mod_weight, micros, width, hidden)
    mod_sum = LineSum(here, order, mod_parts)
    mod_sum.join()
    mod_parts = mod_sum.finish()
    feed_ring.turn()
    qkv_near, out_near = ring.finish_near(attention_widths)
    mod, attn_in, attn_turned, means_one, inverses_one = norm_tokens(
        order, lats, mod_parts, mod_bias
    )
    qkv_mine = qkv_mine.reshape(width, 3 * part)
    parts_mine, heads_mine = attend(order, attn_in, qkv_mine, qkv_bias_mine)
    heads_far = here.to_side(heads_mine)
    qkv_near = qkv_near.reshape(width, 3 * part)
    parts_near, heads_near = attend(order, attn_in, qkv_near, qkv_bias_near)
    heads_far_near = here.to_side(heads_near)
    heads_far = wait(heads_far)
    feed_ring.turn()
    quarters = (heads_mine, heads_near, heads_far, wait(heads_far_near))
    heads_out, out_full, branch, normed_two, inverses_two, mlp_in = attention_out(
        order,
        quarters,
        out_mine.reshape(width, width // 2),
        out_near.reshape(width, width // 2),
        out_bias,
        lats,
        mod,
    )
    cots = (cot_mine, cot_near, cot_far, wait(cot_far_near))
    grad_mlp, down_sums = gate_grad(order, cots, mod)
    feed_ring.turn()
    up_mine, down_mine = feed_ring.finish((hidden_part, width))
    up_near, down_near = here.to_core(up_mine), here.to_core(down_mine)
    up_mine = up_mine.reshape(width, hidden_part)
    down_mine = down_mine.reshape(hidden_part, width)
    act_mine, slope_mine = feed(order, mlp_in, up_mine, up_bias_mine)
    pre_mine, up_sums_mine = feed_back(order, grad_mlp, down_mine, slope_mine)
    up_near = wait(up_near).reshape(width, hidden_part)
    act_near, slope_near = feed(order, mlp_in, up_near, up_bias_near)
    down_near = wait(down_near).reshape(hidden_part, width)
    pre_near, up_sums_near = feed_back(order, grad_mlp, down_near, slope_near)

    mlp_part = feed_in_back(order, pre_mine, up_mine, pre_near, up_near)
    mlp_far = here.to_side(mlp_part)

    def to_core(chunks):
        return [here.to_core(chunk) for chunk in chunks]

    down_met = to_core(weight_grad(order, shards, act_near, grad_mlp, 2))
    up_met = to_core(weight_grad(order, shards, mlp_in, pre_near, 2))
    down_met = wait(*down_met)
    down_sum = Scatter(here, order, weight_sum(order, shards, act_mine, grad_mlp, down_met))
    up_met = wait(*up_met)
    up_sum = Scatter(here, order, weight_sum(order, shards, mlp_in, pre_mine, up_met))
    down_sum.turn()
    feed_own, feed_give = feed_out(order, act_mine, down_mine, act_near, down_near)
    feed_far = here.to_side(feed_give)

    up_sum.turn()
    mlp_far = wait(mlp_far)
    grad_attn, grad_middle, middle_sums = middle_back(
        order, mlp_part, mlp_far, normed_two, inverses_two, cots, mod, branch
    )
    down_sum.turn()
    qkv_grad_near, qv_sums_near = attend_back(order, 1, parts_near, out_full, grad_attn)
    up_sum.turn()
    met = to_core(
        attention_grad(order, shards, attn_turned, qkv_grad_near, heads_out, grad_attn, 8)
    )
    met = wait(*met)
    qkv_grad_mine, qv_sums_mine = attend_back(order, 0, parts_mine, out_full, grad_attn)
    down_sum.turn()
    attention_total = Scatter(
        here,
        order,
        attention_sum(order, shards, attn_turned, qkv_grad_mine, heads_out, grad_attn, met),
    )
    up_sum.turn()
    grad_down = down_sum.finish()
    down_far, down_near = here.to_side(grad_down), here.to_core(grad_down)
    feed_far = wait(feed_far)
    mixed_mine, mixed_give, mix_sums = mix(
        order, feed_own, feed_far, down_bias, lats, branch, cots, mod
    )
    grad_up = up_sum.finish()
    attention_total.turn()
    down_far, down_near = wait(down_far, down_near)
    down_far_near = here.to_core(down_far)
    up_far, up_near = here.to_side(grad_up), here.to_core(grad_up)
    attn_own, attn_give, attn_sums = attention_in_back(
        order, qkv_grad_mine, qkv_mine, qkv_grad_near, qkv_near, lats, means_one, inverses_one
    )
    sums = token_sums(
        order, shards, attn_sums, middle_sums, mix_sums, down_sums, qv_sums_mine, qv_sums_near,
        up_sums_mine, up_sums_near,
    )
    sums_far = here.to_side(sums)
    attention_total.turn()
    sums = add_sums(order, sums, wait(sums_far))
    up_far, up_near, down_far_near = wait(up_far, up_near, down_far_near)
    sums_ring = Lines(here, order, sums)
    grad_down = lay_rows(order, (grad_down, down_near, down_far, down_far_near))
    attention_total.turn()
    sums_ring.join()
    up_far_near = here.to_core(up_far)
    attn_far = here.to_side(wait(attn_give))
    up_far_near = wait(up_far_near)
    grad_up = lay_columns(
        order, (grad_up, up_near, up_far, up_far_near), (hidden_part, shards)
    )
    sums_mine, sums_near = sums_ring.finish()
    sums_mine_far, sums_near_far = here.to_core(sums_mine), here.to_core(sums_near)
    grad_attention = attention_total.finish()
    attention_far = here.to_side(grad_attention)
    attention_near = here.to_core(grad_attention)
    sums_mine_far, sums_near_far = wait(sums_mine_far, sums_near_far)
    mod_all, grad_qv_bias, grad_out_bias, grad_up_bias, grad_down_bias, grad_low = (
        modulation_back(
            order, sums_mine, sums_near, sums_mine_far, sums_near_far, mod_weight, hidden
        )
    )
    low_ring = Lines(here, order, grad_low)
    attn_far = wait(attn_far)
    tokens_mine, tokens_give = tokens_back(
        order, attn_own, attn_far, lats, means_one, inverses_one, mod, grad_middle
    )
    attention_far, attention_near = wait(attention_far, attention_near)
    attention_far_near = here.to_core(attention_far)
    mixed_near, tokens_near = here.to_core(mixed_give), here.to_core(tokens_give)
    low_ring.join()
    attention_far_near = wait(attention_far_near)
    grad_qkv, grad_out = lay_columns(
        order,
        (grad_attention, attention_near, attention_far, attention_far_near),
        (3 * part, 3),
        (width // 4, 1),
    )
    mixed_near, tokens_near = wait(mixed_near, tokens_near)
    mixed, grad_latents = lay_tokens(
        order, (mixed_mine, mixed_near), (tokens_mine, tokens_near)
    )
    grad_condition = condition_back(order, *low_ring.finish(), condition)
    mod_all = wait(mod_all)
    grad_mod_weight = dot(cond_rows, mod_all, 0, 0)
    span = 6 * width // shards
    mod_span = lax.dynamic_slice_in_dim(mod_all, here.shard * span, span, 1)
    grad_mod_bias = jnp.sum(wide(mod_span), axis=0)
    grad_qv_bias, grad_out_bias, grad_up_bias, grad_down_bias = (
        vector.reshape(-1)
        for vector in (grad_qv_bias, grad_out_bias, grad_up_bias, grad_down_bias)
    )

    return (
        mixed,
        grad_latents,
        grad_condition,
        grad_mod_weight,
        grad_mod_bias,
        grad_qkv,
        grad_qv_bias,
        grad_out,
        grad_out_bias,
        grad_up,
        grad_up_bias,
        grad_down,
        grad_down_bias,
    )


def solution(mesh):
    tokens = P("fsdp", "seq", None)
    matrix = P("fsdp", None)
    vector = P("fsdp")
    parameters = (matrix, vector) * 5
    in_specs = (tokens, matrix) + parameters + (tokens,)
    out_specs = (tokens, tokens, matrix) + parameters
    return jax.shard_map(
        per_device, mesh=mesh, in_specs=in_specs, out_specs=out_specs, check_vma=False
    )
```
